32 devices in a mesh: tensor: 4 (over z), dp: 2 (over x), context: 4 (over y, core).
Axes of the slice: x: 2, y: 2, z: 4, core: 2. Of those that a mesh axis runs over, the one named last changes fastest.
Arguments:
- tokens: bfloat16 [4, 1024, 2048], P('dp', 'context'), may hold values from -6 to 6
- segments: int32 [4, 1024], P('dp'), may hold values from 0 to 510, as said below
- expert_ids: int32 [4, 1024, 6], P('dp', 'context'), may hold values from 0 to 15, all different within a row; in each aligned block of 256 rows (0 to 255, 256 to 511, ..., all dimensions but the last counted through in order) at most 192 rows name the same one
- norm_attn: bfloat16 [2048], replicated, may hold values from 0.5 to 1.5
- w_query: bfloat16 [2048, 3072], P(None, 'tensor'), may hold values from -0.125 to 0.125
- w_kv_down: bfloat16 [2048, 576], replicated, may hold values from -0.125 to 0.125
- norm_latent: bfloat16 [512], replicated, may hold values from 0.5 to 1.5
- w_kv_up: bfloat16 [512, 4096], P(None, 'tensor'), may hold values from -0.25 to 0.25
- w_out: bfloat16 [2048, 2048], P('tensor'), may hold values from -1 to 1
- norm_ffn: bfloat16 [2048], replicated, may hold values from 0.5 to 1.5
- w_router: bfloat16 [2048, 16], replicated, may hold values from -0.0625 to 0.0625
- w_shared_gate: bfloat16 [2048, 2816], P(None, 'tensor'), may hold values from -0.125 to 0.125
- w_shared_up: bfloat16 [2048, 2816], P(None, 'tensor'), may hold values from -0.125 to 0.125
- w_shared_down: bfloat16 [2816, 2048], P('tensor'), may hold values from -0.15625 to 0.15625
- w_expert_gate: bfloat16 [16, 2048, 1408], P(('dp', 'context'), None, 'tensor'), may hold values from -0.125 to 0.125
- w_expert_up: bfloat16 [16, 2048, 1408], P(('dp', 'context'), None, 'tensor'), may hold values from -0.125 to 0.125
- w_expert_down: bfloat16 [16, 1408, 2048], P(('dp', 'context'), 'tensor'), may hold values from -2.5 to 2.5
- cotangent: bfloat16 [4, 1024, 2048], P('dp', 'context'), may hold values from -6 to 6
Outputs:
- output: bfloat16 [4, 1024, 2048], P('dp', 'context')
- grad_tokens: bfloat16 [4, 1024, 2048], P('dp', 'context')
- grad_norm_attn: float32 [2048], replicated
- grad_w_query: float32 [2048, 3072], P(None, 'tensor')
- grad_w_kv_down: float32 [2048, 576], replicated
- grad_norm_latent: float32 [512], replicated
- grad_w_kv_up: float32 [512, 4096], P(None, 'tensor')
- grad_w_out: float32 [2048, 2048], P('tensor')
- grad_norm_ffn: float32 [2048], replicated
- grad_w_router: float32 [2048, 16], replicated
- grad_w_shared_gate: float32 [2048, 2816], P(None, 'tensor')
- grad_w_shared_up: float32 [2048, 2816], P(None, 'tensor')
- grad_w_shared_down: float32 [2816, 2048], P('tensor')
- grad_w_expert_gate: float32 [16, 2048, 1408], P(('dp', 'context'), None, 'tensor')
- grad_w_expert_up: float32 [16, 2048, 1408], P(('dp', 'context'), None, 'tensor')
- grad_w_expert_down: float32 [16, 1408, 2048], P(('dp', 'context'), 'tensor')
The draws below stay inside these ranges and needn't reach their ends.
Inputs may be any that keep to these rules, and one draw needn't show every extreme that they name: `segments`: segment numbers start at 0 in every sequence and rise by 0 or 1 from one position to the next; in every sequence one document begins among the first 256 positions and ends among the last 256; the largest segment number, 510, is reached by some sequence in every draw. `expert_ids`: each token names 6 different experts. Within the rows of one device for one sequence (aligned blocks of 256 positions), no expert is named by more than 192 rows, and in some block an expert is named by exactly 192.
All inputs are finite; a program needn't handle non-finite values.
Results may differ from the reference program's by a relative error of at most 0.025.
Values may be sent and summed in bfloat16 or wider, within the bound.
A program may use at most 512 MiB of HBM per device.

```python
import math
from functools import partial
import jax
import jax.numpy as jnp
import numpy as np
from jax import lax

D = 2048
HEADS = 16
NOPE = 128
ROPE = 64
VDIM = 128
LATENT = 512
FE = 1408
TOP = 6
SEQ_LEN = 1024
SHARD = 256
EXPERTS = 16
CAPACITY = 192
SHARED_FF = 2816
SEQS = 4


def draw_segments(key, part):
    key = jax.random.fold_in(key, 7)
    subkeys = jax.random.split(key, 4)
    doc_start = jax.random.randint(subkeys[0], (SEQS, 1), 1, SHARD)
    doc_end = jax.random.randint(subkeys[1], (SEQS, 1), SEQ_LEN - SHARD + 1, SEQ_LEN)
    coin_flips = jax.random.randint(subkeys[2], (SEQS, SEQ_LEN), 0, 6)
    chosen_seq = jax.random.randint(subkeys[3], (), 0, SEQS)
    row_index = jnp.arange(SEQS)[:, None]
    picked = row_index == chosen_seq
    doc_start = jnp.where(picked, SHARD - 1, doc_start)
    doc_end = jnp.where(picked, SEQ_LEN - SHARD + 1, doc_end)
    coin_flips = jnp.where(picked, 0, coin_flips)
    position = jnp.arange(SEQ_LEN)[None, :]
    outside = (position < doc_start) | (position > doc_end)
    breaks = ((position == doc_start) | (position == doc_end) | outside & (coin_flips == 0)) & (position > 0)
    return jnp.cumsum(breaks.astype(jnp.int32), axis=1).astype(jnp.int32)


def block_scale(stream_key, dims, shards, least, largest):
    def one(dim, blocks):
        heights = jax.random.uniform(jax.random.fold_in(jax.random.fold_in(stream_key, 6), dim), (blocks,), jnp.float32, least / len(shards), largest / len(shards))
        return jnp.repeat(jnp.exp(heights), dims[dim] // blocks).reshape((-1,) + (1,) * (len(dims) - dim - 1))

    level = one(*shards[0])
    for cut in shards[1:]:
        level = level * one(*cut)
    return level


def routed_block(key, own, number, rows, count, top, limit, lean):
    ranking = jax.random.permutation(key, count)
    packed, usual = shares(count, rows * top, limit, lean, True), shares(count, rows * top, limit, lean, False)
    places = jnp.arange(count)

    def named(sizes, offset_by):
        used = int((sizes > 0).sum())
        fixed = max(1, used // 4)
        passed = fixed + (places - fixed + offset_by * (used - fixed)) % max(1, count - fixed)
        return jnp.zeros((count,), jnp.int32).at[ranking[jnp.where(places < fixed, places, passed)]].set(jnp.asarray(sizes, jnp.int32))

    sizes = jnp.where(number % 4 == 0, named(packed, number // 4), named(usual, number - number // 4 - 1))
    mixed = jax.random.permutation(jax.random.fold_in(own, 3), count)
    giver, taker = mixed[0:count // 2 * 2:2], mixed[1:count // 2 * 2:2]
    margin = jnp.minimum(sizes[giver] - 1, limit - sizes[taker]) // 2
    margin = jnp.where((giver == ranking[0]) | (taker == ranking[0]) | (sizes[taker] == 0), 0, jnp.maximum(margin, 0))
    passed = jax.random.randint(jax.random.fold_in(own, 4), (count // 2,), 0, 1 << 20) % (margin + 1)
    sizes = sizes.at[giver].add(-passed).at[taker].add(passed)
    items = jnp.searchsorted(jnp.cumsum(sizes), jnp.arange(rows * top), side="right").astype(jnp.int32)
    table = items.reshape(top, rows).T
    table = table[jax.random.permutation(jax.random.fold_in(own, 1), rows)]
    offset_by = jax.random.randint(jax.random.fold_in(own, 2), (rows, 1), 0, top)
    return jnp.take_along_axis(table, (jnp.arange(top)[None, :] + offset_by) % top, axis=1)


def shares(amount, total, most, lean, full):
    loads = [(1 << 20) // math.isqrt(rank ** lean) + 1 for rank in range(1, amount + 1)]
    largest = most if full else min(most, max(-(-total // amount), total * loads[0] // sum(loads)))
    least = 1 if total - largest >= amount - 1 else 0
    given, surplus = [largest] + [least] * (amount - 1), total - largest - least * (amount - 1)
    while surplus > 0:
        movable = [i for i in range(1, amount) if given[i] < largest] or [i for i in range(1, amount) if given[i] < most]
        mass, left = sum([loads[i] for i in movable]), surplus
        for i in movable:
            more = min(most - given[i], max(1, left * loads[i] // mass), surplus)
            given[i] = given[i] + more
            surplus = surplus - more
    return np.array(given)


def normal_values(key, dims, scale, limit, cuts=(), kind=jnp.bfloat16):
    factor_of = block_scale(key, dims, cuts, -0.22, 0.18) if cuts else 1.0
    entries = jax.random.normal(key, dims, jnp.float32) * scale * factor_of
    return jnp.minimum(jnp.maximum(entries, -limit), limit).astype(kind)


def setup_inputs(seed: int = 0) -> dict:
    keys = jax.random.split(jax.random.key(seed), 19)
    tokens = normal_values(keys[0], (SEQS, SEQ_LEN, D), 1.0, 6.0, ((0, 2), (1, 4)))
    segments = draw_segments(jax.random.fold_in(keys[18], 71), 0)
    expert_ids_keys = jax.random.split(jax.random.fold_in(keys[2], 1), SEQS * SEQ_LEN // SHARD)
    expert_ids_turns = jax.random.permutation(jax.random.fold_in(keys[2], 3), SEQS * SEQ_LEN // SHARD)
    expert_ids = jax.vmap(lambda own, number: routed_block(jax.random.fold_in(keys[2], 2), own, number, SHARD, EXPERTS, TOP, CAPACITY, 1))(expert_ids_keys, expert_ids_turns).reshape((SEQS, SEQ_LEN, TOP))
    norm_attn = jnp.clip(1.0 + 0.1 * jax.random.normal(keys[3], (D,), jnp.float32), 0.5, 1.5).astype(jnp.bfloat16)
    w_query = normal_values(keys[4], (D, HEADS * (NOPE + ROPE)), D ** -0.5, 0.125, ((1, 4),))
    w_kv_down = normal_values(keys[5], (D, LATENT + ROPE), D ** -0.5, 0.125)
    norm_latent = jnp.clip(1.0 + 0.1 * jax.random.normal(keys[6], (LATENT,), jnp.float32), 0.5, 1.5).astype(jnp.bfloat16)
    w_kv_up = normal_values(keys[7], (LATENT, HEADS * (NOPE + VDIM)), LATENT ** -0.5, 0.25, ((1, 4),))
    w_out = normal_values(keys[8], (HEADS * VDIM, D), (HEADS * VDIM // 64) ** -0.5, 1.0, ((0, 4),))
    norm_ffn = jnp.clip(1.0 + 0.1 * jax.random.normal(keys[9], (D,), jnp.float32), 0.5, 1.5).astype(jnp.bfloat16)
    w_router = normal_values(keys[10], (D, EXPERTS), (4 * D) ** -0.5, 0.0625)
    w_shared_gate = normal_values(keys[11], (D, SHARED_FF), D ** -0.5, 0.125, ((1, 4),))
    w_shared_up = normal_values(keys[12], (D, SHARED_FF), D ** -0.5, 0.125, ((1, 4),))
    w_shared_down = normal_values(keys[13], (SHARED_FF, D), (SHARED_FF // 2) ** -0.5, 0.15625, ((0, 4),))
    w_expert_gate = normal_values(keys[14], (EXPERTS, D, FE), D ** -0.5, 0.125, ((0, 8), (2, 4)))
    w_expert_up = normal_values(keys[15], (EXPERTS, D, FE), D ** -0.5, 0.125, ((0, 8), (2, 4)))
    w_expert_down = normal_values(keys[16], (EXPERTS, FE, D), (max(FE // 256, 1)) ** -0.5, 2.5, ((0, 8), (1, 4)))
    cotangent = normal_values(keys[17], (SEQS, SEQ_LEN, D), 1.0, 6.0, ((0, 2), (1, 4)))
    return dict(tokens=tokens, segments=segments, expert_ids=expert_ids, norm_attn=norm_attn, w_query=w_query, w_kv_down=w_kv_down, norm_latent=norm_latent, w_kv_up=w_kv_up, w_out=w_out, norm_ffn=norm_ffn, w_router=w_router, w_shared_gate=w_shared_gate, w_shared_up=w_shared_up, w_shared_down=w_shared_down, w_expert_gate=w_expert_gate, w_expert_up=w_expert_up, w_expert_down=w_expert_down, cotangent=cotangent)


EPS = 1e-06

@jax.custom_vjp
def low(v):
    return lax.optimization_barrier(v.astype(jnp.bfloat16)).astype(jnp.float32)

@jax.custom_vjp
def low_back(v):
    return v

def low_keep(v):
    return (low(v), None)

def low_pass(kept, grad):
    return (grad,)

def back_keep(v):
    return (v, None)

def back_low(kept, grad):
    return (low(grad),)
low.defvjp(low_keep, low_pass)
low_back.defvjp(back_keep, back_low)

def matmul(left, right):
    return jnp.dot(left, right, precision=lax.Precision.HIGHEST)

def norm_rows(rows, gain):
    return rows * lax.rsqrt(lax.optimization_barrier(jnp.mean(rows * rows, axis=-1, keepdims=True)) + EPS) * gain

def angles(positions, rope_dim):
    frequency = 10000.0 ** (-(jnp.arange(rope_dim // 2).astype(jnp.float32) * 2.0) / rope_dim)
    turned = positions[:, None] * frequency[None, :]
    return (jnp.cos(turned), jnp.sin(turned))

def rotate(vectors, cosine, sine):
    half_dim = vectors.shape[-1] // 2
    front_part = vectors[..., :half_dim]
    back_part = vectors[..., half_dim:]
    return jnp.concatenate([front_part * cosine - back_part * sine, front_part * sine + back_part * cosine], axis=-1)

def attend(bundle):
    query_rot, key_nope, head_values, key_rope, seg_row = bundle
    seq_len = seg_row.shape[0]
    position = jnp.arange(seq_len)
    allowed = (seg_row[:, None] == seg_row[None, :]) & (position[None, :] <= position[:, None])
    raw = jnp.einsum('chd,lhd->hcl', query_rot[..., :NOPE], key_nope, precision=lax.Precision.HIGHEST)
    raw = raw + jnp.einsum('chd,ld->hcl', query_rot[..., NOPE:], key_rope, precision=lax.Precision.HIGHEST)
    scores = low_back(raw * (NOPE + ROPE) ** (-0.5))
    masked = jnp.where(allowed[None], scores, -1e+30)
    top_score = lax.optimization_barrier(jnp.max(masked, axis=-1, keepdims=True))
    weights_exp = jnp.where(allowed[None], jnp.exp(masked - top_score), 0.0)
    probs_low = low(weights_exp / lax.optimization_barrier(jnp.sum(weights_exp, axis=-1, keepdims=True)))
    mixed = jnp.einsum('hcl,lhd->chd', probs_low, head_values, precision=lax.Precision.HIGHEST)
    return low(low_back(mixed))

def forward(segments, expert_ids, tokens, norm_attn, w_query, w_kv_down, norm_latent, w_kv_up, w_out, norm_ffn, w_router, w_shared_gate, w_shared_up, w_shared_down, w_expert_gate, w_expert_up, w_expert_down):
    seq_count, seq_len, model_width = tokens.shape
    positions = jnp.arange(seq_len).astype(jnp.float32)
    cosine, sine = angles(positions, ROPE)
    x_attn = low(norm_rows(tokens, norm_attn)).reshape(seq_count * seq_len, model_width)
    query = low_back(matmul(x_attn, w_query)).reshape(seq_count, seq_len, HEADS, NOPE + ROPE)
    query_rot = low(jnp.concatenate([query[..., :NOPE], rotate(query[..., NOPE:], cosine[:, None, :], sine[:, None, :])], axis=-1))
    kv_raw = low_back(matmul(x_attn, w_kv_down)).reshape(seq_count, seq_len, LATENT + ROPE)
    latent = low(norm_rows(kv_raw[..., :LATENT], norm_latent))
    key_rope = low(rotate(kv_raw[..., LATENT:], cosine, sine))
    expanded = low(low_back(matmul(latent.reshape(seq_count * seq_len, LATENT), w_kv_up)))
    expanded = expanded.reshape(seq_count, seq_len, HEADS, NOPE + VDIM)
    attended = lax.map(jax.checkpoint(attend), (query_rot, expanded[..., :NOPE], expanded[..., NOPE:], key_rope, segments))
    attn_out = low_back(matmul(attended.reshape(seq_count * seq_len, HEADS * VDIM), w_out))
    hidden_one = tokens.reshape(seq_count * seq_len, model_width) + attn_out
    x_ffn = low(norm_rows(hidden_one, norm_ffn))
    router_probs = jax.nn.softmax(matmul(x_ffn, w_router), axis=-1)
    flat_ids = expert_ids.reshape(seq_count * seq_len, TOP)
    chosen = lax.optimization_barrier(jnp.sum((flat_ids[:, :, None] == jnp.arange(EXPERTS)[None, None, :]).astype(jnp.float32), axis=1))
    combine = router_probs * chosen
    shared_gate = low_back(matmul(x_ffn, w_shared_gate))
    shared_up = low_back(matmul(x_ffn, w_shared_up))
    shared_out = low_back(matmul(low(jax.nn.silu(shared_gate) * shared_up), w_shared_down))

    def expert_step(total, bundle):
        gate_w, up_w, down_w, column = bundle
        gate_pre = low_back(matmul(x_ffn, gate_w))
        up_pre = low_back(matmul(x_ffn, up_w))
        expert_out = low_back(matmul(low(jax.nn.silu(gate_pre) * up_pre), down_w))
        return (total + column[:, None] * expert_out, None)
    routed, unused = lax.scan(jax.checkpoint(expert_step), jnp.zeros_like(hidden_one), (w_expert_gate, w_expert_up, w_expert_down, combine.T))
    hidden_two = hidden_one + routed + shared_out
    return hidden_two.reshape(seq_count, seq_len, model_width)

def reference(tokens, segments, expert_ids, norm_attn, w_query, w_kv_down, norm_latent, w_kv_up, w_out, norm_ffn, w_router, w_shared_gate, w_shared_up, w_shared_down, w_expert_gate, w_expert_up, w_expert_down, cotangent):
    floats = [entry.astype(jnp.float32) for entry in (tokens, norm_attn, w_query, w_kv_down, norm_latent, w_kv_up, w_out, norm_ffn, w_router, w_shared_gate, w_shared_up, w_shared_down, w_expert_gate, w_expert_up, w_expert_down)]
    result, pullback = jax.vjp(partial(forward, segments, expert_ids), *floats)
    grads = pullback(cotangent.astype(jnp.float32))
    return (result.astype(jnp.bfloat16), grads[0].astype(jnp.bfloat16), grads[1], grads[2], grads[3], grads[4], grads[5], grads[6], grads[7], grads[8], grads[9], grads[10], grads[11], grads[12], grads[13], grads[14])
```

```python
import functools

import jax
import jax.numpy as jnp
from jax import lax
from jax.experimental import pallas as pl
from jax.experimental.pallas import tpu as pltpu
from jax.sharding import PartitionSpec as P

D = 2048
NOPE = 128
ROPE = 64
VDIM = 128
LATENT = 512
TOP = 6
EXP_DEV = 2
LANES = 128
GROUP = ("dp", "context")
EVERY = ("dp", "context", "tensor")
BF16 = jnp.bfloat16
F32 = jnp.float32
MESH = pl.DeviceIdType.MESH
MIB = 1024 * 1024

EPS = 1e-06


def rms_scale(rows):
    return lax.rsqrt(jnp.mean(rows * rows, axis=-1, keepdims=True) + EPS)


def norm_back(grad_out, normed, inverse):
    return inverse * (grad_out - normed * jnp.mean(grad_out * normed, axis=-1, keepdims=True))


def angles(positions, rope_dim):
    frequency = 10000.0 ** (-(jnp.arange(rope_dim // 2).astype(jnp.float32) * 2.0) / rope_dim)
    turned = positions[:, None] * frequency[None, :]
    return (jnp.cos(turned), jnp.sin(turned))


def rotate(vectors, cosine, sine):
    half_dim = vectors.shape[-1] // 2
    front_part = vectors[..., :half_dim]
    back_part = vectors[..., half_dim:]
    return jnp.concatenate(
        [front_part * cosine - back_part * sine, front_part * sine + back_part * cosine], axis=-1
    )


def unrotate(vectors, cosine, sine):
    half_dim = vectors.shape[-1] // 2
    front_part = vectors[..., :half_dim]
    back_part = vectors[..., half_dim:]
    return jnp.concatenate(
        [front_part * cosine + back_part * sine, back_part * cosine - front_part * sine], axis=-1
    )


def mm(left, right):
    return jnp.dot(left, right, preferred_element_type=F32)


def mm_nt(left, right):
    return lax.dot_general(left, right, (((1,), (1,)), ((), ())), preferred_element_type=F32)


def mm_tn(left, right):
    return lax.dot_general(left, right, (((0,), (0,)), ((), ())), preferred_element_type=F32)


def ring(axes, sizes):
    place = 0
    total = 1
    for axis, size in zip(axes, sizes):
        place = place * size + lax.axis_index(axis)
        total *= size

    def coordinates(index):
        found = {}
        for axis, size in reversed(list(zip(axes, sizes))):
            found[axis] = lax.rem(index, size)
            index = lax.div(index, size)
        return found

    return place, total, coordinates


def meet(devices):
    barrier = pltpu.get_barrier_semaphore()
    for device in devices:
        pl.semaphore_signal(barrier, inc=1, device_id=device, device_id_type=MESH)
    pl.semaphore_wait(barrier, len(devices))


def link_cost(values, times=1):
    sent = sum(v.size * v.dtype.itemsize for v in values) * times
    return pl.CostEstimate(flops=0, bytes_accessed=20 * sent, transcendentals=0)


def gather_kernel(axes, sizes, columns, v_ref, out_ref, send_sem, recv_sem, own_sem):
    place, total, coordinates = ring(axes, sizes)

    def part(index):
        if columns:
            width = v_ref.shape[1]
            return out_ref.at[:, pl.ds(pl.multiple_of(index * width, LANES), width)]
        return out_ref.at[:, index]

    peers = [lax.rem(place + step, total) for step in range(1, total)]
    meet([coordinates(peer) for peer in peers])
    copies = []
    for step in range(1, total):
        copy = pltpu.make_async_remote_copy(
            src_ref=v_ref,
            dst_ref=part(place),
            send_sem=send_sem.at[step - 1],
            recv_sem=recv_sem.at[step - 1],
            device_id=coordinates(peers[step - 1]),
            device_id_type=MESH,
        )
        copy.start()
        copies.append(copy)
    own = pltpu.make_async_copy(v_ref, part(place), own_sem)
    own.start()
    own.wait()
    for copy in copies:
        copy.wait_send()
    for step in range(1, total):
        source = lax.rem(place - step + total, total)
        pltpu.make_async_remote_copy(
            src_ref=v_ref,
            dst_ref=part(source),
            send_sem=send_sem.at[step - 1],
            recv_sem=recv_sem.at[step - 1],
            device_id=coordinates(peers[step - 1]),
            device_id_type=MESH,
        ).wait_recv()


def push_gather(v, axes, collective_id, columns=False):
    sizes = tuple(lax.axis_size(axis) for axis in axes)
    total = 1
    for size in sizes:
        total *= size
    if columns:
        shape = (v.shape[0], total * v.shape[1])
    else:
        shape = (v.shape[0], total) + v.shape[1:]
    return pl.pallas_call(
        functools.partial(gather_kernel, axes, sizes, columns),
        out_shape=jax.ShapeDtypeStruct(shape, v.dtype),
        in_specs=[pl.BlockSpec(memory_space=pl.ANY)],
        out_specs=pl.BlockSpec(memory_space=pl.ANY),
        scratch_shapes=[
            pltpu.SemaphoreType.DMA((total - 1,)),
            pltpu.SemaphoreType.DMA((total - 1,)),
            pltpu.SemaphoreType.DMA,
        ],
        compiler_params=pltpu.CompilerParams(collective_id=collective_id, has_side_effects=True),
        cost_estimate=link_cost([v], 4 * total),
        name="push_gather",
    )(v)


def scatter_kernel(axes, sizes, v_ref, out_ref, held, send_sem, recv_sem, own_sem):
    place, total, coordinates = ring(axes, sizes)
    peers = [lax.rem(place + step, total) for step in range(1, total)]
    meet([coordinates(peer) for peer in peers])
    copies = []
    for step in range(1, total):
        copy = pltpu.make_async_remote_copy(
            src_ref=v_ref.at[:, peers[step - 1]],
            dst_ref=held.at[step],
            send_sem=send_sem.at[step - 1],
            recv_sem=recv_sem.at[step - 1],
            device_id=coordinates(peers[step - 1]),
            device_id_type=MESH,
        )
        copy.start()
        copies.append(copy)
    own = pltpu.make_async_copy(v_ref.at[:, place], held.at[0], own_sem)
    own.start()
    own.wait()
    for copy in copies:
        copy.wait()
    for lead in range(out_ref.shape[0]):
        rows = out_ref.shape[1]
        chunk = min(rows, 16)

        def add(index, carry):
            at = pl.ds(pl.multiple_of(index * chunk, chunk), chunk)
            value = held[0, lead, at, :].astype(F32)
            for step in range(1, total):
                value = value + held[step, lead, at, :].astype(F32)
            out_ref[lead, at, :] = value
            return carry

        lax.fori_loop(0, rows // chunk, add, 0)


def push_scatter(v, axes, collective_id):
    sizes = tuple(lax.axis_size(axis) for axis in axes)
    lead, total, rows, width = v.shape
    return pl.pallas_call(
        functools.partial(scatter_kernel, axes, sizes),
        out_shape=jax.ShapeDtypeStruct((lead, rows, width), F32),
        in_specs=[pl.BlockSpec(memory_space=pl.ANY)],
        out_specs=pl.BlockSpec(memory_space=pltpu.VMEM),
        scratch_shapes=[
            pltpu.VMEM((total, lead, rows, width), v.dtype),
            pltpu.SemaphoreType.DMA((total - 1,)),
            pltpu.SemaphoreType.DMA((total - 1,)),
            pltpu.SemaphoreType.DMA,
        ],
        compiler_params=pltpu.CompilerParams(
            collective_id=collective_id, has_side_effects=True, vmem_limit_bytes=40 * MIB
        ),
        cost_estimate=link_cost([v], 4),
        name="push_scatter",
    )(v)


def flip(index, mask, bits):
    total = 0
    for bit in range(bits):
        weight = 1 << bit
        ours = lax.rem(lax.div(index, weight), 2)
        theirs = lax.rem(lax.div(mask, weight), 2)
        total = total + lax.rem(ours + theirs, 2) * weight
    return total


def group_layout(axes, sizes):
    place, _, coordinates = ring(axes, sizes)
    return lax.div(place, 2), lax.rem(place, 2), lambda chip, core: coordinates(chip * 2 + core)


def group_sizes(axes):
    sizes = tuple(lax.axis_size(axis) for axis in axes)
    pairs = 1
    for size in sizes:
        pairs *= size
    return sizes, pairs // 2


def group_scatter_kernel(count, pairs, axes, sizes, *refs):
    inputs, outputs, refs = refs[:count], refs[count : 2 * count], refs[2 * count :]
    mine, peer, summed, held = (refs[count * i : count * (i + 1)] for i in range(4))
    load_sem, swap_send, swap_recv, sum_send, sum_recv = refs[4 * count :]
    bits = pairs.bit_length() - 1
    chip, core, device = group_layout(axes, sizes)
    sibling = device(chip, 1 - core)
    meet([sibling] + [device(flip(chip, mask, bits), core) for mask in range(1, pairs)])
    loads = []
    swaps = []
    for i in range(count):
        swap = pltpu.make_async_remote_copy(
            src_ref=inputs[i].at[:, 1 - core],
            dst_ref=peer[i],
            send_sem=swap_send.at[i],
            recv_sem=swap_recv.at[i],
            device_id=sibling,
            device_id_type=MESH,
        )
        swap.start()
        swaps.append(swap)
        load = pltpu.make_async_copy(inputs[i].at[:, core], mine[i], load_sem.at[i])
        load.start()
        loads.append(load)
    pushes = []
    for i in range(count):
        loads[i].wait()
        swaps[i].wait()
        rows = mine[i].shape[1]
        for mask in list(range(1, pairs)) + [0]:
            target = flip(chip, mask, bits)

            def add(index, carry):
                at = pl.ds(pl.multiple_of(index * 16, 16), 16)
                value = mine[i][target, at, :].astype(F32) + peer[i][target, at, :].astype(F32)
                summed[i][mask, at, :] = value.astype(BF16)
                return carry

            lax.fori_loop(0, rows // 16, add, 0)
            if mask:
                push = pltpu.make_async_remote_copy(
                    src_ref=summed[i].at[mask],
                    dst_ref=held[i].at[mask - 1],
                    send_sem=sum_send.at[i, mask - 1],
                    recv_sem=sum_recv.at[i, mask - 1],
                    device_id=device(target, core),
                    device_id_type=MESH,
                )
                push.start()
                pushes.append(push)
    for push in pushes:
        push.wait()
    for i in range(count):
        rows = mine[i].shape[1]

        def total(index, carry):
            at = pl.ds(pl.multiple_of(index * 16, 16), 16)
            value = summed[i][0, at, :].astype(F32)
            for mask in range(1, pairs):
                value = value + held[i][mask - 1, at, :].astype(F32)
            outputs[i][at, :] = value.astype(BF16)
            return carry

        lax.fori_loop(0, rows // 16, total, 0)


def group_scatter(values, axes, collective_id):
    sizes, pairs = group_sizes(axes)
    count = len(values)
    values = [v.reshape((pairs, 2) + v.shape[1:]) for v in values]
    tails = [v.shape[2:] for v in values]
    dma = pltpu.SemaphoreType.DMA
    return pl.pallas_call(
        functools.partial(group_scatter_kernel, count, pairs, axes, sizes),
        out_shape=tuple(jax.ShapeDtypeStruct(tail, BF16) for tail in tails),
        in_specs=[pl.BlockSpec(memory_space=pl.ANY)] * count,
        out_specs=(pl.BlockSpec(memory_space=pltpu.VMEM),) * count,
        scratch_shapes=[pltpu.VMEM((pairs,) + tail, BF16) for tail in tails] * 3
        + [pltpu.VMEM((pairs - 1,) + tail, BF16) for tail in tails]
        + [
            dma((count,)),
            dma((count,)),
            dma((count,)),
            dma((count, pairs - 1)),
            dma((count, pairs - 1)),
        ],
        compiler_params=pltpu.CompilerParams(
            collective_id=collective_id, has_side_effects=True, vmem_limit_bytes=48 * MIB
        ),
        cost_estimate=link_cost(values),
        name="group_scatter",
    )(*values)


def group_gather_kernel(count, pairs, axes, sizes, *refs):
    inputs, outputs = refs[:count], refs[count : 2 * count]
    own_sem, push_send, push_recv, relay_send, relay_recv = refs[2 * count :]
    bits = pairs.bit_length() - 1
    chip, core, device = group_layout(axes, sizes)
    sibling = device(chip, 1 - core)
    meet([sibling] + [device(flip(chip, mask, bits), core) for mask in range(1, pairs)])

    def push(i, mask, source):
        return pltpu.make_async_remote_copy(
            src_ref=inputs[i],
            dst_ref=outputs[i].at[source, core],
            send_sem=push_send.at[i, mask],
            recv_sem=push_recv.at[i, mask],
            device_id=device(flip(chip, mask, bits), core),
            device_id_type=MESH,
        )

    def relay(i, mask, side):
        source = flip(chip, mask, bits)
        return pltpu.make_async_remote_copy(
            src_ref=inputs[i] if mask == 0 else outputs[i].at[source, side],
            dst_ref=outputs[i].at[source, side],
            send_sem=relay_send.at[i, mask],
            recv_sem=relay_recv.at[i, mask],
            device_id=sibling,
            device_id_type=MESH,
        )

    for mask in range(1, pairs):
        for i in range(count):
            push(i, mask, chip).start()
    owns = []
    for i in range(count):
        relay(i, 0, core).start()
        own = pltpu.make_async_copy(inputs[i], outputs[i].at[chip, core], own_sem.at[i])
        own.start()
        owns.append(own)
    for mask in range(1, pairs):
        for i in range(count):
            push(i, mask, flip(chip, mask, bits)).wait_recv()
            relay(i, mask, core).start()
    for own in owns:
        own.wait()
    for mask in range(pairs):
        for i in range(count):
            if mask:
                push(i, mask, chip).wait_send()
            relay(i, mask, core).wait_send()
            relay(i, mask, 1 - core).wait_recv()


def group_gather(values, axes, collective_id):
    sizes, pairs = group_sizes(axes)
    count = len(values)
    dma = pltpu.SemaphoreType.DMA
    gathered = pl.pallas_call(
        functools.partial(group_gather_kernel, count, pairs, axes, sizes),
        out_shape=tuple(jax.ShapeDtypeStruct((pairs, 2) + v.shape, v.dtype) for v in values),
        in_specs=[pl.BlockSpec(memory_space=pl.ANY)] * count,
        out_specs=(pl.BlockSpec(memory_space=pl.ANY),) * count,
        scratch_shapes=[
            dma((count,)),
            dma((count, pairs)),
            dma((count, pairs)),
            dma((count, pairs)),
            dma((count, pairs)),
        ],
        compiler_params=pltpu.CompilerParams(collective_id=collective_id, has_side_effects=True),
        cost_estimate=link_cost(values, 2 * pairs),
        name="group_gather",
    )(*values)
    return [g.reshape((2 * pairs,) + v.shape) for g, v in zip(gathered, values)]


def expert_kernel(
    pairs,
    context_size,
    fe,
    x_ref,
    cot_ref,
    gate_ref,
    up_ref,
    down_ref,
    out_ref,
    part_ref,
    gate_out,
    up_out,
    down_out,
    x_all,
    x_tile,
    cot_tile,
    out_tile,
    grad_tile,
    sum_tile,
    peer_tile,
    grad_gate,
    grad_up,
    hidden_low,
    gate_acc,
    up_acc,
    down_acc,
    x_send,
    x_recv,
    relay_send,
    relay_recv,
    pass_send,
    pass_recv,
    own_sem,
    x_load,
    cot_load,
    out_store,
    swap_send,
    swap_recv,
    sum_send,
    sum_recv,
    acc_store,
    credit,
):
    micro_count, rows = x_ref.shape[0], x_ref.shape[1]
    units = gate_ref.shape[1]
    half = units // EXP_DEV
    experts = 2 * pairs * EXP_DEV
    bits = pairs.bit_length() - 1
    steps = micro_count * pairs
    across = pairs == 4
    tile_rows = 2 * rows
    place = lax.axis_index("dp") * context_size + lax.axis_index("context")
    core = lax.rem(place, 2)
    chip = lax.div(place, 2)

    def device(chip_index, core_index):
        index = chip_index * 2 + core_index
        return {"dp": lax.div(index, context_size), "context": lax.rem(index, context_size)}

    sibling = device(chip, 1 - core)
    meet([sibling] + [device(flip(chip, mask, bits), core) for mask in range(1, pairs)])

    def step_of(step):
        micro = lax.div(step, pairs)
        turn = lax.rem(step, pairs)
        backward = lax.rem(micro, 2)
        return micro, lax.rem(turn + backward, pairs)

    def push_x(micro, mask):
        return pltpu.make_async_remote_copy(
            src_ref=x_ref.at[micro],
            dst_ref=x_all.at[micro, chip, core],
            send_sem=x_send.at[micro, mask],
            recv_sem=x_recv.at[micro, mask],
            device_id=device(flip(chip, mask, bits), core),
            device_id_type=MESH,
        )

    def relay(micro, mask):
        source = flip(chip, mask, bits)
        return pltpu.make_async_remote_copy(
            src_ref=x_all.at[micro, source, core],
            dst_ref=x_all.at[micro, source, core],
            send_sem=relay_send.at[micro, mask],
            recv_sem=relay_recv.at[micro, mask],
            device_id=sibling,
            device_id_type=MESH,
        )

    def relay_arrival(micro, mask):
        source = flip(chip, mask, bits)
        return pltpu.make_async_remote_copy(
            src_ref=x_all.at[micro, source, 1 - core],
            dst_ref=x_all.at[micro, source, 1 - core],
            send_sem=relay_send.at[micro, mask],
            recv_sem=relay_recv.at[micro, mask],
            device_id=sibling,
            device_id_type=MESH,
        )

    def x_arrival(micro, mask):
        return pltpu.make_async_remote_copy(
            src_ref=x_ref.at[micro],
            dst_ref=x_all.at[micro, flip(chip, mask, bits), core],
            send_sem=x_send.at[micro, mask],
            recv_sem=x_recv.at[micro, mask],
            device_id=device(flip(chip, mask, bits), core),
            device_id_type=MESH,
        )

    middle = rows // 2
    parts = (pl.ds(0, middle), pl.ds(middle, rows - middle))

    def pass_on(micro, mask, source, part):
        return pltpu.make_async_remote_copy(
            src_ref=x_all.at[micro, source, core, parts[part]],
            dst_ref=x_all.at[micro, source, core, parts[part]],
            send_sem=pass_send.at[micro, part],
            recv_sem=pass_recv.at[micro, part],
            device_id=device(flip(chip, mask, bits), core),
            device_id_type=MESH,
        )

    def load(step):
        micro, mask = step_of(step)
        slot = lax.rem(step, 2)
        source = flip(chip, mask, bits)
        return (
            pltpu.make_async_copy(x_all.at[micro, source], x_tile.at[slot], x_load.at[slot]),
            pltpu.make_async_copy(
                cot_ref.at[pl.ds(2 * source, 2), micro], cot_tile.at[slot], cot_load.at[slot]
            ),
        )

    def store(step):
        micro, mask = step_of(step)
        slot = lax.rem(step, 2)
        return pltpu.make_async_copy(
            out_tile.at[slot],
            out_ref.at[pl.ds(2 * flip(chip, mask, bits), 2), micro],
            out_store.at[slot],
        )

    def swap(step):
        slot = lax.rem(step, 2)
        return pltpu.make_async_remote_copy(
            src_ref=grad_tile.at[slot, 1 - core],
            dst_ref=peer_tile.at[slot],
            send_sem=swap_send.at[slot],
            recv_sem=swap_recv.at[slot],
            device_id=sibling,
            device_id_type=MESH,
        )

    def push_sum(step):
        micro, mask = step_of(step)
        slot = lax.rem(step, 2)
        return pltpu.make_async_remote_copy(
            src_ref=sum_tile.at[slot],
            dst_ref=part_ref.at[micro, mask],
            send_sem=sum_send.at[slot],
            recv_sem=sum_recv.at[micro, mask],
            device_id=device(flip(chip, mask, bits), core),
            device_id_type=MESH,
        )

    def keep_sum(step):
        micro, mask = step_of(step)
        slot = lax.rem(step, 2)
        return pltpu.make_async_copy(
            sum_tile.at[slot], part_ref.at[micro, mask], sum_send.at[slot]
        )

    def wait_sum_sent(step):
        mask = step_of(step)[1]

        @pl.when(mask > 0)
        def _():
            push_sum(step).wait_send()

        @pl.when(mask == 0)
        def _():
            keep_sum(step).wait()

    def fetch(step):
        micro, mask = step_of(step)

        if not across:

            @pl.when(mask > 0)
            def _():
                x_arrival(micro, mask).wait_recv()
                relay(micro, mask).start()

        else:

            @pl.when((mask == 1) | (mask == 2))
            def _():
                x_arrival(micro, mask).wait_recv()
                relay(micro, mask).start()

            for part in range(2):

                @pl.when(mask == part + 1)
                def _():
                    pass_on(micro, 2 - part, flip(chip, part + 1, bits), part).start()

            @pl.when(mask == 3)
            def _():
                for part in range(2):
                    pass_on(micro, part + 1, flip(chip, 3, bits), part).wait_recv()
                relay(micro, mask).start()

    def begin_load(step):
        micro, mask = step_of(step)
        relay_arrival(micro, mask).wait_recv()
        for copy in load(step):
            copy.start()

    def finish_sum(step):
        slot = lax.rem(step, 2)
        swap(step).wait()

        @pl.when(step >= 2)
        def _():
            wait_sum_sent(step - 2)

        def add(index, carry):
            at = pl.ds(pl.multiple_of(index * 16, 16), 16)
            value = grad_tile[slot, core, at, :].astype(F32) + peer_tile[slot, at, :].astype(F32)
            sum_tile[slot, at, :] = value.astype(BF16)
            return carry

        lax.fori_loop(0, rows // 16, add, 0)

        @pl.when(step < steps - 2)
        def _():
            pl.semaphore_signal(credit, inc=1, device_id=sibling, device_id_type=MESH)

        mask = step_of(step)[1]

        @pl.when(mask > 0)
        def _():
            push_sum(step).start()

        @pl.when(mask == 0)
        def _():
            keep_sum(step).start()

    direct = (1, 2) if across else tuple(range(1, pairs))
    for mask in direct:
        push_x(0, mask).start()
    own_copies = []
    for micro in range(micro_count):
        own = pltpu.make_async_copy(x_ref.at[micro], x_all.at[micro, chip, core], own_sem.at[micro])
        own.start()
        own_copies.append(own)
    for own in own_copies:
        own.wait()
    for micro in range(micro_count):
        relay(micro, 0).start()
    gate_acc[...] = jnp.zeros_like(gate_acc)
    up_acc[...] = jnp.zeros_like(up_acc)
    down_acc[...] = jnp.zeros_like(down_acc)
    begin_load(0)

    chunk = 256 if units % 256 == 0 else LANES
    out_chunk = 512
    slab = half - LANES
    first_lane = fe % LANES

    def work(step, carry):
        slot = lax.rem(step, 2)

        @pl.when(step == 1)
        def _():
            for micro in range(1, micro_count):
                for mask in direct:
                    push_x(micro, mask).start()

        for copy in load(step):
            copy.wait()

        @pl.when(step >= 2)
        def _():
            store(step - 2).wait()

        x_ext = x_tile[slot].reshape(tile_rows, D + LANES)
        x = x_ext[:, :D]
        chosen = x_ext[:, D:].astype(F32)
        cot = cot_tile[slot].reshape(tile_rows, D)
        lane = lax.broadcasted_iota(jnp.int32, (tile_rows, LANES), 1) - first_lane
        valid = (lane >= 0) & (lane < experts)

        slab_chunk = slab // chunk * chunk
        first_gate = mm(x, gate_ref[:, slab_chunk : slab_chunk + chunk])
        slab_gate = first_gate[:, slab - slab_chunk : slab - slab_chunk + LANES]
        logits = jnp.where(valid, slab_gate, -1e30)
        weights = jnp.where(
            valid, jnp.exp(logits - jnp.max(logits, axis=-1, keepdims=True)), 0.0
        )
        router_probs = weights / jnp.sum(weights, axis=-1, keepdims=True)
        named = router_probs * chosen
        picks = [lane == place * EXP_DEV + number for number in range(EXP_DEV)]
        scales = [
            jnp.sum(jnp.where(pick, named, 0.0), axis=-1, keepdims=True) for pick in picks
        ]
        flags = [
            jnp.sum(jnp.where(pick, chosen, 0.0), axis=-1, keepdims=True) for pick in picks
        ]
        dots = [jnp.zeros((tile_rows, 1), F32) for _ in picks]
        column = lax.broadcasted_iota(jnp.int32, (tile_rows, chunk), 1)
        starts = [slab_chunk] + [at for at in range(0, units, chunk) if at != slab_chunk]
        for start in starts:
            at = slice(start, start + chunk)
            gate = first_gate if start == slab_chunk else mm(x, gate_ref[:, at])
            up = mm(x, up_ref[:, at])
            back = mm_nt(cot, down_ref[at, :])
            first, last = start // half, (start + chunk - 1) // half
            scale = scales[first]
            if last > first:
                scale = jnp.where(column < last * half - start, scales[first], scales[last])
            sig = jax.nn.sigmoid(gate)
            act = gate * sig
            hidden = act * up
            grad_hidden = back * scale
            hidden_low[:, at] = (hidden * scale).astype(BF16)
            grad_gate[:, at] = (grad_hidden * up * (sig * (1.0 + gate * (1.0 - sig)))).astype(BF16)
            grad_up[:, at] = (grad_hidden * act).astype(BF16)
            product = hidden * back
            if last > first:
                split = last * half - start
                dots[first] = dots[first] + jnp.sum(product[:, :split], axis=-1, keepdims=True)
                dots[last] = dots[last] + jnp.sum(product[:, split:], axis=-1, keepdims=True)
            else:
                dots[first] = dots[first] + jnp.sum(product, axis=-1, keepdims=True)
        spread = jnp.zeros((tile_rows, LANES), F32)
        for pick, dot, flag in zip(picks, dots, flags):
            spread = spread + jnp.where(pick, dot * flag, 0.0)
        grad_logits = router_probs * (
            spread - jnp.sum(router_probs * spread, axis=-1, keepdims=True)
        )
        grad_gate[:, slab:half] = jnp.where(
            lane < 0, grad_gate[:, slab:half].astype(F32), grad_logits
        ).astype(BF16)

        @pl.when(step + 1 < steps)
        def _():
            fetch(step + 1)

        @pl.when(step >= 2)
        def _():
            pl.semaphore_wait(credit, 1)

        for start in range(0, D, out_chunk):
            at = slice(start, start + out_chunk)
            grad = mm_nt(grad_gate[...], gate_ref[at, :]) + mm_nt(grad_up[...], up_ref[at, :])
            grad_tile[slot, :, :, at] = grad.astype(BF16).reshape(2, rows, out_chunk)
        swap(step).start()

        @pl.when(step >= 1)
        def _():
            finish_sum(step - 1)

        for start in range(0, D, out_chunk):
            at = slice(start, start + out_chunk)
            out_tile[slot, :, :, at] = (
                mm(hidden_low[...], down_ref[:, at]).astype(BF16).reshape(2, rows, out_chunk)
            )
        store(step).start()
        for start in range(0, D, out_chunk):
            at = slice(start, start + out_chunk)
            x_part = x_tile[slot, :, :, at].reshape(tile_rows, out_chunk)
            gate_acc[at, :] += mm_tn(x_part, grad_gate[...])
            up_acc[at, :] += mm_tn(x_part, grad_up[...])

        @pl.when(step + 1 < steps)
        def _():
            begin_load(step + 1)

        for start in range(0, units, chunk):
            at = slice(start, start + chunk)
            down_acc[at, :] += mm_tn(hidden_low[:, at], cot)
        return carry

    lax.fori_loop(0, steps, work, 0)
    finals = []
    for number, (acc, target) in enumerate(
        ((gate_acc, gate_out), (up_acc, up_out), (down_acc, down_out))
    ):
        copy = pltpu.make_async_copy(acc, target, acc_store.at[number])
        copy.start()
        finals.append(copy)
    finish_sum(steps - 1)
    wait_sum_sent(steps - 2)
    wait_sum_sent(steps - 1)
    for copy in finals:
        copy.wait()
    store(steps - 2).wait()
    store(steps - 1).wait()
    for micro in range(micro_count):
        if across:
            for part in range(2):
                pass_on(micro, 2 - part, flip(chip, part + 1, bits), part).wait_send()
        for mask in range(pairs):
            relay(micro, mask).wait_send()
            if mask in direct:
                push_x(micro, mask).wait_send()
            if mask:
                pltpu.make_async_remote_copy(
                    src_ref=sum_tile.at[0],
                    dst_ref=part_ref.at[micro, mask],
                    send_sem=sum_send.at[0],
                    recv_sem=sum_recv.at[micro, mask],
                    device_id=device(flip(chip, mask, bits), core),
                    device_id_type=MESH,
                ).wait_recv()


def expert_pass(x_ext, cot_all, gate_w, up_w, down_w, fe, collective_id):
    micro_count, rows, width = x_ext.shape
    context_size = lax.axis_size("context")
    pairs = lax.axis_size("dp") * context_size // 2
    units = gate_w.shape[1]
    anywhere = pl.BlockSpec(memory_space=pl.ANY)
    weights = pl.BlockSpec(memory_space=pltpu.VMEM)
    dma = pltpu.SemaphoreType.DMA
    return pl.pallas_call(
        functools.partial(expert_kernel, pairs, context_size, fe),
        out_shape=(
            jax.ShapeDtypeStruct((2 * pairs, micro_count, rows, D), BF16),
            jax.ShapeDtypeStruct((micro_count, pairs, rows, D), BF16),
            jax.ShapeDtypeStruct((D, units), F32),
            jax.ShapeDtypeStruct((D, units), F32),
            jax.ShapeDtypeStruct((units, D), F32),
            jax.ShapeDtypeStruct((micro_count, pairs, 2, rows, width), BF16),
        ),
        in_specs=[anywhere, anywhere, weights, weights, weights],
        out_specs=(anywhere,) * 6,
        scratch_shapes=[
            pltpu.VMEM((2, 2, rows, width), BF16),
            pltpu.VMEM((2, 2, rows, D), BF16),
            pltpu.VMEM((2, 2, rows, D), BF16),
            pltpu.VMEM((2, 2, rows, D), BF16),
            pltpu.VMEM((2, rows, D), BF16),
            pltpu.VMEM((2, rows, D), BF16),
            pltpu.VMEM((2 * rows, units), BF16),
            pltpu.VMEM((2 * rows, units), BF16),
            pltpu.VMEM((2 * rows, units), BF16),
            pltpu.VMEM((D, units), F32),
            pltpu.VMEM((D, units), F32),
            pltpu.VMEM((units, D), F32),
            dma((micro_count, pairs)),
            dma((micro_count, pairs)),
            dma((micro_count, pairs)),
            dma((micro_count, pairs)),
            dma((micro_count, 2)),
            dma((micro_count, 2)),
            dma((micro_count,)),
            dma((2,)),
            dma((2,)),
            dma((2,)),
            dma((2,)),
            dma((2,)),
            dma((2,)),
            dma((micro_count, pairs)),
            dma((3,)),
            pltpu.SemaphoreType.REGULAR,
        ],
        compiler_params=pltpu.CompilerParams(
            collective_id=collective_id, has_side_effects=True, vmem_limit_bytes=62 * MIB
        ),
        cost_estimate=pl.CostEstimate(
            flops=36 * pairs * micro_count * rows * D * units,
            bytes_accessed=500_000_000,
            transcendentals=0,
        ),
        name="expert_pass",
    )(x_ext, cot_all, gate_w, up_w, down_w)[:5]


def swiglu_pass(x, cot, gate_w, up_w, down_w):
    gate = mm(x, gate_w)
    up = mm(x, up_w)
    sig = jax.nn.sigmoid(gate)
    act = gate * sig
    back = mm_nt(cot, down_w)
    hidden = (act * up).astype(BF16)
    out = mm(hidden, down_w)
    grad_gate = (back * up * (sig * (1.0 + gate * (1.0 - sig)))).astype(BF16)
    grad_up = (back * act).astype(BF16)
    grad_x = mm_nt(grad_gate, gate_w) + mm_nt(grad_up, up_w)
    weight_grads = [mm_tn(x, grad_gate), mm_tn(x, grad_up), mm_tn(cot, hidden)]
    return out, grad_x, [grad.astype(BF16) for grad in weight_grads]


def per_device(
    tokens,
    segments,
    expert_ids,
    norm_attn,
    w_query,
    w_kv_down,
    norm_latent,
    w_kv_up,
    w_out,
    norm_ffn,
    w_router,
    w_shared_gate,
    w_shared_up,
    w_shared_down,
    w_expert_gate,
    w_expert_up,
    w_expert_down,
    cotangent,
):
    micro_count, block_rows = tokens.shape[:2]
    rows = micro_count * block_rows
    seq_len = segments.shape[1]
    context_size = lax.axis_size("context")
    groups = lax.axis_size("dp") * context_size
    tensor_size = lax.axis_size("tensor")
    group_index = lax.axis_index("dp") * context_size + lax.axis_index("context")
    own_rows = block_rows // tensor_size
    own_start = lax.axis_index("tensor") * own_rows
    experts = EXP_DEV * groups
    heads_local = w_query.shape[1] // (NOPE + ROPE)
    fe_local = w_expert_gate.shape[2]
    half = -(-(fe_local + experts) // LANES) * LANES
    scale_factor = (NOPE + ROPE) ** (-0.5)
    start_row = lax.axis_index("context") * block_rows
    query_index = start_row + jnp.arange(block_rows)
    key_index = jnp.arange(seq_len)
    cos_block, sin_block = angles(query_index.astype(F32), ROPE)
    cos_query = jnp.tile(cos_block, (micro_count, 1))
    sin_query = jnp.tile(sin_block, (micro_count, 1))
    gain_attn = norm_attn.astype(F32)
    gain_latent = norm_latent.astype(F32)
    gain_ffn = norm_ffn.astype(F32)

    def own(values):
        values = values.reshape((micro_count, block_rows) + values.shape[1:])
        part = lax.dynamic_slice_in_dim(values, own_start, own_rows, axis=1)
        return part.reshape((micro_count * own_rows,) + values.shape[2:])

    def to_owner(values, collective_id):
        values = values.astype(BF16).reshape(micro_count, tensor_size, own_rows, values.shape[-1])
        summed = push_scatter(values, ("tensor",), collective_id)
        return summed.reshape(micro_count * own_rows, values.shape[-1])

    def from_owners(values, collective_id):
        values = values.reshape(micro_count, own_rows, values.shape[-1])
        return push_gather(values, ("tensor",), collective_id).reshape(rows, values.shape[-1])

    out_rows = w_out.shape[0] // groups
    out_full = lax.dynamic_slice_in_dim(w_out, group_index * out_rows, out_rows)
    out_full = lax.all_gather(out_full, "tensor", axis=0)
    out_full = lax.all_gather(out_full, GROUP, axis=0)
    out_full = out_full.transpose(1, 0, 2, 3).reshape(tensor_size * w_out.shape[0], D)
    cot_all = lax.all_gather(cotangent, GROUP, axis=0)
    zeros = jnp.zeros((D, half - fe_local - experts), BF16)
    more = jnp.zeros((D, half - fe_local), BF16)
    gate_wide = jnp.concatenate([w_expert_gate[0], w_router, zeros, w_expert_gate[1], more], axis=1)
    up_wide = jnp.concatenate([w_expert_up[0], more, w_expert_up[1], more], axis=1)
    down_wide = jnp.pad(w_expert_down, ((0, 0), (0, half - fe_local), (0, 0)))
    down_wide = down_wide.reshape(EXP_DEV * half, D)
    slots = jnp.arange(LANES) - fe_local % LANES
    named = jnp.any(expert_ids[..., None] == slots, axis=2).astype(BF16)

    x_rows = tokens.reshape(rows, D).astype(F32)
    cot_rows = cotangent.reshape(rows, D)
    inv_attn = rms_scale(x_rows)
    normed_attn = x_rows * inv_attn
    x_attn = (normed_attn * gain_attn).astype(BF16)
    kv_raw = mm(x_attn, w_kv_down)
    latent_raw = kv_raw[:, :LATENT]
    inv_latent = rms_scale(latent_raw)
    normed_latent = latent_raw * inv_latent
    latent = (normed_latent * gain_latent).astype(BF16)
    key_rope = rotate(kv_raw[:, LATENT:], cos_query, sin_query).astype(BF16)
    kv_own = jnp.concatenate([latent, key_rope], axis=1)
    kv_all = group_gather(list(jnp.split(kv_own, micro_count)), ("context",), 1)
    kv_all = jnp.concatenate(kv_all, axis=0).reshape(micro_count * seq_len, LATENT + ROPE)
    query = mm(x_attn, w_query).reshape(rows, heads_local, NOPE + ROPE)
    query_rot = jnp.concatenate(
        [
            query[..., :NOPE],
            rotate(query[..., NOPE:], cos_query[:, None, :], sin_query[:, None, :]),
        ],
        axis=-1,
    ).astype(BF16)
    latent_all = kv_all[:, :LATENT]
    expanded = mm(latent_all, w_kv_up).astype(BF16)
    expanded = expanded.reshape(micro_count, seq_len, heads_local, NOPE + VDIM)
    key_rope_all = kv_all[:, LATENT:].reshape(micro_count, seq_len, ROPE)
    query_rot = query_rot.reshape(micro_count, block_rows, heads_local, NOPE + ROPE)
    seg_query = lax.dynamic_slice_in_dim(segments, start_row, block_rows, axis=1)
    allowed = (seg_query[:, :, None] == segments[:, None, :]) & (
        key_index[None, None, :] <= query_index[None, :, None]
    )
    probs = []
    attended = []
    for m in range(micro_count):
        key_nope, head_values = expanded[m, ..., :NOPE], expanded[m, ..., NOPE:]
        raw = jnp.einsum(
            "chd,lhd->hcl", query_rot[m, ..., :NOPE], key_nope, preferred_element_type=F32
        )
        raw = raw + jnp.einsum(
            "chd,ld->hcl", query_rot[m, ..., NOPE:], key_rope_all[m], preferred_element_type=F32
        )
        scores = jnp.where(allowed[m][None], raw * scale_factor, -1e30)
        top_score = jnp.max(scores, axis=-1, keepdims=True)
        weights_exp = jnp.where(allowed[m][None], jnp.exp(scores - top_score), 0.0)
        probs.append(weights_exp / jnp.sum(weights_exp, axis=-1, keepdims=True))
        part = jnp.einsum(
            "hcl,lhd->chd", probs[m].astype(BF16), head_values, preferred_element_type=F32
        )
        attended.append(part.astype(BF16).reshape(block_rows, heads_local * VDIM))
    attended = jnp.concatenate(attended, axis=0)
    attended_all = push_gather(attended, ("tensor",), 2, columns=True)
    hidden_one = x_rows + mm(attended_all, out_full)
    inv_ffn = rms_scale(hidden_one)
    normed_ffn = hidden_one * inv_ffn
    x_ffn = (normed_ffn * gain_ffn).astype(BF16)
    x_ext = jnp.concatenate([x_ffn.reshape(micro_count, block_rows, D), named], axis=-1)

    shared_out, shared_grad_x, shared_grads = swiglu_pass(
        x_ffn, cot_rows, w_shared_gate, w_shared_up, w_shared_down
    )
    out_part, grad_part, gate_grad, up_grad, down_grad = expert_pass(
        x_ext, cot_all, gate_wide, up_wide, down_wide, fe_local, 3
    )
    router_grad = gate_grad[:, fe_local : fe_local + experts]

    def unit_columns(grad):
        return jnp.stack([grad[:, half * e : half * e + fe_local] for e in range(EXP_DEV)])

    down_grad = down_grad.reshape(EXP_DEV, half, D)[:, :fe_local]
    grad_sum = jnp.sum(grad_part.astype(F32), axis=1).reshape(rows, D) + shared_grad_x
    grad_x_ffn = to_owner(grad_sum, 4)
    out_sum = lax.psum_scatter(out_part, GROUP, scatter_dimension=0, tiled=False).reshape(rows, D)
    out_sum = lax.psum((out_sum.astype(F32) + shared_out).astype(BF16), "tensor")
    output = (hidden_one + out_sum.astype(F32)).astype(BF16)

    normed_own = own(normed_ffn)
    norm_ffn_grad = jnp.sum(grad_x_ffn * normed_own, axis=0)
    grad_one = own(cot_rows).astype(F32) + norm_back(
        grad_x_ffn * gain_ffn, normed_own, own(inv_ffn)
    )
    grad_attn_low = from_owners(grad_one.astype(BF16), 5)
    out_grad = mm_tn(grad_attn_low, attended).astype(BF16)
    early = jnp.concatenate(shared_grads + [out_grad], axis=1)
    early = lax.psum_scatter(early, GROUP, scatter_dimension=0, tiled=True)
    early = lax.all_gather(early, GROUP, axis=0, tiled=True)
    grad_attended = mm_nt(grad_attn_low, w_out).astype(BF16)
    grad_attended = grad_attended.reshape(micro_count, block_rows, heads_local, VDIM)
    grad_expanded = []
    grad_key_rope = []
    grad_query = []
    for m in range(micro_count):
        key_nope, head_values = expanded[m, ..., :NOPE], expanded[m, ..., NOPE:]
        grad_probs = jnp.einsum(
            "chd,lhd->hcl", grad_attended[m], head_values, preferred_element_type=F32
        )
        grad_scores = (
            probs[m] * (grad_probs - jnp.sum(probs[m] * grad_probs, axis=-1, keepdims=True))
        ).astype(BF16)
        grad_values = jnp.einsum(
            "hcl,chd->lhd", probs[m].astype(BF16), grad_attended[m], preferred_element_type=F32
        )
        grad_key_nope = scale_factor * jnp.einsum(
            "hcl,chd->lhd", grad_scores, query_rot[m, ..., :NOPE], preferred_element_type=F32
        )
        grad_key_rope.append(
            scale_factor
            * jnp.einsum(
                "hcl,chd->ld", grad_scores, query_rot[m, ..., NOPE:], preferred_element_type=F32
            )
        )
        grad_query_nope = scale_factor * jnp.einsum(
            "hcl,lhd->chd", grad_scores, key_nope, preferred_element_type=F32
        )
        grad_query_rope = scale_factor * jnp.einsum(
            "hcl,ld->chd", grad_scores, key_rope_all[m], preferred_element_type=F32
        )
        grad_expanded.append(
            jnp.concatenate([grad_key_nope, grad_values], axis=-1)
            .reshape(seq_len, heads_local * (NOPE + VDIM))
            .astype(BF16)
        )
        grad_query.append(
            jnp.concatenate(
                [
                    grad_query_nope,
                    unrotate(grad_query_rope, cos_block[:, None, :], sin_block[:, None, :]),
                ],
                axis=-1,
            ).reshape(block_rows, heads_local * (NOPE + ROPE))
        )
    grad_expanded = jnp.concatenate(grad_expanded, axis=0)
    grad_key_rope = jnp.concatenate(grad_key_rope, axis=0)
    grad_query_raw = jnp.concatenate(grad_query, axis=0).astype(BF16)
    kv_up_grad = mm_tn(latent_all, grad_expanded)
    grad_kv_part = jnp.concatenate([mm_nt(grad_expanded, w_kv_up), grad_key_rope], axis=1)
    grad_kv = group_scatter(
        [
            part.reshape(context_size, block_rows, LATENT + ROPE)
            for part in jnp.split(grad_kv_part.astype(BF16), micro_count)
        ],
        ("context",),
        6,
    )
    grad_kv = jnp.concatenate(grad_kv, axis=0)
    query_grad = mm_tn(x_attn, grad_query_raw).astype(BF16)
    grad_x_heads = mm_nt(grad_query_raw, w_query).astype(BF16)
    router_part = router_grad.astype(BF16).reshape(tensor_size, micro_count, own_rows, -1)
    router_part = router_part.transpose(1, 0, 2, 3).reshape(rows, -1)
    late = to_owner(jnp.concatenate([grad_x_heads, grad_kv, router_part], axis=1), 7)
    grad_x_heads, grad_latent, grad_rope_key, router_own = jnp.split(
        late, [D, D + LATENT, D + LATENT + ROPE], axis=1
    )
    normed_latent_own = own(normed_latent)
    norm_latent_grad = jnp.sum(grad_latent * normed_latent_own, axis=0)
    grad_latent_raw = norm_back(grad_latent * gain_latent, normed_latent_own, own(inv_latent))
    grad_kv_raw = jnp.concatenate(
        [grad_latent_raw, unrotate(grad_rope_key, own(cos_query), own(sin_query))], axis=-1
    ).astype(BF16)
    grad_x_attn = grad_x_heads + mm_nt(grad_kv_raw, w_kv_down)
    normed_attn_own = own(normed_attn)
    norm_attn_grad = jnp.sum(grad_x_attn * normed_attn_own, axis=0)
    grad_input = grad_one + norm_back(grad_x_attn * gain_attn, normed_attn_own, own(inv_attn))
    finished = from_owners(jnp.concatenate([grad_input.astype(BF16), grad_kv_raw], axis=1), 8)
    grad_tokens, grad_kv_raw = finished[:, :D], finished[:, D:]

    slice_rows = D // tensor_size
    x_slice = lax.dynamic_slice_in_dim(
        x_attn, lax.axis_index("tensor") * slice_rows, slice_rows, axis=1
    )
    kv_down_grad = mm_tn(x_slice, grad_kv_raw).astype(BF16)
    query_part, kv_up_part, kv_down_part, router_part = group_scatter(
        [
            query_grad.reshape(groups, D // groups, -1),
            kv_up_grad.astype(BF16).reshape(groups, LATENT // groups, -1),
            kv_down_grad.reshape(groups, slice_rows // groups, -1),
            router_own.astype(BF16).reshape(groups, 16, -1),
        ],
        GROUP,
        9,
    )
    router_width = router_part.shape[1]
    router_part = jnp.pad(router_part, ((0, 0), (0, LATENT + ROPE - router_width)))
    sliced = jnp.concatenate([kv_down_part, router_part], axis=0)
    sliced = push_gather(sliced[None], ("tensor",), 10)
    query_grad, kv_up_grad, sliced = group_gather(
        [query_part, kv_up_part, sliced.reshape(-1, LATENT + ROPE)], GROUP, 11
    )
    sliced = sliced.reshape(groups, tensor_size, -1, LATENT + ROPE).transpose(1, 0, 2, 3)
    kv_down_grad = sliced[:, :, :-16].reshape(D, LATENT + ROPE).astype(F32)
    router_grad = sliced[:, :, -16:, :router_width].reshape(D, experts).astype(F32)
    small = jnp.concatenate([norm_attn_grad, norm_ffn_grad, norm_latent_grad])
    small = jnp.sum(push_gather(small.reshape(1, -1, LANES), EVERY, 12), axis=(0, 1)).reshape(-1)
    ff_local = w_shared_gate.shape[1]
    early = early.astype(F32)
    return (
        output.reshape(tokens.shape),
        grad_tokens.reshape(tokens.shape),
        small[:D],
        query_grad.reshape(D, -1).astype(F32),
        kv_down_grad,
        small[D + D :],
        kv_up_grad.reshape(LATENT, -1).astype(F32),
        early[:, 3 * ff_local :].T,
        small[D : D + D],
        router_grad,
        early[:, :ff_local],
        early[:, ff_local : 2 * ff_local],
        early[:, 2 * ff_local : 3 * ff_local].T,
        unit_columns(gate_grad),
        unit_columns(up_grad),
        down_grad,
    )


def solution(mesh):
    return jax.shard_map(
        per_device,
        mesh=mesh,
        in_specs=(
            P("dp", "context", None),
            P("dp", None),
            P("dp", "context", None),
            P(),
            P(None, "tensor"),
            P(),
            P(),
            P(None, "tensor"),
            P("tensor", None),
            P(),
            P(),
            P(None, "tensor"),
            P(None, "tensor"),
            P("tensor", None),
            P(("dp", "context"), None, "tensor"),
            P(("dp", "context"), None, "tensor"),
            P(("dp", "context"), "tensor", None),
            P("dp", "context", None),
        ),
        out_specs=(
            P("dp", "context", None),
            P("dp", "context", None),
            P(),
            P(None, "tensor"),
            P(),
            P(),
            P(None, "tensor"),
            P("tensor", None),
            P(),
            P(),
            P(None, "tensor"),
            P(None, "tensor"),
            P("tensor", None),
            P(("dp", "context"), None, "tensor"),
            P(("dp", "context"), None, "tensor"),
            P(("dp", "context"), "tensor", None),
        ),
        check_vma=False,
    )
```

```python
import functools

import jax
import jax.numpy as jnp
from jax import lax
from jax.experimental import pallas as pl
from jax.experimental.pallas import tpu as pltpu
from jax.sharding import PartitionSpec as P

D = 2048
NOPE = 128
ROPE = 64
VDIM = 128
LATENT = 512
TOP = 6
EXP_DEV = 2
LANES = 128
GROUP = ("dp", "context")
EVERY = ("dp", "context", "tensor")
BF16 = jnp.bfloat16
F32 = jnp.float32
MESH = pl.DeviceIdType.MESH
MIB = 1024 * 1024

EPS = 1e-06


def rms_scale(rows):
    return lax.rsqrt(jnp.mean(rows * rows, axis=-1, keepdims=True) + EPS)


def norm_back(grad_out, normed, inverse):
    return inverse * (grad_out - normed * jnp.mean(grad_out * normed, axis=-1, keepdims=True))


def angles(positions, rope_dim):
    frequency = 10000.0 ** (-(jnp.arange(rope_dim // 2).astype(jnp.float32) * 2.0) / rope_dim)
    turned = positions[:, None] * frequency[None, :]
    return (jnp.cos(turned), jnp.sin(turned))


def rotate(vectors, cosine, sine):
    half_dim = vectors.shape[-1] // 2
    front_part = vectors[..., :half_dim]
    back_part = vectors[..., half_dim:]
    return jnp.concatenate(
        [front_part * cosine - back_part * sine, front_part * sine + back_part * cosine], axis=-1
    )


def unrotate(vectors, cosine, sine):
    half_dim = vectors.shape[-1] // 2
    front_part = vectors[..., :half_dim]
    back_part = vectors[..., half_dim:]
    return jnp.concatenate(
        [front_part * cosine + back_part * sine, back_part * cosine - front_part * sine], axis=-1
    )


def mm(left, right):
    return jnp.dot(left, right, preferred_element_type=F32)


def mm_nt(left, right):
    return lax.dot_general(left, right, (((1,), (1,)), ((), ())), preferred_element_type=F32)


def mm_tn(left, right):
    return lax.dot_general(left, right, (((0,), (0,)), ((), ())), preferred_element_type=F32)


def ring(axes, sizes):
    place = 0
    total = 1
    for axis, size in zip(axes, sizes):
        place = place * size + lax.axis_index(axis)
        total *= size

    def coordinates(index):
        found = {}
        for axis, size in reversed(list(zip(axes, sizes))):
            found[axis] = lax.rem(index, size)
            index = lax.div(index, size)
        return found

    return place, total, coordinates


def meet(devices):
    barrier = pltpu.get_barrier_semaphore()
    for device in devices:
        pl.semaphore_signal(barrier, inc=1, device_id=device, device_id_type=MESH)
    pl.semaphore_wait(barrier, len(devices))


def flip(index, mask, bits):
    total = 0
    for bit in range(bits):
        weight = 1 << bit
        ours = lax.rem(lax.div(index, weight), 2)
        theirs = lax.rem(lax.div(mask, weight), 2)
        total = total + lax.rem(ours + theirs, 2) * weight
    return total


def group_layout(axes, sizes):
    place, _, coordinates = ring(axes, sizes)
    return lax.div(place, 2), lax.rem(place, 2), lambda chip, core: coordinates(chip * 2 + core)


def group_sizes(axes):
    sizes = tuple(lax.axis_size(axis) for axis in axes)
    pairs = 1
    for size in sizes:
        pairs *= size
    return sizes, pairs // 2


def add_rows(out, terms, rows):
    def add(index, carry):
        at = pl.ds(pl.multiple_of(index * 16, 16), 16)
        value = terms[0](at).astype(F32)
        for term in terms[1:]:
            value = value + term(at).astype(F32)
        out(at, value)
        return carry

    lax.fori_loop(0, rows // 16, add, 0)


class LineGather:
    def __init__(self, v, axis):
        self.axis, self.size = axis, lax.axis_size(axis)
        dma = pltpu.SemaphoreType.DMA
        self.inputs = [(v, pltpu.VMEM)]
        shape = (v.shape[0], self.size) + v.shape[1:]
        self.outputs = [(jax.ShapeDtypeStruct(shape, v.dtype), pl.ANY)]
        self.scratch = [dma((2, self.size)), dma((2, self.size)), dma]

    def greets(self):
        index = lax.axis_index(self.axis)
        return [
            {self.axis: lax.rem(index + step, self.size)} for step in (1, self.size - 1)
        ]

    def run(self, v_ref, out_ref, send_sem, recv_sem, own_sem):
        index, size = lax.axis_index(self.axis), self.size

        def copy(way, hop, first):
            step = 1 - 2 * way
            source = lax.rem(index - step * (hop - 1) + size, size)
            return pltpu.make_async_remote_copy(
                src_ref=v_ref if first else out_ref.at[:, source],
                dst_ref=out_ref.at[:, source],
                send_sem=send_sem.at[way, hop],
                recv_sem=recv_sem.at[way, hop],
                device_id={self.axis: lax.rem(index + step + size, size)},
                device_id_type=MESH,
            )

        def arrival(way, hop):
            step = 1 - 2 * way
            source = lax.rem(index - step * hop + size, size)
            return pltpu.make_async_remote_copy(
                src_ref=v_ref,
                dst_ref=out_ref.at[:, source],
                send_sem=send_sem.at[way, hop],
                recv_sem=recv_sem.at[way, hop],
                device_id={self.axis: lax.rem(index + step + size, size)},
                device_id_type=MESH,
            )

        def sends(way, hop):
            if way == 0:
                return (index + 1 < size) & (index - hop + 1 >= 0)
            return (index - 1 >= 0) & (index + hop - 1 < size)

        def receives(way, hop):
            return index - hop >= 0 if way == 0 else index + hop < size

        for way in range(2):

            @pl.when(sends(way, 1))
            def _():
                copy(way, 1, True).start()

        own = pltpu.make_async_copy(v_ref, out_ref.at[:, index], own_sem)
        own.start()
        yield
        for hop in range(1, size):
            for way in range(2):

                @pl.when(receives(way, hop))
                def _():
                    arrival(way, hop).wait_recv()

                if hop + 1 < size:

                    @pl.when(sends(way, hop + 1))
                    def _():
                        copy(way, hop + 1, False).start()

            yield
        own.wait()
        for hop in range(1, size):
            for way in range(2):

                @pl.when(sends(way, hop))
                def _():
                    copy(way, hop, hop == 1).wait_send()


class LineScatter:
    def __init__(self, v, axis):
        self.axis, self.size = axis, lax.axis_size(axis)
        lead, total, rows, width = v.shape
        self.lead, self.rows = lead, rows
        if not isinstance(v, jax.ShapeDtypeStruct):
            v = v.reshape(lead, total * rows, width)
        dma = pltpu.SemaphoreType.DMA
        self.inputs = [(v, pltpu.VMEM)]
        self.outputs = [(jax.ShapeDtypeStruct((lead, rows, width), F32), pltpu.VMEM)]
        self.scratch = [
            pltpu.VMEM((2, total, lead, rows, width), v.dtype),
            dma((2, total)),
            dma((2, total)),
        ]

    greets = LineGather.greets

    def run(self, v_ref, out_ref, held, send_sem, recv_sem):
        index, size, rows = lax.axis_index(self.axis), self.size, self.rows

        def block(target):
            return pl.ds(pl.multiple_of(target * rows, rows), rows)

        def ours(lead, target):
            return lambda at: v_ref[
                lead, pl.ds(pl.multiple_of(target * rows + at.start, 16), 16), :
            ]

        def copy(way, target, first):
            step = 1 - 2 * way
            return pltpu.make_async_remote_copy(
                src_ref=v_ref.at[:, block(target)] if first else held.at[way, target],
                dst_ref=held.at[way, target],
                send_sem=send_sem.at[way, target],
                recv_sem=recv_sem.at[way, target],
                device_id={self.axis: lax.rem(index + step + size, size)},
                device_id_type=MESH,
            )

        def start(way):
            return index == 0 if way == 0 else index == size - 1

        def between(way, target):
            return (index > 0) & (index < target) if way == 0 else (index < size - 1) & (index > target)

        def targets(way):
            return range(size - 1, 0, -1) if way == 0 else range(size - 1)

        for way in range(2):

            @pl.when(start(way))
            def _():
                copy(way, targets(way)[0], True).start()

        yield
        def hand_on(way, position):
            target = targets(way)[position]
            if position + 1 < size - 1:

                @pl.when(start(way))
                def _():
                    copy(way, target, True).wait_send()
                    copy(way, targets(way)[position + 1], True).start()

            @pl.when(between(way, target))
            def _():
                copy(way, target, False).wait_recv()
                for lead in range(self.lead):

                    def store(at, value):
                        held[way, target, lead, at, :] = value.astype(BF16)

                    add_rows(
                        store,
                        [
                            lambda at: held[way, target, lead, at, :],
                            ours(lead, target),
                        ],
                        self.rows,
                    )
                copy(way, target, False).start()

        for position in range(size - 1):
            @pl.when(index < size // 2)
            def _():
                hand_on(0, position)
                hand_on(1, position)

            @pl.when(index >= size // 2)
            def _():
                hand_on(1, position)
                hand_on(0, position)

            yield
        for way in range(2):

            @pl.when(jnp.logical_not(start(way)))
            def _():
                copy(way, index, False).wait_recv()

        for lead in range(self.lead):

            def store(at, value, lead=lead):
                out_ref[lead, at, :] = value

            own = [ours(lead, index)]
            right = [lambda at, lead=lead: held[0, index, lead, at, :]]
            left = [lambda at, lead=lead: held[1, index, lead, at, :]]

            @pl.when(index == 0)
            def _():
                add_rows(store, own + left, self.rows)

            @pl.when(index == size - 1)
            def _():
                add_rows(store, own + right, self.rows)

            @pl.when((index > 0) & (index < size - 1))
            def _():
                add_rows(store, own + right + left, self.rows)

        for way in range(2):

            @pl.when(start(way))
            def _():
                copy(way, targets(way)[size - 2], True).wait_send()

            for target in targets(way):

                @pl.when(between(way, target))
                def _():
                    copy(way, target, False).wait_send()


class GroupScatter:
    def __init__(self, v, axes):
        self.axes = axes
        self.sizes, self.pairs = group_sizes(axes)
        tail = v.shape[1:]
        self.across = self.pairs == 4 and tail[0] % 32 == 0
        v = v.reshape((self.pairs, 2) + tail)
        self.rows = tail[0]
        dma = pltpu.SemaphoreType.DMA
        self.inputs = [(v, pl.ANY)]
        self.outputs = [(jax.ShapeDtypeStruct(tail, BF16), pltpu.VMEM)]
        self.scratch = [pltpu.VMEM((self.pairs,) + tail, BF16)] * 4 + [
            pltpu.VMEM((2, tail[0] // 2 if self.across else 16) + tail[1:], BF16),
            dma,
            dma,
            dma,
            dma((self.pairs,)),
            dma((self.pairs,)),
            dma((2,)),
            dma((2,)),
        ]

    def greets(self):
        chip, core, device = group_layout(self.axes, self.sizes)
        bits = self.pairs.bit_length() - 1
        return [device(chip, 1 - core)] + [
            device(flip(chip, mask, bits), core) for mask in range(1, self.pairs)
        ]

    def run(
        self,
        v_ref,
        out_ref,
        mine,
        peer,
        summed,
        held,
        passed,
        load_sem,
        swap_send,
        swap_recv,
        sum_send,
        sum_recv,
        pass_send,
        pass_recv,
    ):
        pairs, rows = self.pairs, self.rows
        bits = pairs.bit_length() - 1
        chip, core, device = group_layout(self.axes, self.sizes)
        swap = pltpu.make_async_remote_copy(
            src_ref=v_ref.at[:, 1 - core],
            dst_ref=peer,
            send_sem=swap_send,
            recv_sem=swap_recv,
            device_id=device(chip, 1 - core),
            device_id_type=MESH,
        )
        swap.start()
        load = pltpu.make_async_copy(v_ref.at[:, core], mine, load_sem)
        load.start()
        yield

        def push(mask):
            return pltpu.make_async_remote_copy(
                src_ref=summed.at[mask],
                dst_ref=held.at[mask],
                send_sem=sum_send.at[mask],
                recv_sem=sum_recv.at[mask],
                device_id=device(flip(chip, mask, bits), core),
                device_id_type=MESH,
            )

        middle = rows // 2
        halves = (pl.ds(0, middle), pl.ds(middle, rows - middle))

        def pass_on(part):
            return pltpu.make_async_remote_copy(
                src_ref=summed.at[3, halves[part]],
                dst_ref=passed.at[part],
                send_sem=pass_send.at[part],
                recv_sem=pass_recv.at[part],
                device_id=device(flip(chip, part + 1, bits), core),
                device_id_type=MESH,
            )

        load.wait()
        swap.wait()
        for mask in range(pairs - 1, -1, -1):
            target = flip(chip, mask, bits)

            def store(at, value, mask=mask):
                summed[mask, at, :] = value.astype(BF16)

            add_rows(
                store,
                [
                    lambda at, target=target: mine[target, at, :],
                    lambda at, target=target: peer[target, at, :],
                ],
                rows,
            )
            if self.across and mask == 3:
                for part in range(2):
                    pass_on(part).start()
            if not self.across and mask:
                push(mask).start()
        yield
        direct = (1, 2) if self.across else range(1, pairs)
        if self.across:
            for part in range(2):
                pass_on(part).wait_recv()
                mask = 2 - part
                start = part * middle

                def store(at, value, mask=mask, start=start):
                    summed[mask, pl.ds(pl.multiple_of(start + at.start, 16), 16), :] = value.astype(
                        BF16
                    )

                add_rows(
                    store,
                    [
                        lambda at, mask=mask, start=start: summed[
                            mask, pl.ds(pl.multiple_of(start + at.start, 16), 16), :
                        ],
                        lambda at, part=part: passed[part, at, :],
                    ],
                    middle,
                )
                push(mask).start()
        yield
        for mask in direct:
            push(mask).wait_recv()

        def finish(at, value):
            out_ref[at, :] = value.astype(BF16)

        add_rows(
            finish,
            [lambda at: summed[0, at, :]]
            + [lambda at, mask=mask: held[mask, at, :] for mask in direct],
            rows,
        )
        yield
        for mask in direct:
            push(mask).wait_send()
        if self.across:
            for part in range(2):
                pass_on(part).wait_send()


class GroupGather:
    def __init__(self, v, axes):
        self.axes = axes
        self.sizes, self.pairs = group_sizes(axes)
        self.rows = v.shape[0]
        self.across = self.pairs == 4 and v.shape[0] % 32 == 0
        dma = pltpu.SemaphoreType.DMA
        self.inputs = [(v, pltpu.VMEM)]
        self.outputs = [(jax.ShapeDtypeStruct((self.pairs, 2) + v.shape, v.dtype), pl.ANY)]
        self.scratch = [dma] + [dma((self.pairs,))] * 4 + [dma((2,))] * 2

    greets = GroupScatter.greets

    def run(
        self,
        v_ref,
        out_ref,
        own_sem,
        push_send,
        push_recv,
        relay_send,
        relay_recv,
        pass_send,
        pass_recv,
    ):
        pairs, rows = self.pairs, self.rows
        bits = pairs.bit_length() - 1
        chip, core, device = group_layout(self.axes, self.sizes)
        middle = rows // 2
        halves = (pl.ds(0, middle), pl.ds(middle, rows - middle))

        def push(mask, source):
            return pltpu.make_async_remote_copy(
                src_ref=v_ref,
                dst_ref=out_ref.at[source, core],
                send_sem=push_send.at[mask],
                recv_sem=push_recv.at[mask],
                device_id=device(flip(chip, mask, bits), core),
                device_id_type=MESH,
            )

        def pass_on(mask, source, part):
            return pltpu.make_async_remote_copy(
                src_ref=out_ref.at[source, core, halves[part]],
                dst_ref=out_ref.at[source, core, halves[part]],
                send_sem=pass_send.at[part],
                recv_sem=pass_recv.at[part],
                device_id=device(flip(chip, mask, bits), core),
                device_id_type=MESH,
            )

        def relay(mask, side):
            source = flip(chip, mask, bits)
            return pltpu.make_async_remote_copy(
                src_ref=v_ref if mask == 0 else out_ref.at[source, side],
                dst_ref=out_ref.at[source, side],
                send_sem=relay_send.at[mask],
                recv_sem=relay_recv.at[mask],
                device_id=device(chip, 1 - core),
                device_id_type=MESH,
            )

        direct = (1, 2) if self.across else tuple(range(1, pairs))
        for mask in direct:
            push(mask, chip).start()
        relay(0, core).start()
        own = pltpu.make_async_copy(v_ref, out_ref.at[chip, core], own_sem)
        own.start()
        yield
        for mask in direct:
            push(mask, flip(chip, mask, bits)).wait_recv()
            if self.across:
                pass_on(3 - mask, flip(chip, mask, bits), mask - 1).start()
            relay(mask, core).start()
        yield
        if self.across:
            for part in range(2):
                pass_on(part + 1, flip(chip, 3, bits), part).wait_recv()
            relay(3, core).start()
        own.wait()
        yield
        for mask in range(pairs):
            relay(mask, 1 - core).wait_recv()
        for mask in range(pairs):
            relay(mask, core).wait_send()
            if mask in direct:
                push(mask, chip).wait_send()
                if self.across:
                    pass_on(3 - mask, flip(chip, mask, bits), mask - 1).wait_send()


class ContextThenLine:
    def __init__(self, values, axes, axis):
        self.first = [GroupScatter(v, axes) for v in values]
        rows, width = values[0].shape[1:]
        total = lax.axis_size(axis)
        self.second = LineScatter(
            jax.ShapeDtypeStruct((len(values), total, rows // total, width), BF16), axis
        )
        self.inputs = [entry for job in self.first for entry in job.inputs]
        self.outputs = self.second.outputs
        self.scratch = [pltpu.VMEM((len(values), rows, width), BF16)]
        self.scratch += [entry for job in self.first for entry in job.scratch]
        self.scratch += self.second.scratch

    def greets(self):
        return [device for job in self.first + [self.second] for device in job.greets()]

    def run(self, *refs):
        refs = list(refs)
        count = len(self.first)
        inputs, out_ref, between, refs = refs[:count], refs[count], refs[count + 1], refs[count + 2 :]
        steps = []
        for number, job in enumerate(self.first):
            used = len(job.scratch)
            steps.append(job.run(inputs[number], between.at[number], *refs[:used]))
            refs = refs[used:]
        for _ in zip(*steps):
            yield
        for step in steps:
            for _ in step:
                pass
        yield from self.second.run(between, out_ref, *refs)


class GroupSum:
    def __init__(self, v, axes):
        self.first = GroupScatter(v, axes)
        self.second = GroupGather(jax.ShapeDtypeStruct(v.shape[1:], BF16), axes)
        self.inputs, self.outputs = self.first.inputs, self.second.outputs
        self.scratch = [pltpu.VMEM(v.shape[1:], BF16)] + self.first.scratch + self.second.scratch
        self.greets = self.first.greets

    def run(self, v_ref, out_ref, between, *refs):
        used = len(self.first.scratch)
        yield from self.first.run(v_ref, between, *refs[:used])
        yield from self.second.run(between, out_ref, *refs[used:])


def exchange_kernel(jobs, *refs):
    refs = list(refs)
    taken = [[], [], []]
    for number, part in enumerate(("inputs", "outputs", "scratch")):
        for job in jobs:
            count = len(getattr(job, part))
            taken[number].append(refs[:count])
            refs = refs[count:]
    meet([device for job in jobs for device in job.greets()])
    running = [
        job.run(*taken[0][at], *taken[1][at], *taken[2][at]) for at, job in enumerate(jobs)
    ]
    while running:
        left = []
        for step in running:
            try:
                next(step)
                left.append(step)
            except StopIteration:
                pass
        running = left


def exchange(jobs, collective_id, micros):
    inputs = [entry for job in jobs for entry in job.inputs]
    outputs = [entry for job in jobs for entry in job.outputs]
    return pl.pallas_call(
        functools.partial(exchange_kernel, jobs),
        out_shape=tuple(shape for shape, _ in outputs),
        in_specs=[pl.BlockSpec(memory_space=space) for _, space in inputs],
        out_specs=tuple(pl.BlockSpec(memory_space=space) for _, space in outputs),
        scratch_shapes=[entry for job in jobs for entry in job.scratch],
        compiler_params=pltpu.CompilerParams(
            collective_id=collective_id, has_side_effects=True, vmem_limit_bytes=56 * MIB
        ),
        cost_estimate=pl.CostEstimate(
            flops=0, bytes_accessed=3_600_000 * micros, transcendentals=0
        ),
        name="exchange_" + "_".join(type(job).__name__ for job in jobs[:3]),
    )(*[value for value, _ in inputs])


def turn(vectors, cosine, sine):
    half_dim = vectors.shape[-1] // 2
    swapped = jnp.concatenate([vectors[:, half_dim:], vectors[:, :half_dim]], axis=1)
    return vectors * cosine + swapped * sine


def head_scores(query, key_nope, key_rope, allowed):
    raw = mm_nt(query[:, :NOPE], key_nope) + mm_nt(query[:, NOPE:], key_rope)
    return jnp.where(allowed, raw * (NOPE + ROPE) ** (-0.5), -1e30)


def allowed_keys(row_ref, column_ref, row_place_ref, column_place_ref):
    return (row_ref[0] == column_ref[0]) & (column_place_ref[...] <= row_place_ref[...])


def attend_kernel(
    x_ref,
    kv_ref,
    row_ref,
    column_ref,
    row_place_ref,
    column_place_ref,
    cos_ref,
    sin_ref,
    query_w,
    up_w,
    out_w,
    part_ref,
    attended_ref,
    query_ref,
    expanded_ref,
    log_ref,
):
    heads = query_w.shape[1] // (NOPE + ROPE)
    allowed = allowed_keys(row_ref, column_ref, row_place_ref, column_place_ref)
    latent = kv_ref[0, :, :LATENT]
    key_rope = kv_ref[0, :, LATENT:]
    query = mm(x_ref[...], query_w[...])
    for head in range(heads):
        start = head * (NOPE + ROPE)
        rope = turn(query[:, start + NOPE : start + NOPE + ROPE], cos_ref[...], sin_ref[...])
        query_ref[0, head, :, :NOPE] = query[:, start : start + NOPE].astype(BF16)
        query_ref[0, head, :, NOPE:] = rope.astype(BF16)
        at = slice(head * (NOPE + VDIM), (head + 1) * (NOPE + VDIM))
        expanded_ref[0, :, at] = mm(latent, up_w[:, at]).astype(BF16)
        key_nope = expanded_ref[0, :, at.start : at.start + NOPE]
        values = expanded_ref[0, :, at.start + NOPE : at.stop]
        scores = head_scores(query_ref[0, head], key_nope, key_rope, allowed)
        top = jnp.max(scores, axis=-1, keepdims=True)
        weights = jnp.where(allowed, jnp.exp(scores - top), 0.0)
        total = jnp.sum(weights, axis=-1, keepdims=True)
        log_ref[0, head] = top + jnp.log(total)
        probs = (weights / total).astype(BF16)
        attended_ref[:, head * VDIM : (head + 1) * VDIM] = mm(probs, values).astype(BF16)
    part_ref[...] = mm(attended_ref[...], out_w[...]).astype(BF16)


def attend_back_kernel(
    grad_ref,
    attended_ref,
    x_ref,
    kv_ref,
    row_ref,
    column_ref,
    row_place_ref,
    column_place_ref,
    cos_ref,
    sin_ref,
    query_ref,
    expanded_ref,
    log_ref,
    query_w,
    up_w,
    out_w,
    kv_grad_ref,
    x_grad_ref,
    query_w_ref,
    up_w_ref,
    out_w_ref,
    query_grad,
    expanded_grad,
):
    heads = query_w.shape[1] // (NOPE + ROPE)
    scale = (NOPE + ROPE) ** (-0.5)
    allowed = allowed_keys(row_ref, column_ref, row_place_ref, column_place_ref)
    latent = kv_ref[0, :, :LATENT]
    key_rope = kv_ref[0, :, LATENT:]
    grad = grad_ref[...]
    attended_grad = mm_nt(grad, out_w[...]).astype(BF16)
    rope_grad = jnp.zeros((kv_ref.shape[1], ROPE), F32)
    for head in range(heads):
        first = head * (NOPE + VDIM)
        key_nope = expanded_ref[0, :, first : first + NOPE]
        values = expanded_ref[0, :, first + NOPE : first + NOPE + VDIM]
        query = query_ref[0, head]
        scores = head_scores(query, key_nope, key_rope, allowed)
        probs = jnp.where(allowed, jnp.exp(scores - log_ref[0, head]), 0.0)
        own_grad = attended_grad[:, head * VDIM : (head + 1) * VDIM]
        probs_grad = mm_nt(own_grad, values)
        moved = probs * (probs_grad - jnp.sum(probs * probs_grad, axis=-1, keepdims=True))
        moved = moved.astype(BF16)
        expanded_grad[:, first : first + NOPE] = (
            scale * mm_tn(moved, query[:, :NOPE])
        ).astype(BF16)
        expanded_grad[:, first + NOPE : first + NOPE + VDIM] = mm_tn(
            probs.astype(BF16), own_grad
        ).astype(BF16)
        rope_grad = rope_grad + mm_tn(moved, query[:, NOPE:])
        start = head * (NOPE + ROPE)
        query_grad[:, start : start + NOPE] = (scale * mm(moved, key_nope)).astype(BF16)
        query_grad[:, start + NOPE : start + NOPE + ROPE] = turn(
            scale * mm(moved, key_rope), cos_ref[...], -sin_ref[...]
        ).astype(BF16)
    kv_grad_ref[0, :, :LATENT] = mm_nt(expanded_grad[...], up_w[...]).astype(BF16)
    kv_grad_ref[0, :, LATENT:] = (scale * rope_grad).astype(BF16)
    x_grad_ref[...] = mm_nt(query_grad[...], query_w[...]).astype(BF16)
    pieces = (
        (query_w_ref, x_ref[...], query_grad[...]),
        (up_w_ref, latent, expanded_grad[...]),
        (out_w_ref, attended_ref[...], grad),
    )

    @pl.when(pl.program_id(0) == 0)
    def _():
        for target, left, right in pieces:
            target[...] = mm_tn(left, right)

    @pl.when(pl.program_id(0) > 0)
    def _():
        for target, left, right in pieces:
            target[...] += mm_tn(left, right)


def attention_specs(micro_count, rows, seq_len, heads):
    per_micro = lambda *shape: pl.BlockSpec((1,) + shape, lambda m: (m,) + (0,) * len(shape))
    rows_of = lambda width: pl.BlockSpec((rows, width), lambda m: (m, 0))
    whole = lambda *shape: pl.BlockSpec(
        shape, lambda m: (0,) * len(shape), pipeline_mode=pl.Buffered(1)
    )
    places = [
        per_micro(rows, 1),
        per_micro(1, seq_len),
        whole(rows, 1),
        whole(1, seq_len),
        whole(rows, ROPE),
        whole(rows, ROPE),
    ]
    weights = [
        whole(D, heads * (NOPE + ROPE)),
        whole(LATENT, heads * (NOPE + VDIM)),
        whole(heads * VDIM, D),
    ]
    kept = [
        rows_of(heads * VDIM),
        per_micro(heads, rows, NOPE + ROPE),
        per_micro(seq_len, heads * (NOPE + VDIM)),
        per_micro(heads, rows, 1),
    ]
    return per_micro, rows_of, whole, places, weights, kept


def attend(x_attn, kv_all, places, weights, micro_count, heads):
    rows, seq_len = x_attn.shape[0] // micro_count, kv_all.shape[1]
    per_micro, rows_of, _, place_specs, weight_specs, kept = attention_specs(
        micro_count, rows, seq_len, heads
    )
    total = micro_count * rows
    return pl.pallas_call(
        attend_kernel,
        grid=(micro_count,),
        in_specs=[rows_of(D), per_micro(seq_len, LATENT + ROPE)] + place_specs + weight_specs,
        out_specs=[rows_of(D)] + kept,
        out_shape=[
            jax.ShapeDtypeStruct((total, D), BF16),
            jax.ShapeDtypeStruct((total, heads * VDIM), BF16),
            jax.ShapeDtypeStruct((micro_count, heads, rows, NOPE + ROPE), BF16),
            jax.ShapeDtypeStruct((micro_count, seq_len, heads * (NOPE + VDIM)), BF16),
            jax.ShapeDtypeStruct((micro_count, heads, rows, 1), F32),
        ],
        compiler_params=pltpu.CompilerParams(vmem_limit_bytes=56 * MIB),
        cost_estimate=pl.CostEstimate(
            flops=9_000_000_000, bytes_accessed=60_000_000, transcendentals=0
        ),
        name="attend",
    )(x_attn, kv_all, *places, *weights)


def attend_back(grad, x_attn, kv_all, places, weights, kept, micro_count, heads):
    rows, seq_len = x_attn.shape[0] // micro_count, kv_all.shape[1]
    per_micro, rows_of, whole, place_specs, weight_specs, kept_specs = attention_specs(
        micro_count, rows, seq_len, heads
    )
    total = micro_count * rows
    return pl.pallas_call(
        attend_back_kernel,
        grid=(micro_count,),
        in_specs=[rows_of(D), kept_specs[0], rows_of(D), per_micro(seq_len, LATENT + ROPE)]
        + place_specs
        + kept_specs[1:]
        + weight_specs,
        out_specs=[per_micro(seq_len, LATENT + ROPE), rows_of(D)] + weight_specs,
        out_shape=[
            jax.ShapeDtypeStruct((micro_count, seq_len, LATENT + ROPE), BF16),
            jax.ShapeDtypeStruct((total, D), BF16),
            jax.ShapeDtypeStruct(weights[0].shape, F32),
            jax.ShapeDtypeStruct(weights[1].shape, F32),
            jax.ShapeDtypeStruct(weights[2].shape, F32),
        ],
        scratch_shapes=[
            pltpu.VMEM((rows, heads * (NOPE + ROPE)), BF16),
            pltpu.VMEM((seq_len, heads * (NOPE + VDIM)), BF16),
        ],
        compiler_params=pltpu.CompilerParams(vmem_limit_bytes=60 * MIB),
        cost_estimate=pl.CostEstimate(
            flops=20_000_000_000, bytes_accessed=100_000_000, transcendentals=0
        ),
        name="attend_back",
    )(grad, kept[0], x_attn, kv_all, *places, *kept[1:], *weights)


PEER_SLOTS = 4


def expert_kernel(
    pairs,
    context_size,
    fe,
    x_ref,
    cot_ref,
    gate_in,
    up_in,
    down_in,
    router_in,
    shared_gate_in,
    shared_up_in,
    shared_down_in,
    out_ref,
    part_ref,
    gate_out,
    up_out,
    down_out,
    router_out,
    shared_out,
    shared_part,
    shared_grads,
    x_all,
    gate_ref,
    up_ref,
    down_ref,
    x_tile,
    cot_tile,
    out_tile,
    grad_tile,
    peer_tile,
    grad_gate,
    grad_up,
    hidden_low,
    gate_acc,
    up_acc,
    down_acc,
    x_send,
    x_recv,
    relay_send,
    relay_recv,
    pass_send,
    pass_recv,
    x_load,
    cot_load,
    out_store,
    swap_send,
    swap_recv,
    sum_send,
    sum_recv,
    weight_load,
    grad_store,
    shared_store,
    acc_store,
    credit,
):
    micro_count, rows = x_ref.shape[0], x_ref.shape[1]
    units = gate_ref.shape[0]
    shared_units = shared_gate_in.shape[0]
    half = units // EXP_DEV
    experts = 2 * pairs * EXP_DEV
    bits = pairs.bit_length() - 1
    steps = micro_count * pairs
    across = pairs == 4
    place = lax.axis_index("dp") * context_size + lax.axis_index("context")
    core = lax.rem(place, 2)
    chip = lax.div(place, 2)

    def device(chip_index, core_index):
        index = chip_index * 2 + core_index
        return {"dp": lax.div(index, context_size), "context": lax.rem(index, context_size)}

    sibling = device(chip, 1 - core)
    meet([sibling] + [device(flip(chip, mask, bits), core) for mask in range(1, pairs)])

    def step_of(step):
        micro = lax.div(step, pairs)
        turn = lax.rem(step, pairs)
        backward = lax.rem(micro, 2)
        return micro, lax.rem(turn + backward, pairs)

    def push_x(micro, mask):
        return pltpu.make_async_remote_copy(
            src_ref=x_ref.at[micro],
            dst_ref=x_all.at[micro, chip, core],
            send_sem=x_send.at[micro, mask],
            recv_sem=x_recv.at[micro, mask],
            device_id=device(flip(chip, mask, bits), core),
            device_id_type=MESH,
        )

    def relay(micro, mask, own=False):
        source = flip(chip, mask, bits)
        return pltpu.make_async_remote_copy(
            src_ref=x_ref.at[micro] if own else x_all.at[micro, source, core],
            dst_ref=x_all.at[micro, source, core],
            send_sem=relay_send.at[micro, mask],
            recv_sem=relay_recv.at[micro, mask],
            device_id=sibling,
            device_id_type=MESH,
        )

    def relay_arrival(micro, mask):
        source = flip(chip, mask, bits)
        return pltpu.make_async_remote_copy(
            src_ref=x_all.at[micro, source, 1 - core],
            dst_ref=x_all.at[micro, source, 1 - core],
            send_sem=relay_send.at[micro, mask],
            recv_sem=relay_recv.at[micro, mask],
            device_id=sibling,
            device_id_type=MESH,
        )

    def x_arrival(micro, mask):
        return pltpu.make_async_remote_copy(
            src_ref=x_ref.at[micro],
            dst_ref=x_all.at[micro, flip(chip, mask, bits), core],
            send_sem=x_send.at[micro, mask],
            recv_sem=x_recv.at[micro, mask],
            device_id=device(flip(chip, mask, bits), core),
            device_id_type=MESH,
        )

    middle = rows // 2
    parts = (pl.ds(0, middle), pl.ds(middle, rows - middle))

    def pass_on(micro, mask, source, part):
        return pltpu.make_async_remote_copy(
            src_ref=x_all.at[micro, source, core, parts[part]],
            dst_ref=x_all.at[micro, source, core, parts[part]],
            send_sem=pass_send.at[micro, part],
            recv_sem=pass_recv.at[micro, part],
            device_id=device(flip(chip, mask, bits), core),
            device_id_type=MESH,
        )

    def half_tile(side):
        return pl.ds(pl.multiple_of(side * rows, rows), rows)

    def load_cot(step):
        micro, mask = step_of(step)
        slot = lax.rem(step, 2)
        source = flip(chip, mask, bits)
        return [
            pltpu.make_async_copy(
                cot_ref.at[2 * source + side, micro],
                cot_tile.at[slot, half_tile(side)],
                cot_load.at[slot, side],
            )
            for side in range(2)
        ]

    def load_own(step):
        slot = lax.rem(step, 2)
        return pltpu.make_async_copy(
            x_ref.at[step_of(step)[0]], x_tile.at[slot, half_tile(core)], x_load.at[slot, 0]
        )

    def load_x(step, number):
        micro, mask = step_of(step)
        slot = lax.rem(step, 2)
        side = core if number == 0 else 1 - core
        return pltpu.make_async_copy(
            x_all.at[micro, flip(chip, mask, bits), side],
            x_tile.at[slot, half_tile(side)],
            x_load.at[slot, number],
        )

    def store(step):
        micro, mask = step_of(step)
        return [
            pltpu.make_async_copy(
                out_tile.at[pl.ds(side * rows, rows)],
                out_ref.at[2 * flip(chip, mask, bits) + side, micro],
                out_store.at[side],
            )
            for side in range(2)
        ]

    def swap(step):
        slot = lax.rem(step, 2)
        held = lax.rem(step, PEER_SLOTS)
        return pltpu.make_async_remote_copy(
            src_ref=grad_tile.at[pl.ds(pl.multiple_of((1 - core) * rows, rows), rows)],
            dst_ref=peer_tile.at[held],
            send_sem=swap_send.at[slot],
            recv_sem=swap_recv.at[held],
            device_id=sibling,
            device_id_type=MESH,
        )

    def push_sum(step):
        micro, mask = step_of(step)
        slot = lax.rem(step, PEER_SLOTS)
        return pltpu.make_async_remote_copy(
            src_ref=peer_tile.at[slot],
            dst_ref=part_ref.at[micro, mask],
            send_sem=sum_send.at[slot],
            recv_sem=sum_recv.at[micro, mask],
            device_id=device(flip(chip, mask, bits), core),
            device_id_type=MESH,
        )

    def keep_sum(step):
        micro, mask = step_of(step)
        slot = lax.rem(step, PEER_SLOTS)
        return pltpu.make_async_copy(
            peer_tile.at[slot], part_ref.at[micro, mask], sum_send.at[slot]
        )

    def wait_sum_sent(step):
        mask = step_of(step)[1]

        @pl.when(mask > 0)
        def _():
            push_sum(step).wait_send()

        @pl.when(mask == 0)
        def _():
            keep_sum(step).wait()

    def fetch(step):
        micro, mask = step_of(step)

        if not across:

            @pl.when(mask > 0)
            def _():
                x_arrival(micro, mask).wait_recv()
                relay(micro, mask).start()

        else:

            @pl.when((mask == 1) | (mask == 2))
            def _():
                x_arrival(micro, mask).wait_recv()
                relay(micro, mask).start()

            for part in range(2):

                @pl.when(mask == part + 1)
                def _():
                    pass_on(micro, 2 - part, flip(chip, part + 1, bits), part).start()

            @pl.when(mask == 3)
            def _():
                for part in range(2):
                    pass_on(micro, part + 1, flip(chip, 3, bits), part).wait_recv()
                relay(micro, mask).start()

        for copy in load_cot(step):
            copy.start()

        @pl.when(mask == 0)
        def _():
            load_own(step).start()

        @pl.when(mask > 0)
        def _():
            load_x(step, 0).start()

    def fetch_relayed(step):
        micro, mask = step_of(step)
        relay_arrival(micro, mask).wait_recv()
        load_x(step, 1).start()

    def finish_sum(step):
        slot = lax.rem(step, 2)
        held = lax.rem(step, PEER_SLOTS)
        swap(step).wait()

        def add(index, carry):
            at = pl.ds(pl.multiple_of(index * 16, 16), 16)
            mine = pl.ds(pl.multiple_of(core * rows + index * 16, 16), 16)
            value = grad_tile[mine, :].astype(F32) + peer_tile[held, at, :].astype(F32)
            peer_tile[held, at, :] = value.astype(BF16)
            return carry

        lax.fori_loop(0, rows // 16, add, 0)

        mask = step_of(step)[1]

        @pl.when(mask > 0)
        def _():
            push_sum(step).start()

        @pl.when(mask == 0)
        def _():
            keep_sum(step).start()

    direct = (1, 2) if across else tuple(range(1, pairs))
    for mask in direct:
        push_x(0, mask).start()
    for micro in range(micro_count):
        relay(micro, 0, own=True).start()

    def weights_in(pieces):
        copies = []
        for number, (source, target, start) in enumerate(pieces):
            copies.append(
                pltpu.make_async_copy(
                    source, target.at[pl.ds(start, source.shape[0])], weight_load.at[number]
                )
            )
        return copies

    shared_weights = weights_in(
        [(shared_gate_in, gate_ref, 0), (shared_up_in, up_ref, 0), (shared_down_in, down_ref, 0)]
    )
    for copy in shared_weights:
        copy.start()
    shared_rows = []
    for micro in range(micro_count):
        at = pl.ds(micro * rows, rows)
        shared_rows.append(
            pltpu.make_async_copy(x_ref.at[micro], x_tile.at[1, at], x_load.at[1, micro])
        )
        shared_rows.append(
            pltpu.make_async_copy(cot_ref.at[place, micro], cot_tile.at[1, at], cot_load.at[1, micro])
        )
    for copy in shared_rows:
        copy.start()
    for target in (gate_ref, up_ref, down_ref):
        target[shared_units:, :] = jnp.zeros((units - shared_units, D), BF16)
    fetch(0)

    chunk = 256 if units % 256 == 0 else LANES
    out_chunk = 512
    slab = half - LANES
    first_lane = fe % LANES
    slab_chunk = slab // chunk * chunk

    def hidden_pass(x, cot, here, start, gate, scale):
        at = slice(start, start + chunk)
        up = mm_nt(x, up_ref[at, :])
        back = mm_nt(cot, down_ref[at, :])
        sig = jax.nn.sigmoid(gate)
        act = gate * sig
        hidden = act * up
        grad_hidden = back if scale is None else back * scale
        scaled = hidden if scale is None else hidden * scale
        hidden_low[here, at] = scaled.astype(BF16)
        grad_gate[here, at] = (grad_hidden * up * (sig * (1.0 + gate * (1.0 - sig)))).astype(BF16)
        grad_up[here, at] = (grad_hidden * act).astype(BF16)
        return hidden * back

    def grad_pass():
        for start in range(0, D, out_chunk):
            at = slice(start, start + out_chunk)
            grad = mm(grad_gate[...], gate_ref[:, at]) + mm(grad_up[...], up_ref[:, at])
            grad_tile[:, at] = grad.astype(BF16)

    def out_pass():
        for start in range(0, D, out_chunk):
            at = slice(start, start + out_chunk)
            out_tile[:, at] = mm(hidden_low[...], down_ref[:, at]).astype(BF16)

    for copy in shared_weights + shared_rows:
        copy.wait()
    row_halves = (slice(0, rows), slice(rows, 2 * rows))
    for here in row_halves:
        x, cot = x_tile[1, here, :D], cot_tile[1, here]
        for start in range(0, units, chunk):
            gate = mm_nt(x, gate_ref[start : start + chunk, :])
            hidden_pass(x, cot, here, start, gate, None)
    grad_pass()
    out_pass()
    expert_weights = weights_in(
        [
            piece
            for number in range(EXP_DEV)
            for piece in (
                (gate_in.at[number], gate_ref, number * half),
                (up_in.at[number], up_ref, number * half),
                (down_in.at[number], down_ref, number * half),
            )
        ]
        + [(router_in, gate_ref, fe)]
    )
    for copy in expert_weights:
        copy.start()
    for target in (gate_ref, up_ref, down_ref):
        for number in range(EXP_DEV):
            first = number * half + fe
            if target is gate_ref and number == 0:
                first += experts
            last = (number + 1) * half
            if last > first:
                target[first:last, :] = jnp.zeros((last - first, D), BF16)
    shared_stores = []
    for micro in range(micro_count):
        at = pl.ds(micro * rows, rows)
        shared_stores.append(
            pltpu.make_async_copy(out_tile.at[at], shared_out.at[micro], shared_store.at[micro, 0])
        )
        shared_stores.append(
            pltpu.make_async_copy(
                grad_tile.at[at], shared_part.at[micro], shared_store.at[micro, 1]
            )
        )
    for copy in shared_stores:
        copy.start()
    fetch_relayed(0)
    for copy in shared_stores:
        copy.wait()
    staged = []
    for which, (left, right) in enumerate(
        ((grad_gate, x_tile[1, :, :D]), (grad_up, x_tile[1, :, :D]), (hidden_low, cot_tile[1]))
    ):
        for start in range(0, units, rows):
            stage = len(staged) % 2 * rows
            if len(staged) >= 2:
                staged[-2].wait()
            out_tile[stage : stage + rows, :] = mm_tn(
                left[:, start : start + rows], right
            ).astype(BF16)
            copy = pltpu.make_async_copy(
                out_tile.at[pl.ds(stage, rows)],
                shared_grads.at[which, pl.ds(start, rows)],
                grad_store.at[len(staged) % 2],
            )
            copy.start()
            staged.append(copy)
    for acc in (gate_acc, up_acc, down_acc):
        acc[...] = jnp.zeros_like(acc)
    for copy in staged[-2:] + expert_weights:
        copy.wait()

    def work(step, carry):
        slot = lax.rem(step, 2)

        for copy in load_cot(step):
            copy.wait()
        for number in range(2):
            load_x(step, number).wait()

        for here in row_halves:
            x = x_tile[slot, here, :D]
            chosen = x_tile[slot, here, D:].astype(F32)
            cot = cot_tile[slot, here]
            lane = lax.broadcasted_iota(jnp.int32, (rows, LANES), 1) - first_lane
            valid = (lane >= 0) & (lane < experts)

            first_gate = mm_nt(x, gate_ref[slab_chunk : slab_chunk + chunk, :])
            slab_gate = first_gate[:, slab - slab_chunk : slab - slab_chunk + LANES]
            logits = jnp.where(valid, slab_gate, -1e30)
            weights = jnp.where(
                valid, jnp.exp(logits - jnp.max(logits, axis=-1, keepdims=True)), 0.0
            )
            router_probs = weights / jnp.sum(weights, axis=-1, keepdims=True)
            named = router_probs * chosen
            picks = [lane == place * EXP_DEV + number for number in range(EXP_DEV)]
            scales = [
                jnp.sum(jnp.where(pick, named, 0.0), axis=-1, keepdims=True) for pick in picks
            ]
            flags = [
                jnp.sum(jnp.where(pick, chosen, 0.0), axis=-1, keepdims=True) for pick in picks
            ]
            dots = [jnp.zeros((rows, 1), F32) for _ in picks]
            column = lax.broadcasted_iota(jnp.int32, (rows, chunk), 1)
            starts = [slab_chunk] + [at for at in range(0, units, chunk) if at != slab_chunk]
            for start in starts:
                if start == slab_chunk:
                    gate = first_gate
                else:
                    gate = mm_nt(x, gate_ref[start : start + chunk, :])
                first, last = start // half, (start + chunk - 1) // half
                scale = scales[first]
                if last > first:
                    scale = jnp.where(column < last * half - start, scales[first], scales[last])
                product = hidden_pass(x, cot, here, start, gate, scale)
                if last > first:
                    split = last * half - start
                    dots[first] = dots[first] + jnp.sum(product[:, :split], axis=-1, keepdims=True)
                    dots[last] = dots[last] + jnp.sum(product[:, split:], axis=-1, keepdims=True)
                else:
                    dots[first] = dots[first] + jnp.sum(product, axis=-1, keepdims=True)
            spread = jnp.zeros((rows, LANES), F32)
            for pick, dot, flag in zip(picks, dots, flags):
                spread = spread + jnp.where(pick, dot * flag, 0.0)
            grad_logits = router_probs * (
                spread - jnp.sum(router_probs * spread, axis=-1, keepdims=True)
            )
            grad_gate[here, slab:half] = jnp.where(
                lane < 0, grad_gate[here, slab:half].astype(F32), grad_logits
            ).astype(BF16)

        @pl.when(step + 1 < steps)
        def _():
            fetch(step + 1)

        @pl.when(step == 1)
        def _():
            for micro in range(1, micro_count):
                for mask in direct:
                    push_x(micro, mask).start()

        @pl.when(step >= 1)
        def _():
            finish_sum(step - 1)

        @pl.when(step >= PEER_SLOTS)
        def _():
            wait_sum_sent(step - PEER_SLOTS)
            pl.semaphore_signal(credit, inc=1, device_id=sibling, device_id_type=MESH)
            pl.semaphore_wait(credit, 1)

        grad_pass()
        swap(step).start()


        @pl.when(step >= 1)
        def _():
            for copy in store(step - 1):
                copy.wait()

        out_pass()
        for copy in store(step):
            copy.start()

        @pl.when(step + 1 < steps)
        def _():
            fetch_relayed(step + 1)

        for acc, left, right in (
            (gate_acc, grad_gate, x_tile),
            (up_acc, grad_up, x_tile),
            (down_acc, hidden_low, cot_tile),
        ):
            for start in range(0, D, out_chunk):
                at = slice(start, start + out_chunk)
                acc[:, at] += mm_tn(left[...], right[slot, :, at])
        return carry


    lax.fori_loop(0, steps, work, 0)
    finals = [
        pltpu.make_async_copy(
            gate_acc.at[pl.ds(fe, experts)], router_out, acc_store.at[EXP_DEV, 0]
        )
    ]
    for number in range(EXP_DEV):
        for which, (acc, target) in enumerate(
            ((gate_acc, gate_out), (up_acc, up_out), (down_acc, down_out))
        ):
            finals.append(
                pltpu.make_async_copy(
                    acc.at[pl.ds(number * half, fe)],
                    target.at[number],
                    acc_store.at[number, which],
                )
            )
    for copy in finals:
        copy.start()
    finish_sum(steps - 1)
    for back in range(PEER_SLOTS, 0, -1):
        wait_sum_sent(steps - back)
    for copy in finals:
        copy.wait()
    for copy in store(steps - 1):
        copy.wait()
    for micro in range(micro_count):
        if across:
            for part in range(2):
                pass_on(micro, 2 - part, flip(chip, part + 1, bits), part).wait_send()
        for mask in range(pairs):
            relay(micro, mask).wait_send()
            if mask in direct:
                push_x(micro, mask).wait_send()
            if mask:
                pltpu.make_async_remote_copy(
                    src_ref=peer_tile.at[0],
                    dst_ref=part_ref.at[micro, mask],
                    send_sem=sum_send.at[0],
                    recv_sem=sum_recv.at[micro, mask],
                    device_id=device(flip(chip, mask, bits), core),
                    device_id_type=MESH,
                ).wait_recv()


def expert_pass(
    x_ext, cot_all, gate_w, up_w, down_w, router_w, shared_gate, shared_up, shared_down, collective_id
):
    micro_count, rows, width = x_ext.shape
    context_size = lax.axis_size("context")
    pairs = lax.axis_size("dp") * context_size // 2
    fe, experts, shared_units = gate_w.shape[1], router_w.shape[0], shared_gate.shape[0]
    half = -(-(fe + experts) // LANES) * LANES
    units = EXP_DEV * half
    dma = pltpu.SemaphoreType.DMA
    wide = jax.ShapeDtypeStruct((EXP_DEV, fe, D), F32)
    own = jax.ShapeDtypeStruct((micro_count, rows, D), BF16)
    return pl.pallas_call(
        functools.partial(expert_kernel, pairs, context_size, fe),
        out_shape=(
            jax.ShapeDtypeStruct((2 * pairs, micro_count, rows, D), BF16),
            jax.ShapeDtypeStruct((micro_count, pairs, rows, D), BF16),
            wide,
            wide,
            wide,
            jax.ShapeDtypeStruct((experts, D), F32),
            own,
            own,
            jax.ShapeDtypeStruct((3, units, D), BF16),
            jax.ShapeDtypeStruct((micro_count, pairs, 2, rows, width), BF16),
        ),
        in_specs=[pl.BlockSpec(memory_space=pl.ANY)] * 9,
        out_specs=(pl.BlockSpec(memory_space=pl.ANY),) * 10,
        scratch_shapes=[
            pltpu.VMEM((units, D), BF16),
            pltpu.VMEM((units, D), BF16),
            pltpu.VMEM((units, D), BF16),
            pltpu.VMEM((2, 2 * rows, width), BF16),
            pltpu.VMEM((2, 2 * rows, D), BF16),
            pltpu.VMEM((2 * rows, D), BF16),
            pltpu.VMEM((2 * rows, D), BF16),
            pltpu.VMEM((PEER_SLOTS, rows, D), BF16),
            pltpu.VMEM((2 * rows, units), BF16),
            pltpu.VMEM((2 * rows, units), BF16),
            pltpu.VMEM((2 * rows, units), BF16),
            pltpu.VMEM((units, D), F32),
            pltpu.VMEM((units, D), F32),
            pltpu.VMEM((units, D), F32),
            dma((micro_count, pairs)),
            dma((micro_count, pairs)),
            dma((micro_count, pairs)),
            dma((micro_count, pairs)),
            dma((micro_count, 2)),
            dma((micro_count, 2)),
            dma((2, 2)),
            dma((2, 2)),
            dma((2,)),
            dma((2,)),
            dma((PEER_SLOTS,)),
            dma((PEER_SLOTS,)),
            dma((micro_count, pairs)),
            dma((3 * EXP_DEV + 1,)),
            dma((2,)),
            dma((micro_count, 2)),
            dma((EXP_DEV + 1, 3)),
            pltpu.SemaphoreType.REGULAR,
        ],
        compiler_params=pltpu.CompilerParams(
            collective_id=collective_id, has_side_effects=True, vmem_limit_bytes=62 * MIB
        ),
        cost_estimate=pl.CostEstimate(
            flops=36 * (pairs * micro_count + 1) * rows * D * units,
            bytes_accessed=500_000_000,
            transcendentals=0,
        ),
        name="expert_pass",
    )(x_ext, cot_all, gate_w, up_w, down_w, router_w, shared_gate, shared_up, shared_down)[:9]


def per_device(
    tokens,
    segments,
    expert_ids,
    norm_attn,
    w_query,
    w_kv_down,
    norm_latent,
    w_kv_up,
    w_out,
    norm_ffn,
    w_router,
    w_shared_gate,
    w_shared_up,
    w_shared_down,
    w_expert_gate,
    w_expert_up,
    w_expert_down,
    cotangent,
):
    micro_count, block_rows = tokens.shape[:2]
    rows = micro_count * block_rows
    seq_len = segments.shape[1]
    context_size = lax.axis_size("context")
    groups = lax.axis_size("dp") * context_size
    tensor_size = lax.axis_size("tensor")
    group_index = lax.axis_index("dp") * context_size + lax.axis_index("context")
    own_rows = block_rows // tensor_size
    own_start = lax.axis_index("tensor") * own_rows
    experts = EXP_DEV * groups
    heads_local = w_query.shape[1] // (NOPE + ROPE)
    fe_local = w_expert_gate.shape[2]
    start_row = lax.axis_index("context") * block_rows
    query_index = start_row + jnp.arange(block_rows)
    key_index = jnp.arange(seq_len)
    cos_block, sin_block = angles(query_index.astype(F32), ROPE)
    cos_query = jnp.tile(cos_block, (micro_count, 1))
    sin_query = jnp.tile(sin_block, (micro_count, 1))
    gain_attn = norm_attn.astype(F32)
    gain_latent = norm_latent.astype(F32)
    gain_ffn = norm_ffn.astype(F32)

    def own(values):
        values = values.reshape((micro_count, block_rows) + values.shape[1:])
        part = lax.dynamic_slice_in_dim(values, own_start, own_rows, axis=1)
        return part.reshape((micro_count * own_rows,) + values.shape[2:])

    def to_owner(values):
        values = values.astype(BF16).reshape(micro_count, tensor_size, own_rows, values.shape[-1])
        return LineScatter(values, "tensor")

    def from_owners(values):
        return LineGather(values.reshape(micro_count, own_rows, values.shape[-1]), "tensor")

    def flat(values):
        return values.reshape(-1, values.shape[-1])

    ff_local = w_shared_gate.shape[1]
    slots = jnp.arange(LANES) - fe_local % LANES
    named = jnp.any(expert_ids[..., None] == slots, axis=2).astype(BF16)

    x_rows = tokens.reshape(rows, D).astype(F32)
    cot_rows = cotangent.reshape(rows, D)
    inv_attn = rms_scale(x_rows)
    normed_attn = x_rows * inv_attn
    x_attn = (normed_attn * gain_attn).astype(BF16)
    kv_raw = mm(x_attn, w_kv_down)
    latent_raw = kv_raw[:, :LATENT]
    inv_latent = rms_scale(latent_raw)
    normed_latent = latent_raw * inv_latent
    latent = (normed_latent * gain_latent).astype(BF16)
    key_rope = rotate(kv_raw[:, LATENT:], cos_query, sin_query).astype(BF16)
    kv_own = jnp.concatenate([latent, key_rope], axis=1)
    kv_all = exchange(
        [GroupGather(part, ("context",)) for part in jnp.split(kv_own, micro_count)], 1, 20
    )
    kv_all = jnp.concatenate([flat(part) for part in kv_all], axis=0)
    kv_all, cot_late = lax.optimization_barrier((kv_all, cotangent))
    cot_all = lax.all_gather(cot_late, GROUP, axis=0)
    kv_all = kv_all.reshape(micro_count, seq_len, LATENT + ROPE)
    seg_query = lax.dynamic_slice_in_dim(segments, start_row, block_rows, axis=1)
    places = (
        seg_query[:, :, None],
        segments[:, None, :],
        query_index[:, None],
        key_index[None, :],
        jnp.tile(cos_block, (1, 2)),
        jnp.concatenate([-sin_block, sin_block], axis=1),
    )
    weights = (w_query, w_kv_up, w_out)
    attn_part, *kept = attend(x_attn, kv_all, places, weights, micro_count, heads_local)
    (attn_sum,) = exchange([to_owner(attn_part)], 2, 40)
    hidden_one = own(x_rows) + flat(attn_sum)
    inv_ffn = rms_scale(hidden_one)
    normed_ffn = hidden_one * inv_ffn
    x_ffn = (normed_ffn * gain_ffn).astype(BF16)
    (x_ffn,) = exchange([from_owners(x_ffn)], 3, 40)
    x_ffn = flat(x_ffn.reshape(rows, D))
    x_ext = jnp.concatenate([x_ffn.reshape(micro_count, block_rows, D), named], axis=-1)

    (
        out_part,
        grad_part,
        gate_grad,
        up_grad,
        down_grad,
        router_grad,
        shared_out,
        shared_part,
        shared_grads,
    ) = expert_pass(
        x_ext,
        cot_all,
        w_expert_gate.transpose(0, 2, 1),
        w_expert_up.transpose(0, 2, 1),
        w_expert_down,
        w_router.T,
        w_shared_gate.T,
        w_shared_up.T,
        w_shared_down,
        4,
    )
    grad_sum = jnp.sum(grad_part.astype(F32), axis=1) + shared_part.astype(F32)
    grad_sum = grad_sum.reshape(rows, D)
    shared_units = shared_grads.shape[1]
    shared_grads = shared_grads.reshape(groups, -1, D)
    shared_grads = lax.psum_scatter(shared_grads, GROUP, scatter_dimension=0, tiled=False)
    out_sum = lax.psum_scatter(out_part, GROUP, scatter_dimension=0, tiled=False)
    (grad_x_ffn,) = exchange([to_owner(grad_sum)], 5, 40)
    grad_x_ffn = flat(grad_x_ffn)

    norm_ffn_grad = jnp.sum(grad_x_ffn * normed_ffn, axis=0)
    grad_one = own(cot_rows).astype(F32) + norm_back(grad_x_ffn * gain_ffn, normed_ffn, inv_ffn)
    (grad_attn_low,) = exchange([from_owners(grad_one.astype(BF16))], 6, 40)
    grad_attn_low = grad_attn_low.reshape(rows, D)
    grad_kv_part, grad_x_heads, query_grad, kv_up_grad, out_grad = attend_back(
        grad_attn_low, x_attn, kv_all, places, weights, kept, micro_count, heads_local
    )
    grad_x_heads, shared_grads = lax.optimization_barrier((grad_x_heads, shared_grads))
    shared_grads = lax.all_gather(shared_grads, GROUP, axis=0, tiled=True)
    router_part = router_grad.T.astype(BF16).reshape(tensor_size, micro_count, own_rows, -1)
    router_part = router_part.transpose(1, 0, 2, 3).reshape(rows, -1)
    late, grad_kv, query_part, kv_up_part, out_grad = exchange(
        [
            to_owner(jnp.concatenate([grad_x_heads, router_part], axis=1)),
            ContextThenLine(
                [
                    grad_kv_part[m].reshape(context_size, block_rows, LATENT + ROPE)
                    for m in range(micro_count)
                ],
                ("context",),
                "tensor",
            ),
            GroupScatter(query_grad.astype(BF16).reshape(groups, D // groups, -1), GROUP),
            GroupScatter(kv_up_grad.astype(BF16).reshape(groups, LATENT // groups, -1), GROUP),
            GroupScatter(out_grad.astype(BF16).reshape(groups, -1, D), GROUP),
        ],
        8,
        50,
    )
    late = flat(late)
    late, out_sum = lax.optimization_barrier((late, out_sum))
    out_sum = out_sum.reshape(rows, D).astype(F32) + shared_out.reshape(rows, D).astype(F32)
    out_sum = out_sum.astype(BF16).reshape(micro_count, tensor_size, own_rows, D)
    out_sum = out_sum.transpose(1, 0, 2, 3)
    out_sum = lax.psum_scatter(out_sum, "tensor", scatter_dimension=0, tiled=False)
    grad_x_heads, router_own = late[:, :D], late[:, D:]
    grad_kv = flat(grad_kv)
    grad_latent, grad_rope_key = grad_kv[:, :LATENT], grad_kv[:, LATENT:]
    normed_latent_own = own(normed_latent)
    norm_latent_grad = jnp.sum(grad_latent * normed_latent_own, axis=0)
    grad_latent_raw = norm_back(grad_latent * gain_latent, normed_latent_own, own(inv_latent))
    grad_kv_raw = jnp.concatenate(
        [grad_latent_raw, unrotate(grad_rope_key, own(cos_query), own(sin_query))], axis=-1
    ).astype(BF16)
    grad_x_attn = grad_x_heads + mm_nt(grad_kv_raw, w_kv_down)
    normed_attn_own = own(normed_attn)
    norm_attn_grad = jnp.sum(grad_x_attn * normed_attn_own, axis=0)
    grad_input = grad_one + norm_back(grad_x_attn * gain_attn, normed_attn_own, own(inv_attn))
    finished, small, router_all, query_grad, kv_up_grad, out_grad = exchange(
        [
            from_owners(jnp.concatenate([grad_input.astype(BF16), grad_kv_raw], axis=1)),
            LineGather(
                jnp.concatenate([norm_attn_grad, norm_ffn_grad, norm_latent_grad]).reshape(
                    1, -1, LANES
                ),
                "tensor",
            ),
            LineGather(router_own.astype(BF16)[None], "tensor"),
            GroupGather(query_part, GROUP),
            GroupGather(kv_up_part, GROUP),
            GroupGather(out_grad, GROUP),
        ],
        9,
        60,
    )
    finished = finished.reshape(rows, -1)
    out_sum, finished = lax.optimization_barrier((out_sum, finished))
    output = (hidden_one + flat(out_sum).astype(F32)).astype(BF16)
    output = lax.all_gather(output, "tensor", axis=0)
    output = output.reshape(tensor_size, micro_count, own_rows, D).transpose(1, 0, 2, 3)
    grad_tokens, grad_kv_raw = finished[:, :D], finished[:, D:]
    kv_width = -(-grad_kv_raw.shape[1] // (16 * groups)) * 16 * groups
    grad_kv_raw = jnp.pad(grad_kv_raw, ((0, 0), (0, kv_width - grad_kv_raw.shape[1])))
    kv_down_grad = mm_tn(grad_kv_raw, x_attn).astype(BF16)
    small = jnp.sum(small, axis=(0, 1)).astype(BF16)
    kv_down_grad, router_grad, small = exchange(
        [
            GroupSum(part.reshape(groups, -1, part.shape[-1]), GROUP)
            for part in (
                kv_down_grad,
                router_all.reshape(groups * 16, -1),
                small.reshape(groups * 16, -1),
            )
        ],
        10,
        35,
    )
    kv_down_grad = kv_down_grad.reshape(-1, D)[: LATENT + ROPE].astype(F32).T
    router_grad = router_grad.reshape(D, experts).astype(F32)
    small = small.reshape(-1).astype(F32)
    return (
        output.reshape(tokens.shape),
        grad_tokens.reshape(tokens.shape),
        small[:D],
        flat(query_grad).reshape(D, -1).astype(F32),
        kv_down_grad,
        small[D + D :],
        kv_up_grad.reshape(LATENT, -1).astype(F32),
        out_grad.reshape(-1, D).astype(F32),
        small[D : D + D],
        router_grad,
        shared_grads[:ff_local].astype(F32).T,
        shared_grads[shared_units : shared_units + ff_local].astype(F32).T,
        shared_grads[2 * shared_units : 2 * shared_units + ff_local].astype(F32),
        gate_grad.transpose(0, 2, 1),
        up_grad.transpose(0, 2, 1),
        down_grad,
    )


def solution(mesh):
    return jax.shard_map(
        per_device,
        mesh=mesh,
        in_specs=(
            P("dp", "context", None),
            P("dp", None),
            P("dp", "context", None),
            P(),
            P(None, "tensor"),
            P(),
            P(),
            P(None, "tensor"),
            P("tensor", None),
            P(),
            P(),
            P(None, "tensor"),
            P(None, "tensor"),
            P("tensor", None),
            P(("dp", "context"), None, "tensor"),
            P(("dp", "context"), None, "tensor"),
            P(("dp", "context"), "tensor", None),
            P("dp", "context", None),
        ),
        out_specs=(
            P("dp", "context", None),
            P("dp", "context", None),
            P(),
            P(None, "tensor"),
            P(),
            P(),
            P(None, "tensor"),
            P("tensor", None),
            P(),
            P(),
            P(None, "tensor"),
            P(None, "tensor"),
            P("tensor", None),
            P(("dp", "context"), None, "tensor"),
            P(("dp", "context"), None, "tensor"),
            P(("dp", "context"), "tensor", None),
        ),
        check_vma=False,
    )
```

```python
import functools

import jax
import jax.numpy as jnp
from jax import lax
from jax.experimental import pallas as pl
from jax.experimental.pallas import tpu as pltpu
from jax.sharding import PartitionSpec as P

D = 2048
NOPE = 128
ROPE = 64
VDIM = 128
LATENT = 512
TOP = 6
EXP_DEV = 2
LANES = 128
GROUP = ("dp", "context")
EVERY = ("dp", "context", "tensor")
BF16 = jnp.bfloat16
F32 = jnp.float32
MESH = pl.DeviceIdType.MESH
MIB = 1024 * 1024

EPS = 1e-06


def rms_scale(rows):
    return lax.rsqrt(jnp.mean(rows * rows, axis=-1, keepdims=True) + EPS)


def norm_back(grad_out, normed, inverse):
    return inverse * (grad_out - normed * jnp.mean(grad_out * normed, axis=-1, keepdims=True))


def angles(positions, rope_dim):
    frequency = 10000.0 ** (-(jnp.arange(rope_dim // 2).astype(jnp.float32) * 2.0) / rope_dim)
    turned = positions[:, None] * frequency[None, :]
    return (jnp.cos(turned), jnp.sin(turned))


def rotate(vectors, cosine, sine):
    half_dim = vectors.shape[-1] // 2
    front_part = vectors[..., :half_dim]
    back_part = vectors[..., half_dim:]
    return jnp.concatenate(
        [front_part * cosine - back_part * sine, front_part * sine + back_part * cosine], axis=-1
    )


def unrotate(vectors, cosine, sine):
    half_dim = vectors.shape[-1] // 2
    front_part = vectors[..., :half_dim]
    back_part = vectors[..., half_dim:]
    return jnp.concatenate(
        [front_part * cosine + back_part * sine, back_part * cosine - front_part * sine], axis=-1
    )


def mm(left, right):
    return jnp.dot(left, right, preferred_element_type=F32)


def mm_nt(left, right):
    return lax.dot_general(left, right, (((1,), (1,)), ((), ())), preferred_element_type=F32)


def mm_tn(left, right):
    return lax.dot_general(left, right, (((0,), (0,)), ((), ())), preferred_element_type=F32)


def ring(axes, sizes):
    place = 0
    total = 1
    for axis, size in zip(axes, sizes):
        place = place * size + lax.axis_index(axis)
        total *= size

    def coordinates(index):
        found = {}
        for axis, size in reversed(list(zip(axes, sizes))):
            found[axis] = lax.rem(index, size)
            index = lax.div(index, size)
        return found

    return place, total, coordinates


def meet(devices):
    barrier = pltpu.get_barrier_semaphore()
    for device in devices:
        pl.semaphore_signal(barrier, inc=1, device_id=device, device_id_type=MESH)
    pl.semaphore_wait(barrier, len(devices))


def flip(index, mask, bits):
    total = 0
    for bit in range(bits):
        weight = 1 << bit
        ours = lax.rem(lax.div(index, weight), 2)
        theirs = lax.rem(lax.div(mask, weight), 2)
        total = total + lax.rem(ours + theirs, 2) * weight
    return total


def group_layout(axes, sizes):
    place, _, coordinates = ring(axes, sizes)
    return lax.div(place, 2), lax.rem(place, 2), lambda chip, core: coordinates(chip * 2 + core)


def group_sizes(axes):
    sizes = tuple(lax.axis_size(axis) for axis in axes)
    pairs = 1
    for size in sizes:
        pairs *= size
    return sizes, pairs // 2


def add_rows(out, terms, rows):
    def add(index, carry):
        at = pl.ds(pl.multiple_of(index * 16, 16), 16)
        value = terms[0](at).astype(F32)
        for term in terms[1:]:
            value = value + term(at).astype(F32)
        out(at, value)
        return carry

    lax.fori_loop(0, rows // 16, add, 0)


class LineGather:
    def __init__(self, v, axis):
        self.axis, self.size = axis, lax.axis_size(axis)
        dma = pltpu.SemaphoreType.DMA
        self.inputs = [(v, pltpu.VMEM)]
        shape = (v.shape[0], self.size) + v.shape[1:]
        self.outputs = [(jax.ShapeDtypeStruct(shape, v.dtype), pl.ANY)]
        self.scratch = [dma((2, self.size)), dma((2, self.size)), dma]

    def greets(self):
        index = lax.axis_index(self.axis)
        return [
            {self.axis: lax.rem(index + step, self.size)} for step in (1, self.size - 1)
        ]

    def run(self, v_ref, out_ref, send_sem, recv_sem, own_sem):
        index, size = lax.axis_index(self.axis), self.size

        def copy(way, hop, first):
            step = 1 - 2 * way
            source = lax.rem(index - step * (hop - 1) + size, size)
            return pltpu.make_async_remote_copy(
                src_ref=v_ref if first else out_ref.at[:, source],
                dst_ref=out_ref.at[:, source],
                send_sem=send_sem.at[way, hop],
                recv_sem=recv_sem.at[way, hop],
                device_id={self.axis: lax.rem(index + step + size, size)},
                device_id_type=MESH,
            )

        def arrival(way, hop):
            step = 1 - 2 * way
            source = lax.rem(index - step * hop + size, size)
            return pltpu.make_async_remote_copy(
                src_ref=v_ref,
                dst_ref=out_ref.at[:, source],
                send_sem=send_sem.at[way, hop],
                recv_sem=recv_sem.at[way, hop],
                device_id={self.axis: lax.rem(index + step + size, size)},
                device_id_type=MESH,
            )

        def sends(way, hop):
            if way == 0:
                return (index + 1 < size) & (index - hop + 1 >= 0)
            return (index - 1 >= 0) & (index + hop - 1 < size)

        def receives(way, hop):
            return index - hop >= 0 if way == 0 else index + hop < size

        for way in range(2):

            @pl.when(sends(way, 1))
            def _():
                copy(way, 1, True).start()

        own = pltpu.make_async_copy(v_ref, out_ref.at[:, index], own_sem)
        own.start()
        yield
        for hop in range(1, size):
            for way in range(2):

                @pl.when(receives(way, hop))
                def _():
                    arrival(way, hop).wait_recv()

                if hop + 1 < size:

                    @pl.when(sends(way, hop + 1))
                    def _():
                        copy(way, hop + 1, False).start()

            yield
        own.wait()
        for hop in range(1, size):
            for way in range(2):

                @pl.when(sends(way, hop))
                def _():
                    copy(way, hop, hop == 1).wait_send()


class LineScatter:
    def __init__(self, v, axis):
        self.axis, self.size = axis, lax.axis_size(axis)
        lead, total, rows, width = v.shape
        self.lead, self.rows = lead, rows
        if not isinstance(v, jax.ShapeDtypeStruct):
            v = v.reshape(lead, total * rows, width)
        dma = pltpu.SemaphoreType.DMA
        self.inputs = [(v, pltpu.VMEM)]
        self.outputs = [(jax.ShapeDtypeStruct((lead, rows, width), F32), pltpu.VMEM)]
        self.scratch = [
            pltpu.VMEM((2, total, lead, rows, width), v.dtype),
            dma((2, total)),
            dma((2, total)),
        ]

    greets = LineGather.greets

    def run(self, v_ref, out_ref, held, send_sem, recv_sem):
        index, size, rows = lax.axis_index(self.axis), self.size, self.rows

        def block(target):
            return pl.ds(pl.multiple_of(target * rows, rows), rows)

        def ours(lead, target):
            return lambda at: v_ref[
                lead, pl.ds(pl.multiple_of(target * rows + at.start, 16), 16), :
            ]

        def copy(way, target, first):
            step = 1 - 2 * way
            return pltpu.make_async_remote_copy(
                src_ref=v_ref.at[:, block(target)] if first else held.at[way, target],
                dst_ref=held.at[way, target],
                send_sem=send_sem.at[way, target],
                recv_sem=recv_sem.at[way, target],
                device_id={self.axis: lax.rem(index + step + size, size)},
                device_id_type=MESH,
            )

        def start(way):
            return index == 0 if way == 0 else index == size - 1

        def between(way, target):
            return (index > 0) & (index < target) if way == 0 else (index < size - 1) & (index > target)

        def targets(way):
            return range(size - 1, 0, -1) if way == 0 else range(size - 1)

        for way in range(2):

            @pl.when(start(way))
            def _():
                copy(way, targets(way)[0], True).start()

        yield
        def hand_on(way, position):
            target = targets(way)[position]
            if position + 1 < size - 1:

                @pl.when(start(way))
                def _():
                    copy(way, target, True).wait_send()
                    copy(way, targets(way)[position + 1], True).start()

            @pl.when(between(way, target))
            def _():
                copy(way, target, False).wait_recv()
                for lead in range(self.lead):

                    def store(at, value):
                        held[way, target, lead, at, :] = value.astype(BF16)

                    add_rows(
                        store,
                        [
                            lambda at: held[way, target, lead, at, :],
                            ours(lead, target),
                        ],
                        self.rows,
                    )
                copy(way, target, False).start()

        for position in range(size - 1):
            @pl.when(index < size // 2)
            def _():
                hand_on(0, position)
                hand_on(1, position)

            @pl.when(index >= size // 2)
            def _():
                hand_on(1, position)
                hand_on(0, position)

            yield
        for way in range(2):

            @pl.when(jnp.logical_not(start(way)))
            def _():
                copy(way, index, False).wait_recv()

        for lead in range(self.lead):

            def store(at, value, lead=lead):
                out_ref[lead, at, :] = value

            own = [ours(lead, index)]
            right = [lambda at, lead=lead: held[0, index, lead, at, :]]
            left = [lambda at, lead=lead: held[1, index, lead, at, :]]

            @pl.when(index == 0)
            def _():
                add_rows(store, own + left, self.rows)

            @pl.when(index == size - 1)
            def _():
                add_rows(store, own + right, self.rows)

            @pl.when((index > 0) & (index < size - 1))
            def _():
                add_rows(store, own + right + left, self.rows)

        for way in range(2):

            @pl.when(start(way))
            def _():
                copy(way, targets(way)[size - 2], True).wait_send()

            for target in targets(way):

                @pl.when(between(way, target))
                def _():
                    copy(way, target, False).wait_send()


class GroupScatter:
    def __init__(self, v, axes, pick=None):
        self.axes, self.pick = axes, pick
        self.sizes, self.pairs = group_sizes(axes)
        tail = v.shape[1:] if pick is None else v.shape[2:]
        self.across = self.pairs == 4 and tail[0] % 32 == 0
        v = v.reshape((self.pairs, 2) + v.shape[1:])
        self.rows = tail[0]
        dma = pltpu.SemaphoreType.DMA
        self.inputs = [(v, pl.ANY)]
        self.outputs = [(jax.ShapeDtypeStruct(tail, BF16), pltpu.VMEM)]
        self.scratch = [pltpu.VMEM((self.pairs,) + tail, BF16)] * 4 + [
            pltpu.VMEM((2, tail[0] // 2 if self.across else 16) + tail[1:], BF16),
            dma,
            dma,
            dma,
            dma((self.pairs,)),
            dma((self.pairs,)),
            dma((2,)),
            dma((2,)),
        ]

    def greets(self):
        chip, core, device = group_layout(self.axes, self.sizes)
        bits = self.pairs.bit_length() - 1
        return [device(chip, 1 - core)] + [
            device(flip(chip, mask, bits), core) for mask in range(1, self.pairs)
        ]

    def run(
        self,
        v_ref,
        out_ref,
        mine,
        peer,
        summed,
        held,
        passed,
        load_sem,
        swap_send,
        swap_recv,
        sum_send,
        sum_recv,
        pass_send,
        pass_recv,
    ):
        pairs, rows = self.pairs, self.rows
        bits = pairs.bit_length() - 1
        chip, core, device = group_layout(self.axes, self.sizes)

        def side(which):
            if self.pick is None:
                return v_ref.at[:, which]
            return v_ref.at[:, which, self.pick]

        swap = pltpu.make_async_remote_copy(
            src_ref=side(1 - core),
            dst_ref=peer,
            send_sem=swap_send,
            recv_sem=swap_recv,
            device_id=device(chip, 1 - core),
            device_id_type=MESH,
        )
        swap.start()
        load = pltpu.make_async_copy(side(core), mine, load_sem)
        load.start()
        yield

        def push(mask):
            return pltpu.make_async_remote_copy(
                src_ref=summed.at[mask],
                dst_ref=held.at[mask],
                send_sem=sum_send.at[mask],
                recv_sem=sum_recv.at[mask],
                device_id=device(flip(chip, mask, bits), core),
                device_id_type=MESH,
            )

        middle = rows // 2
        halves = (pl.ds(0, middle), pl.ds(middle, rows - middle))

        def pass_on(part):
            return pltpu.make_async_remote_copy(
                src_ref=summed.at[3, halves[part]],
                dst_ref=passed.at[part],
                send_sem=pass_send.at[part],
                recv_sem=pass_recv.at[part],
                device_id=device(flip(chip, part + 1, bits), core),
                device_id_type=MESH,
            )

        load.wait()
        swap.wait()
        for mask in range(pairs - 1, -1, -1):
            target = flip(chip, mask, bits)

            def store(at, value, mask=mask):
                summed[mask, at, :] = value.astype(BF16)

            add_rows(
                store,
                [
                    lambda at, target=target: mine[target, at, :],
                    lambda at, target=target: peer[target, at, :],
                ],
                rows,
            )
            if self.across and mask == 3:
                for part in range(2):
                    pass_on(part).start()
            if not self.across and mask:
                push(mask).start()
        yield
        direct = (1, 2) if self.across else range(1, pairs)
        if self.across:
            for part in range(2):
                pass_on(part).wait_recv()
                mask = 2 - part
                start = part * middle

                def store(at, value, mask=mask, start=start):
                    summed[mask, pl.ds(pl.multiple_of(start + at.start, 16), 16), :] = value.astype(
                        BF16
                    )

                add_rows(
                    store,
                    [
                        lambda at, mask=mask, start=start: summed[
                            mask, pl.ds(pl.multiple_of(start + at.start, 16), 16), :
                        ],
                        lambda at, part=part: passed[part, at, :],
                    ],
                    middle,
                )
                push(mask).start()
        yield
        for mask in direct:
            push(mask).wait_recv()

        def finish(at, value):
            out_ref[at, :] = value.astype(BF16)

        add_rows(
            finish,
            [lambda at: summed[0, at, :]]
            + [lambda at, mask=mask: held[mask, at, :] for mask in direct],
            rows,
        )
        yield
        for mask in direct:
            push(mask).wait_send()
        if self.across:
            for part in range(2):
                pass_on(part).wait_send()


class GroupGather:
    def __init__(self, v, axes):
        self.axes = axes
        self.sizes, self.pairs = group_sizes(axes)
        self.rows = v.shape[0]
        self.across = self.pairs == 4 and v.shape[0] % 32 == 0
        dma = pltpu.SemaphoreType.DMA
        self.inputs = [(v, pltpu.VMEM)]
        self.outputs = [(jax.ShapeDtypeStruct((self.pairs, 2) + v.shape, v.dtype), pl.ANY)]
        self.scratch = [dma] + [dma((self.pairs,))] * 4 + [dma((2,))] * 2

    greets = GroupScatter.greets

    def run(
        self,
        v_ref,
        out_ref,
        own_sem,
        push_send,
        push_recv,
        relay_send,
        relay_recv,
        pass_send,
        pass_recv,
    ):
        pairs, rows = self.pairs, self.rows
        bits = pairs.bit_length() - 1
        chip, core, device = group_layout(self.axes, self.sizes)
        middle = rows // 2
        halves = (pl.ds(0, middle), pl.ds(middle, rows - middle))

        def push(mask, source):
            return pltpu.make_async_remote_copy(
                src_ref=v_ref,
                dst_ref=out_ref.at[source, core],
                send_sem=push_send.at[mask],
                recv_sem=push_recv.at[mask],
                device_id=device(flip(chip, mask, bits), core),
                device_id_type=MESH,
            )

        def pass_on(mask, source, part):
            return pltpu.make_async_remote_copy(
                src_ref=out_ref.at[source, core, halves[part]],
                dst_ref=out_ref.at[source, core, halves[part]],
                send_sem=pass_send.at[part],
                recv_sem=pass_recv.at[part],
                device_id=device(flip(chip, mask, bits), core),
                device_id_type=MESH,
            )

        def relay(mask, side):
            source = flip(chip, mask, bits)
            return pltpu.make_async_remote_copy(
                src_ref=v_ref if mask == 0 else out_ref.at[source, side],
                dst_ref=out_ref.at[source, side],
                send_sem=relay_send.at[mask],
                recv_sem=relay_recv.at[mask],
                device_id=device(chip, 1 - core),
                device_id_type=MESH,
            )

        direct = (1, 2) if self.across else tuple(range(1, pairs))
        for mask in direct:
            push(mask, chip).start()
        relay(0, core).start()
        own = pltpu.make_async_copy(v_ref, out_ref.at[chip, core], own_sem)
        own.start()
        yield
        for mask in direct:
            push(mask, flip(chip, mask, bits)).wait_recv()
            if self.across:
                pass_on(3 - mask, flip(chip, mask, bits), mask - 1).start()
            relay(mask, core).start()
        yield
        if self.across:
            for part in range(2):
                pass_on(part + 1, flip(chip, 3, bits), part).wait_recv()
            relay(3, core).start()
        own.wait()
        yield
        for mask in range(pairs):
            relay(mask, 1 - core).wait_recv()
        for mask in range(pairs):
            relay(mask, core).wait_send()
            if mask in direct:
                push(mask, chip).wait_send()
                if self.across:
                    pass_on(3 - mask, flip(chip, mask, bits), mask - 1).wait_send()


class ContextThenLine:
    def __init__(self, values, axes, axis):
        self.first = [GroupScatter(v, axes) for v in values]
        rows, width = values[0].shape[1:]
        total = lax.axis_size(axis)
        self.second = LineScatter(
            jax.ShapeDtypeStruct((len(values), total, rows // total, width), BF16), axis
        )
        self.inputs = [entry for job in self.first for entry in job.inputs]
        self.outputs = self.second.outputs
        self.scratch = [pltpu.VMEM((len(values), rows, width), BF16)]
        self.scratch += [entry for job in self.first for entry in job.scratch]
        self.scratch += self.second.scratch

    def greets(self):
        return [device for job in self.first + [self.second] for device in job.greets()]

    def run(self, *refs):
        refs = list(refs)
        count = len(self.first)
        inputs, out_ref, between, refs = refs[:count], refs[count], refs[count + 1], refs[count + 2 :]
        steps = []
        for number, job in enumerate(self.first):
            used = len(job.scratch)
            steps.append(job.run(inputs[number], between.at[number], *refs[:used]))
            refs = refs[used:]
        for _ in zip(*steps):
            yield
        for step in steps:
            for _ in step:
                pass
        yield from self.second.run(between, out_ref, *refs)


class SumThenShare:
    def __init__(self, parts, extras, finish, shares, results):
        self.parts, self.finish = parts, finish
        self.gathers = [LineGather(share, "tensor") for share in shares]
        self.counts = (len(extras), len(results))
        self.inputs = [entry for job in parts for entry in job.inputs]
        self.inputs += [(extra, pltpu.VMEM) for extra in extras]
        self.outputs = [entry for job in self.gathers for entry in job.outputs]
        self.outputs += [(result, pltpu.VMEM) for result in results]
        self.scratch = [pltpu.VMEM(shape.shape, shape.dtype) for job in parts for shape, _ in job.outputs]
        self.scratch += [pltpu.VMEM(share.shape, share.dtype) for share in shares]
        for job in parts + self.gathers:
            self.scratch += job.scratch

    def greets(self):
        return [device for job in self.parts + self.gathers[:1] for device in job.greets()]

    def run(self, *refs):
        refs = list(refs)

        def take(count):
            taken = refs[:count]
            del refs[:count]
            return taken

        part_inputs = [take(len(job.inputs)) for job in self.parts]
        extras = take(self.counts[0])
        outputs = take(len(self.gathers))
        results = take(self.counts[1])
        sums = take(len(self.parts))
        shares = take(len(self.gathers))
        running = [
            job.run(*inputs, total, *take(len(job.scratch)))
            for job, inputs, total in zip(self.parts, part_inputs, sums)
        ]
        gathers = [
            job.run(share, output, *take(len(job.scratch)))
            for job, share, output in zip(self.gathers, shares, outputs)
        ]
        yield from side_by_side(running)
        self.finish(sums, extras, shares, results)
        yield from side_by_side(gathers)


def side_by_side(running):
    while running:
        left = []
        for step in running:
            try:
                next(step)
                left.append(step)
            except StopIteration:
                pass
        running = left
        yield


class GroupSum:
    def __init__(self, v, axes):
        self.first = GroupScatter(v, axes)
        self.second = GroupGather(jax.ShapeDtypeStruct(v.shape[1:], BF16), axes)
        self.inputs, self.outputs = self.first.inputs, self.second.outputs
        self.scratch = [pltpu.VMEM(v.shape[1:], BF16)] + self.first.scratch + self.second.scratch
        self.greets = self.first.greets

    def run(self, v_ref, out_ref, between, *refs):
        used = len(self.first.scratch)
        yield from self.first.run(v_ref, between, *refs[:used])
        yield from self.second.run(between, out_ref, *refs[used:])


def exchange_kernel(jobs, *refs):
    refs = list(refs)
    taken = [[], [], []]
    for number, part in enumerate(("inputs", "outputs", "scratch")):
        for job in jobs:
            count = len(getattr(job, part))
            taken[number].append(refs[:count])
            refs = refs[count:]
    meet([device for job in jobs for device in job.greets()])
    running = [
        job.run(*taken[0][at], *taken[1][at], *taken[2][at]) for at, job in enumerate(jobs)
    ]
    for _ in side_by_side(running):
        pass


def exchange(jobs, collective_id, micros):
    inputs = [entry for job in jobs for entry in job.inputs]
    outputs = [entry for job in jobs for entry in job.outputs]
    return pl.pallas_call(
        functools.partial(exchange_kernel, jobs),
        out_shape=tuple(shape for shape, _ in outputs),
        in_specs=[pl.BlockSpec(memory_space=space) for _, space in inputs],
        out_specs=tuple(pl.BlockSpec(memory_space=space) for _, space in outputs),
        scratch_shapes=[entry for job in jobs for entry in job.scratch],
        compiler_params=pltpu.CompilerParams(
            collective_id=collective_id, has_side_effects=True, vmem_limit_bytes=56 * MIB
        ),
        cost_estimate=pl.CostEstimate(
            flops=0, bytes_accessed=360_000 * micros, transcendentals=0
        ),
        name="exchange_" + "_".join(type(job).__name__ for job in jobs[:3]),
    )(*[value for value, _ in inputs])


KV_WIDTH = 640


def turn(vectors, cosine, sine):
    half_dim = vectors.shape[-1] // 2
    swapped = jnp.concatenate([vectors[:, half_dim:], vectors[:, :half_dim]], axis=1)
    return vectors * cosine + swapped * sine


def head_scores(query, key_nope, key_rope, allowed):
    raw = mm_nt(query[:, :NOPE], key_nope) + mm_nt(query[:, NOPE:], key_rope)
    return jnp.where(allowed, raw * (NOPE + ROPE) ** (-0.5), -1e30)


def allowed_keys(row_ref, column_ref, row_place_ref, column_place_ref):
    return (row_ref[0] == column_ref[0]) & (column_place_ref[...] <= row_place_ref[...])


def attend_kernel(
    x_ref,
    kv_ref,
    row_ref,
    column_ref,
    row_place_ref,
    column_place_ref,
    cos_ref,
    sin_ref,
    query_w,
    up_w,
    out_w,
    part_ref,
    attended_ref,
    query_ref,
    expanded_ref,
    log_ref,
):
    heads = query_w.shape[1] // (NOPE + ROPE)
    allowed = allowed_keys(row_ref, column_ref, row_place_ref, column_place_ref)
    latent = kv_ref[:, :LATENT]
    key_rope = kv_ref[:, LATENT : LATENT + ROPE]
    query = mm(x_ref[...], query_w[...])
    for head in range(heads):
        start = head * (NOPE + ROPE)
        rope = turn(query[:, start + NOPE : start + NOPE + ROPE], cos_ref[...], sin_ref[...])
        query_ref[0, head, :, :NOPE] = query[:, start : start + NOPE].astype(BF16)
        query_ref[0, head, :, NOPE:] = rope.astype(BF16)
        at = slice(head * (NOPE + VDIM), (head + 1) * (NOPE + VDIM))
        expanded_ref[0, :, at] = mm(latent, up_w[:, at]).astype(BF16)
        key_nope = expanded_ref[0, :, at.start : at.start + NOPE]
        values = expanded_ref[0, :, at.start + NOPE : at.stop]
        scores = head_scores(query_ref[0, head], key_nope, key_rope, allowed)
        top = jnp.max(scores, axis=-1, keepdims=True)
        weights = jnp.where(allowed, jnp.exp(scores - top), 0.0)
        total = jnp.sum(weights, axis=-1, keepdims=True)
        log_ref[0, head] = top + jnp.log(total)
        probs = (weights / total).astype(BF16)
        attended_ref[:, head * VDIM : (head + 1) * VDIM] = mm(probs, values).astype(BF16)
    part_ref[...] = mm(attended_ref[...], out_w[...]).astype(BF16)


def attend_back_kernel(
    grad_ref,
    attended_ref,
    x_ref,
    kv_ref,
    row_ref,
    column_ref,
    row_place_ref,
    column_place_ref,
    cos_ref,
    sin_ref,
    query_ref,
    expanded_ref,
    log_ref,
    query_w,
    up_w,
    out_w,
    kv_grad_ref,
    x_grad_ref,
    query_w_ref,
    up_w_ref,
    out_w_ref,
    query_grad,
    expanded_grad,
    query_w_sum,
    up_w_sum,
    out_w_sum,
):
    heads = query_w.shape[1] // (NOPE + ROPE)
    scale = (NOPE + ROPE) ** (-0.5)
    allowed = allowed_keys(row_ref, column_ref, row_place_ref, column_place_ref)
    latent = kv_ref[:, :LATENT]
    key_rope = kv_ref[:, LATENT : LATENT + ROPE]
    grad = grad_ref[...]
    attended_grad = mm_nt(grad, out_w[...]).astype(BF16)
    rope_grad = jnp.zeros((kv_ref.shape[0], ROPE), F32)
    for head in range(heads):
        first = head * (NOPE + VDIM)
        key_nope = expanded_ref[0, :, first : first + NOPE]
        values = expanded_ref[0, :, first + NOPE : first + NOPE + VDIM]
        query = query_ref[0, head]
        scores = head_scores(query, key_nope, key_rope, allowed)
        probs = jnp.where(allowed, jnp.exp(scores - log_ref[0, head]), 0.0)
        own_grad = attended_grad[:, head * VDIM : (head + 1) * VDIM]
        probs_grad = mm_nt(own_grad, values)
        moved = probs * (probs_grad - jnp.sum(probs * probs_grad, axis=-1, keepdims=True))
        moved = moved.astype(BF16)
        expanded_grad[:, first : first + NOPE] = (
            scale * mm_tn(moved, query[:, :NOPE])
        ).astype(BF16)
        expanded_grad[:, first + NOPE : first + NOPE + VDIM] = mm_tn(
            probs.astype(BF16), own_grad
        ).astype(BF16)
        rope_grad = rope_grad + mm_tn(moved, query[:, NOPE:])
        start = head * (NOPE + ROPE)
        query_grad[:, start : start + NOPE] = (scale * mm(moved, key_nope)).astype(BF16)
        query_grad[:, start + NOPE : start + NOPE + ROPE] = turn(
            scale * mm(moved, key_rope), cos_ref[...], -sin_ref[...]
        ).astype(BF16)
    kv_grad_ref[0, :, :LATENT] = mm_nt(expanded_grad[...], up_w[...]).astype(BF16)
    kv_grad_ref[0, :, LATENT:] = (scale * rope_grad).astype(BF16)
    x_grad_ref[...] = mm_nt(query_grad[...], query_w[...]).astype(BF16)
    pieces = (
        (query_w_sum, query_w_ref, x_ref[...], query_grad[...]),
        (up_w_sum, up_w_ref, latent, expanded_grad[...]),
        (out_w_sum, out_w_ref, attended_ref[...], grad),
    )
    step = pl.program_id(0)

    @pl.when(step == 0)
    def _():
        for total, _, left, right in pieces:
            total[...] = mm_tn(left, right)

    @pl.when(step > 0)
    def _():
        for total, _, left, right in pieces:
            total[...] += mm_tn(left, right)

    @pl.when(step == pl.num_programs(0) - 1)
    def _():
        for total, target, _, _ in pieces:
            target[...] = total[...].astype(BF16)


def attention_specs(micro_count, rows, seq_len, heads):
    per_micro = lambda *shape: pl.BlockSpec((1,) + shape, lambda m: (m,) + (0,) * len(shape))
    rows_of = lambda width: pl.BlockSpec((rows, width), lambda m: (m, 0))
    whole = lambda *shape: pl.BlockSpec(
        shape, lambda m: (0,) * len(shape), pipeline_mode=pl.Buffered(1)
    )
    places = [
        per_micro(rows, 1),
        per_micro(1, seq_len),
        whole(rows, 1),
        whole(1, seq_len),
        whole(rows, ROPE),
        whole(rows, ROPE),
    ]
    weights = [
        whole(D, heads * (NOPE + ROPE)),
        whole(LATENT, heads * (NOPE + VDIM)),
        whole(heads * VDIM, D),
    ]
    kept = [
        rows_of(heads * VDIM),
        per_micro(heads, rows, NOPE + ROPE),
        per_micro(seq_len, heads * (NOPE + VDIM)),
        per_micro(heads, rows, 1),
    ]
    return per_micro, rows_of, whole, places, weights, kept


def kv_spec(seq_len):
    return pl.BlockSpec((seq_len, KV_WIDTH), lambda m: (0, m))


def attend(x_attn, kv_all, places, weights, micro_count, heads):
    rows, seq_len = x_attn.shape[0] // micro_count, kv_all.shape[0]
    per_micro, rows_of, _, place_specs, weight_specs, kept = attention_specs(
        micro_count, rows, seq_len, heads
    )
    total = micro_count * rows
    return pl.pallas_call(
        attend_kernel,
        grid=(micro_count,),
        in_specs=[rows_of(D), kv_spec(seq_len)] + place_specs + weight_specs,
        out_specs=[rows_of(D)] + kept,
        out_shape=[
            jax.ShapeDtypeStruct((total, D), BF16),
            jax.ShapeDtypeStruct((total, heads * VDIM), BF16),
            jax.ShapeDtypeStruct((micro_count, heads, rows, NOPE + ROPE), BF16),
            jax.ShapeDtypeStruct((micro_count, seq_len, heads * (NOPE + VDIM)), BF16),
            jax.ShapeDtypeStruct((micro_count, heads, rows, 1), F32),
        ],
        compiler_params=pltpu.CompilerParams(vmem_limit_bytes=56 * MIB),
        cost_estimate=pl.CostEstimate(
            flops=9_000_000_000, bytes_accessed=60_000_000, transcendentals=0
        ),
        name="attend",
    )(x_attn, kv_all, *places, *weights)


def attend_back(grad, x_attn, kv_all, places, weights, kept, micro_count, heads):
    rows, seq_len = x_attn.shape[0] // micro_count, kv_all.shape[0]
    per_micro, rows_of, whole, place_specs, weight_specs, kept_specs = attention_specs(
        micro_count, rows, seq_len, heads
    )
    total = micro_count * rows
    return pl.pallas_call(
        attend_back_kernel,
        grid=(micro_count,),
        in_specs=[rows_of(D), kept_specs[0], rows_of(D), kv_spec(seq_len)]
        + place_specs
        + kept_specs[1:]
        + weight_specs,
        out_specs=[per_micro(seq_len, LATENT + ROPE), rows_of(D)] + weight_specs,
        out_shape=[
            jax.ShapeDtypeStruct((micro_count, seq_len, LATENT + ROPE), BF16),
            jax.ShapeDtypeStruct((total, D), BF16),
            jax.ShapeDtypeStruct(weights[0].shape, BF16),
            jax.ShapeDtypeStruct(weights[1].shape, BF16),
            jax.ShapeDtypeStruct(weights[2].shape, BF16),
        ],
        scratch_shapes=[
            pltpu.VMEM((rows, heads * (NOPE + ROPE)), BF16),
            pltpu.VMEM((seq_len, heads * (NOPE + VDIM)), BF16),
            pltpu.VMEM(weights[0].shape, F32),
            pltpu.VMEM(weights[1].shape, F32),
            pltpu.VMEM(weights[2].shape, F32),
        ],
        compiler_params=pltpu.CompilerParams(vmem_limit_bytes=60 * MIB),
        cost_estimate=pl.CostEstimate(
            flops=2_000_000_000, bytes_accessed=10_000_000, transcendentals=0
        ),
        name="attend_back",
    )(grad, kept[0], x_attn, kv_all, *places, *kept[1:], *weights)


PEER_SLOTS = 4


def expert_kernel(
    pairs,
    context_size,
    fe,
    x_ref,
    cot_ref,
    gate_in,
    up_in,
    down_in,
    router_in,
    shared_gate_in,
    shared_up_in,
    shared_down_in,
    out_ref,
    part_ref,
    gate_out,
    up_out,
    down_out,
    router_out,
    shared_out,
    shared_part,
    shared_grads,
    x_all,
    gate_ref,
    up_ref,
    down_ref,
    x_tile,
    cot_tile,
    out_tile,
    grad_tile,
    peer_tile,
    grad_gate,
    grad_up,
    hidden_low,
    gate_acc,
    up_acc,
    down_acc,
    x_send,
    x_recv,
    relay_send,
    relay_recv,
    pass_send,
    pass_recv,
    x_load,
    cot_load,
    out_store,
    swap_send,
    swap_recv,
    sum_send,
    sum_recv,
    weight_load,
    grad_store,
    shared_store,
    acc_store,
    credit,
):
    micro_count, rows = x_ref.shape[0], x_ref.shape[1]
    units = gate_ref.shape[0]
    shared_units = shared_gate_in.shape[0]
    half = units // EXP_DEV
    experts = 2 * pairs * EXP_DEV
    bits = pairs.bit_length() - 1
    steps = micro_count * pairs
    across = pairs == 4
    place = lax.axis_index("dp") * context_size + lax.axis_index("context")
    core = lax.rem(place, 2)
    chip = lax.div(place, 2)

    def device(chip_index, core_index):
        index = chip_index * 2 + core_index
        return {"dp": lax.div(index, context_size), "context": lax.rem(index, context_size)}

    sibling = device(chip, 1 - core)
    meet([sibling] + [device(flip(chip, mask, bits), core) for mask in range(1, pairs)])

    def step_of(step):
        micro = lax.div(step, pairs)
        turn = lax.rem(step, pairs)
        backward = lax.rem(micro, 2)
        return micro, lax.rem(turn + backward, pairs)

    def push_x(micro, mask):
        return pltpu.make_async_remote_copy(
            src_ref=x_ref.at[micro],
            dst_ref=x_all.at[micro, chip, core],
            send_sem=x_send.at[micro, mask],
            recv_sem=x_recv.at[micro, mask],
            device_id=device(flip(chip, mask, bits), core),
            device_id_type=MESH,
        )

    def relay(micro, mask, own=False):
        source = flip(chip, mask, bits)
        return pltpu.make_async_remote_copy(
            src_ref=x_ref.at[micro] if own else x_all.at[micro, source, core],
            dst_ref=x_all.at[micro, source, core],
            send_sem=relay_send.at[micro, mask],
            recv_sem=relay_recv.at[micro, mask],
            device_id=sibling,
            device_id_type=MESH,
        )

    def relay_arrival(micro, mask):
        source = flip(chip, mask, bits)
        return pltpu.make_async_remote_copy(
            src_ref=x_all.at[micro, source, 1 - core],
            dst_ref=x_all.at[micro, source, 1 - core],
            send_sem=relay_send.at[micro, mask],
            recv_sem=relay_recv.at[micro, mask],
            device_id=sibling,
            device_id_type=MESH,
        )

    def x_arrival(micro, mask):
        return pltpu.make_async_remote_copy(
            src_ref=x_ref.at[micro],
            dst_ref=x_all.at[micro, flip(chip, mask, bits), core],
            send_sem=x_send.at[micro, mask],
            recv_sem=x_recv.at[micro, mask],
            device_id=device(flip(chip, mask, bits), core),
            device_id_type=MESH,
        )

    middle = rows // 2
    parts = (pl.ds(0, middle), pl.ds(middle, rows - middle))

    def pass_on(micro, mask, source, part):
        return pltpu.make_async_remote_copy(
            src_ref=x_all.at[micro, source, core, parts[part]],
            dst_ref=x_all.at[micro, source, core, parts[part]],
            send_sem=pass_send.at[micro, part],
            recv_sem=pass_recv.at[micro, part],
            device_id=device(flip(chip, mask, bits), core),
            device_id_type=MESH,
        )

    def half_tile(side):
        return pl.ds(pl.multiple_of(side * rows, rows), rows)

    def load_cot(step):
        micro, mask = step_of(step)
        slot = lax.rem(step, 2)
        source = flip(chip, mask, bits)
        return [
            pltpu.make_async_copy(
                cot_ref.at[2 * source + side, micro],
                cot_tile.at[slot, half_tile(side)],
                cot_load.at[slot, side],
            )
            for side in range(2)
        ]

    def load_own(step):
        slot = lax.rem(step, 2)
        return pltpu.make_async_copy(
            x_ref.at[step_of(step)[0]], x_tile.at[slot, half_tile(core)], x_load.at[slot, 0]
        )

    def load_x(step, number):
        micro, mask = step_of(step)
        slot = lax.rem(step, 2)
        side = core if number == 0 else 1 - core
        return pltpu.make_async_copy(
            x_all.at[micro, flip(chip, mask, bits), side],
            x_tile.at[slot, half_tile(side)],
            x_load.at[slot, number],
        )

    def store(step):
        micro, mask = step_of(step)
        return [
            pltpu.make_async_copy(
                out_tile.at[pl.ds(side * rows, rows)],
                out_ref.at[2 * flip(chip, mask, bits) + side, micro],
                out_store.at[side],
            )
            for side in range(2)
        ]

    def swap(step):
        slot = lax.rem(step, 2)
        held = lax.rem(step, PEER_SLOTS)
        return pltpu.make_async_remote_copy(
            src_ref=grad_tile.at[pl.ds(pl.multiple_of((1 - core) * rows, rows), rows)],
            dst_ref=peer_tile.at[held],
            send_sem=swap_send.at[slot],
            recv_sem=swap_recv.at[held],
            device_id=sibling,
            device_id_type=MESH,
        )

    def push_sum(step):
        micro, mask = step_of(step)
        slot = lax.rem(step, PEER_SLOTS)
        return pltpu.make_async_remote_copy(
            src_ref=peer_tile.at[slot],
            dst_ref=part_ref.at[micro, mask],
            send_sem=sum_send.at[slot],
            recv_sem=sum_recv.at[micro, mask],
            device_id=device(flip(chip, mask, bits), core),
            device_id_type=MESH,
        )

    def keep_sum(step):
        micro, mask = step_of(step)
        slot = lax.rem(step, PEER_SLOTS)
        return pltpu.make_async_copy(
            peer_tile.at[slot], part_ref.at[micro, mask], sum_send.at[slot]
        )

    def wait_sum_sent(step):
        mask = step_of(step)[1]

        @pl.when(mask > 0)
        def _():
            push_sum(step).wait_send()

        @pl.when(mask == 0)
        def _():
            keep_sum(step).wait()

    def fetch(step):
        micro, mask = step_of(step)

        if not across:

            @pl.when(mask > 0)
            def _():
                x_arrival(micro, mask).wait_recv()
                relay(micro, mask).start()

        else:

            @pl.when((mask == 1) | (mask == 2))
            def _():
                x_arrival(micro, mask).wait_recv()
                relay(micro, mask).start()

            for part in range(2):

                @pl.when(mask == part + 1)
                def _():
                    pass_on(micro, 2 - part, flip(chip, part + 1, bits), part).start()

            @pl.when(mask == 3)
            def _():
                for part in range(2):
                    pass_on(micro, part + 1, flip(chip, 3, bits), part).wait_recv()
                relay(micro, mask).start()

        for copy in load_cot(step):
            copy.start()

        @pl.when(mask == 0)
        def _():
            load_own(step).start()

        @pl.when(mask > 0)
        def _():
            load_x(step, 0).start()

    def fetch_relayed(step):
        micro, mask = step_of(step)
        relay_arrival(micro, mask).wait_recv()
        load_x(step, 1).start()

    def finish_sum(step):
        slot = lax.rem(step, 2)
        held = lax.rem(step, PEER_SLOTS)
        swap(step).wait()

        def add(index, carry):
            at = pl.ds(pl.multiple_of(index * 16, 16), 16)
            mine = pl.ds(pl.multiple_of(core * rows + index * 16, 16), 16)
            value = grad_tile[mine, :].astype(F32) + peer_tile[held, at, :].astype(F32)
            peer_tile[held, at, :] = value.astype(BF16)
            return carry

        lax.fori_loop(0, rows // 16, add, 0)

        mask = step_of(step)[1]

        @pl.when(mask > 0)
        def _():
            push_sum(step).start()

        @pl.when(mask == 0)
        def _():
            keep_sum(step).start()

    direct = (1, 2) if across else tuple(range(1, pairs))
    for mask in direct:
        push_x(0, mask).start()
    for micro in range(micro_count):
        relay(micro, 0, own=True).start()

    def weights_in(pieces):
        copies = []
        for number, (source, target, start) in enumerate(pieces):
            copies.append(
                pltpu.make_async_copy(
                    source, target.at[pl.ds(start, source.shape[0])], weight_load.at[number]
                )
            )
        return copies

    shared_weights = weights_in(
        [(shared_gate_in, gate_ref, 0), (shared_up_in, up_ref, 0), (shared_down_in, down_ref, 0)]
    )
    for copy in shared_weights:
        copy.start()
    shared_rows = []
    for micro in range(micro_count):
        at = pl.ds(micro * rows, rows)
        shared_rows.append(
            pltpu.make_async_copy(x_ref.at[micro], x_tile.at[1, at], x_load.at[1, micro])
        )
        shared_rows.append(
            pltpu.make_async_copy(cot_ref.at[place, micro], cot_tile.at[1, at], cot_load.at[1, micro])
        )
    for copy in shared_rows:
        copy.start()
    for target in (gate_ref, up_ref, down_ref):
        target[shared_units:, :] = jnp.zeros((units - shared_units, D), BF16)
    fetch(0)

    chunk = 256 if units % 256 == 0 else LANES
    out_chunk = 512
    slab = half - LANES
    first_lane = fe % LANES
    slab_chunk = slab // chunk * chunk

    def hidden_pass(x, cot, here, start, gate, scale):
        at = slice(start, start + chunk)
        up = mm_nt(x, up_ref[at, :])
        back = mm_nt(cot, down_ref[at, :])
        sig = jax.nn.sigmoid(gate)
        act = gate * sig
        hidden = act * up
        grad_hidden = back if scale is None else back * scale
        scaled = hidden if scale is None else hidden * scale
        hidden_low[here, at] = scaled.astype(BF16)
        grad_gate[here, at] = (grad_hidden * up * (sig * (1.0 + gate * (1.0 - sig)))).astype(BF16)
        grad_up[here, at] = (grad_hidden * act).astype(BF16)
        return hidden * back

    def grad_pass():
        for start in range(0, D, out_chunk):
            at = slice(start, start + out_chunk)
            grad = mm(grad_gate[...], gate_ref[:, at]) + mm(grad_up[...], up_ref[:, at])
            grad_tile[:, at] = grad.astype(BF16)

    def out_pass():
        for start in range(0, D, out_chunk):
            at = slice(start, start + out_chunk)
            out_tile[:, at] = mm(hidden_low[...], down_ref[:, at]).astype(BF16)

    for copy in shared_weights + shared_rows:
        copy.wait()
    row_halves = (slice(0, rows), slice(rows, 2 * rows))
    for here in row_halves:
        x, cot = x_tile[1, here, :D], cot_tile[1, here]
        for start in range(0, units, chunk):
            gate = mm_nt(x, gate_ref[start : start + chunk, :])
            hidden_pass(x, cot, here, start, gate, None)
    grad_pass()
    out_pass()
    expert_weights = weights_in(
        [
            piece
            for number in range(EXP_DEV)
            for piece in (
                (gate_in.at[number], gate_ref, number * half),
                (up_in.at[number], up_ref, number * half),
                (down_in.at[number], down_ref, number * half),
            )
        ]
        + [(router_in, gate_ref, fe)]
    )
    for copy in expert_weights:
        copy.start()
    for target in (gate_ref, up_ref, down_ref):
        for number in range(EXP_DEV):
            first = number * half + fe
            if target is gate_ref and number == 0:
                first += experts
            last = (number + 1) * half
            if last > first:
                target[first:last, :] = jnp.zeros((last - first, D), BF16)
    shared_stores = []
    for micro in range(micro_count):
        at = pl.ds(micro * rows, rows)
        shared_stores.append(
            pltpu.make_async_copy(out_tile.at[at], shared_out.at[micro], shared_store.at[micro, 0])
        )
        shared_stores.append(
            pltpu.make_async_copy(
                grad_tile.at[at], shared_part.at[micro], shared_store.at[micro, 1]
            )
        )
    for copy in shared_stores:
        copy.start()
    fetch_relayed(0)
    for copy in shared_stores:
        copy.wait()
    staged = []
    for which, (left, right) in enumerate(
        ((grad_gate, x_tile[1, :, :D]), (grad_up, x_tile[1, :, :D]), (hidden_low, cot_tile[1]))
    ):
        for start in range(0, units, rows):
            stage = len(staged) % 2 * rows
            if len(staged) >= 2:
                staged[-2].wait()
            out_tile[stage : stage + rows, :] = mm_tn(
                left[:, start : start + rows], right
            ).astype(BF16)
            copy = pltpu.make_async_copy(
                out_tile.at[pl.ds(stage, rows)],
                shared_grads.at[which, pl.ds(start, rows)],
                grad_store.at[len(staged) % 2],
            )
            copy.start()
            staged.append(copy)
    for acc in (gate_acc, up_acc, down_acc):
        acc[...] = jnp.zeros_like(acc)
    for copy in staged[-2:] + expert_weights:
        copy.wait()

    def work(step, carry):
        slot = lax.rem(step, 2)

        for copy in load_cot(step):
            copy.wait()
        for number in range(2):
            load_x(step, number).wait()

        for here in row_halves:
            x = x_tile[slot, here, :D]
            chosen = x_tile[slot, here, D:].astype(F32)
            cot = cot_tile[slot, here]
            lane = lax.broadcasted_iota(jnp.int32, (rows, LANES), 1) - first_lane
            valid = (lane >= 0) & (lane < experts)

            first_gate = mm_nt(x, gate_ref[slab_chunk : slab_chunk + chunk, :])
            slab_gate = first_gate[:, slab - slab_chunk : slab - slab_chunk + LANES]
            logits = jnp.where(valid, slab_gate, -1e30)
            weights = jnp.where(
                valid, jnp.exp(logits - jnp.max(logits, axis=-1, keepdims=True)), 0.0
            )
            router_probs = weights / jnp.sum(weights, axis=-1, keepdims=True)
            named = router_probs * chosen
            picks = [lane == place * EXP_DEV + number for number in range(EXP_DEV)]
            scales = [
                jnp.sum(jnp.where(pick, named, 0.0), axis=-1, keepdims=True) for pick in picks
            ]
            flags = [
                jnp.sum(jnp.where(pick, chosen, 0.0), axis=-1, keepdims=True) for pick in picks
            ]
            dots = [jnp.zeros((rows, 1), F32) for _ in picks]
            column = lax.broadcasted_iota(jnp.int32, (rows, chunk), 1)
            starts = [slab_chunk] + [at for at in range(0, units, chunk) if at != slab_chunk]
            for start in starts:
                if start == slab_chunk:
                    gate = first_gate
                else:
                    gate = mm_nt(x, gate_ref[start : start + chunk, :])
                first, last = start // half, (start + chunk - 1) // half
                scale = scales[first]
                if last > first:
                    scale = jnp.where(column < last * half - start, scales[first], scales[last])
                product = hidden_pass(x, cot, here, start, gate, scale)
                if last > first:
                    split = last * half - start
                    dots[first] = dots[first] + jnp.sum(product[:, :split], axis=-1, keepdims=True)
                    dots[last] = dots[last] + jnp.sum(product[:, split:], axis=-1, keepdims=True)
                else:
                    dots[first] = dots[first] + jnp.sum(product, axis=-1, keepdims=True)
            spread = jnp.zeros((rows, LANES), F32)
            for pick, dot, flag in zip(picks, dots, flags):
                spread = spread + jnp.where(pick, dot * flag, 0.0)
            grad_logits = router_probs * (
                spread - jnp.sum(router_probs * spread, axis=-1, keepdims=True)
            )
            grad_gate[here, slab:half] = jnp.where(
                lane < 0, grad_gate[here, slab:half].astype(F32), grad_logits
            ).astype(BF16)

        @pl.when(step + 1 < steps)
        def _():
            fetch(step + 1)

        @pl.when(step == 0)
        def _():
            for micro in range(1, micro_count):
                for mask in direct:
                    push_x(micro, mask).start()

        @pl.when(step >= 1)
        def _():
            finish_sum(step - 1)

        @pl.when(step >= PEER_SLOTS)
        def _():
            wait_sum_sent(step - PEER_SLOTS)
            pl.semaphore_signal(credit, inc=1, device_id=sibling, device_id_type=MESH)
            pl.semaphore_wait(credit, 1)

        grad_pass()
        swap(step).start()


        @pl.when(step >= 1)
        def _():
            for copy in store(step - 1):
                copy.wait()

        out_pass()
        for copy in store(step):
            copy.start()

        @pl.when(step + 1 < steps)
        def _():
            fetch_relayed(step + 1)

        for acc, left, right in (
            (gate_acc, grad_gate, x_tile),
            (up_acc, grad_up, x_tile),
            (down_acc, hidden_low, cot_tile),
        ):
            for start in range(0, D, out_chunk):
                at = slice(start, start + out_chunk)
                acc[:, at] += mm_tn(left[...], right[slot, :, at])
        return carry


    lax.fori_loop(0, steps, work, 0)
    finals = [
        pltpu.make_async_copy(
            gate_acc.at[pl.ds(fe, experts)], router_out, acc_store.at[EXP_DEV, 0]
        )
    ]
    for number in range(EXP_DEV):
        for which, (acc, target) in enumerate(
            ((gate_acc, gate_out), (up_acc, up_out), (down_acc, down_out))
        ):
            finals.append(
                pltpu.make_async_copy(
                    acc.at[pl.ds(number * half, fe)],
                    target.at[number],
                    acc_store.at[number, which],
                )
            )
    for copy in finals:
        copy.start()
    finish_sum(steps - 1)
    for back in range(PEER_SLOTS, 0, -1):
        wait_sum_sent(steps - back)
    for copy in finals:
        copy.wait()
    for copy in store(steps - 1):
        copy.wait()
    for micro in range(micro_count):
        if across:
            for part in range(2):
                pass_on(micro, 2 - part, flip(chip, part + 1, bits), part).wait_send()
        for mask in range(pairs):
            relay(micro, mask).wait_send()
            if mask in direct:
                push_x(micro, mask).wait_send()
            if mask:
                pltpu.make_async_remote_copy(
                    src_ref=peer_tile.at[0],
                    dst_ref=part_ref.at[micro, mask],
                    send_sem=sum_send.at[0],
                    recv_sem=sum_recv.at[micro, mask],
                    device_id=device(flip(chip, mask, bits), core),
                    device_id_type=MESH,
                ).wait_recv()


def expert_pass(
    x_ext, cot_all, gate_w, up_w, down_w, router_w, shared_gate, shared_up, shared_down, collective_id
):
    micro_count, rows, width = x_ext.shape
    context_size = lax.axis_size("context")
    pairs = lax.axis_size("dp") * context_size // 2
    fe, experts, shared_units = gate_w.shape[1], router_w.shape[0], shared_gate.shape[0]
    half = -(-(fe + experts) // LANES) * LANES
    units = EXP_DEV * half
    dma = pltpu.SemaphoreType.DMA
    wide = jax.ShapeDtypeStruct((EXP_DEV, fe, D), F32)
    own = jax.ShapeDtypeStruct((micro_count, rows, D), BF16)
    return pl.pallas_call(
        functools.partial(expert_kernel, pairs, context_size, fe),
        out_shape=(
            jax.ShapeDtypeStruct((2 * pairs, micro_count, rows, D), BF16),
            jax.ShapeDtypeStruct((micro_count, pairs, rows, D), BF16),
            wide,
            wide,
            wide,
            jax.ShapeDtypeStruct((experts, D), F32),
            own,
            own,
            jax.ShapeDtypeStruct((3, units, D), BF16),
            jax.ShapeDtypeStruct((micro_count, pairs, 2, rows, width), BF16),
        ),
        in_specs=[pl.BlockSpec(memory_space=pl.ANY)] * 9,
        out_specs=(pl.BlockSpec(memory_space=pl.ANY),) * 10,
        scratch_shapes=[
            pltpu.VMEM((units, D), BF16),
            pltpu.VMEM((units, D), BF16),
            pltpu.VMEM((units, D), BF16),
            pltpu.VMEM((2, 2 * rows, width), BF16),
            pltpu.VMEM((2, 2 * rows, D), BF16),
            pltpu.VMEM((2 * rows, D), BF16),
            pltpu.VMEM((2 * rows, D), BF16),
            pltpu.VMEM((PEER_SLOTS, rows, D), BF16),
            pltpu.VMEM((2 * rows, units), BF16),
            pltpu.VMEM((2 * rows, units), BF16),
            pltpu.VMEM((2 * rows, units), BF16),
            pltpu.VMEM((units, D), F32),
            pltpu.VMEM((units, D), F32),
            pltpu.VMEM((units, D), F32),
            dma((micro_count, pairs)),
            dma((micro_count, pairs)),
            dma((micro_count, pairs)),
            dma((micro_count, pairs)),
            dma((micro_count, 2)),
            dma((micro_count, 2)),
            dma((2, 2)),
            dma((2, 2)),
            dma((2,)),
            dma((2,)),
            dma((PEER_SLOTS,)),
            dma((PEER_SLOTS,)),
            dma((micro_count, pairs)),
            dma((3 * EXP_DEV + 1,)),
            dma((2,)),
            dma((micro_count, 2)),
            dma((EXP_DEV + 1, 3)),
            pltpu.SemaphoreType.REGULAR,
        ],
        compiler_params=pltpu.CompilerParams(
            collective_id=collective_id, has_side_effects=True, vmem_limit_bytes=62 * MIB
        ),
        cost_estimate=pl.CostEstimate(
            flops=36 * (pairs * micro_count + 1) * rows * D * units,
            bytes_accessed=500_000_000,
            transcendentals=0,
        ),
        name="expert_pass",
    )(x_ext, cot_all, gate_w, up_w, down_w, router_w, shared_gate, shared_up, shared_down)[:9]


def per_device(
    tokens,
    segments,
    expert_ids,
    norm_attn,
    w_query,
    w_kv_down,
    norm_latent,
    w_kv_up,
    w_out,
    norm_ffn,
    w_router,
    w_shared_gate,
    w_shared_up,
    w_shared_down,
    w_expert_gate,
    w_expert_up,
    w_expert_down,
    cotangent,
):
    micro_count, block_rows = tokens.shape[:2]
    rows = micro_count * block_rows
    seq_len = segments.shape[1]
    context_size = lax.axis_size("context")
    groups = lax.axis_size("dp") * context_size
    tensor_size = lax.axis_size("tensor")
    group_index = lax.axis_index("dp") * context_size + lax.axis_index("context")
    own_rows = block_rows // tensor_size
    own_start = lax.axis_index("tensor") * own_rows
    experts = EXP_DEV * groups
    heads_local = w_query.shape[1] // (NOPE + ROPE)
    fe_local = w_expert_gate.shape[2]
    start_row = lax.axis_index("context") * block_rows
    query_index = start_row + jnp.arange(block_rows)
    key_index = jnp.arange(seq_len)
    cos_block, sin_block = angles(query_index.astype(F32), ROPE)
    cos_query = jnp.tile(cos_block, (micro_count, 1))
    sin_query = jnp.tile(sin_block, (micro_count, 1))
    gain_attn = norm_attn.astype(F32)
    gain_latent = norm_latent.astype(F32)
    gain_ffn = norm_ffn.astype(F32)

    def own(values):
        values = values.reshape((micro_count, block_rows) + values.shape[1:])
        part = lax.dynamic_slice_in_dim(values, own_start, own_rows, axis=1)
        return part.reshape((micro_count * own_rows,) + values.shape[2:])

    def to_owner(values):
        values = values.astype(BF16).reshape(micro_count, tensor_size, own_rows, values.shape[-1])
        return LineScatter(values, "tensor")

    def from_owners(values):
        return LineGather(values.reshape(micro_count, own_rows, values.shape[-1]), "tensor")

    def flat(values):
        return values.reshape(-1, values.shape[-1])

    ff_local = w_shared_gate.shape[1]
    slots = jnp.arange(LANES) - fe_local % LANES
    named = jnp.any(expert_ids[..., None] == slots, axis=2).astype(BF16)

    x_rows = tokens.reshape(rows, D).astype(F32)
    cot_rows = cotangent.reshape(rows, D)
    inv_attn = rms_scale(x_rows)
    normed_attn = x_rows * inv_attn
    x_attn = (normed_attn * gain_attn).astype(BF16)
    kv_raw = mm(x_attn, w_kv_down)
    latent_raw = kv_raw[:, :LATENT]
    inv_latent = rms_scale(latent_raw)
    normed_latent = latent_raw * inv_latent
    latent = (normed_latent * gain_latent).astype(BF16)
    key_rope = rotate(kv_raw[:, LATENT:], cos_query, sin_query).astype(BF16)
    blank = jnp.zeros((rows, KV_WIDTH - LATENT - ROPE), BF16)
    kv_own = jnp.concatenate([latent, key_rope, blank], axis=1)
    kv_own = kv_own.reshape(micro_count, block_rows, KV_WIDTH).transpose(1, 0, 2)
    kv_own = kv_own.reshape(block_rows, micro_count * KV_WIDTH)
    (kv_all,) = exchange([GroupGather(kv_own, ("context",))], 1, 20)
    kv_all, cot_late = lax.optimization_barrier((kv_all, cotangent))
    cot_all = lax.all_gather(cot_late, GROUP, axis=0)
    kv_all = kv_all.reshape(seq_len, micro_count * KV_WIDTH)
    seg_query = lax.dynamic_slice_in_dim(segments, start_row, block_rows, axis=1)
    places = (
        seg_query[:, :, None],
        segments[:, None, :],
        query_index[:, None],
        key_index[None, :],
        jnp.tile(cos_block, (1, 2)),
        jnp.concatenate([-sin_block, sin_block], axis=1),
    )
    weights = (w_query, w_kv_up, w_out)
    attn_part, *kept = attend(x_attn, kv_all, places, weights, micro_count, heads_local)
    own_shape = (micro_count, own_rows, D)
    tokens_own = own(tokens.reshape(rows, D)).reshape(own_shape)

    def finish_attention(sums, extras, shares, results):
        for m in range(micro_count):
            hidden = extras[0][m].astype(F32) + sums[0][m]
            results[0][m] = hidden
            shares[0][m] = (hidden * rms_scale(hidden) * extras[1][...]).astype(BF16)

    x_ffn, hidden_one = exchange(
        [
            SumThenShare(
                [to_owner(attn_part)],
                [tokens_own, gain_ffn[None]],
                finish_attention,
                [jax.ShapeDtypeStruct(own_shape, BF16)],
                [jax.ShapeDtypeStruct(own_shape, F32)],
            )
        ],
        2,
        80,
    )
    x_ffn = x_ffn.reshape(rows, D)
    x_ext = jnp.concatenate([x_ffn.reshape(micro_count, block_rows, D), named], axis=-1)

    (
        out_part,
        grad_part,
        gate_grad,
        up_grad,
        down_grad,
        router_grad,
        shared_out,
        shared_part,
        shared_grads,
    ) = expert_pass(
        x_ext,
        cot_all,
        w_expert_gate.transpose(0, 2, 1),
        w_expert_up.transpose(0, 2, 1),
        w_expert_down,
        w_router.T,
        w_shared_gate.T,
        w_shared_up.T,
        w_shared_down,
        4,
    )
    grad_sum = jnp.sum(grad_part.astype(F32), axis=1) + shared_part.astype(F32)
    grad_sum = grad_sum.reshape(rows, D)
    shared_units = shared_grads.shape[1]
    shared_grads = shared_grads.reshape(groups, -1, D)
    shared_grads = lax.psum_scatter(shared_grads, GROUP, scatter_dimension=0, tiled=False)
    cot_own = own(cot_rows).reshape(own_shape)

    def finish_experts(sums, extras, shares, results):
        hidden, cot, gain = extras
        gain_grad = jnp.zeros((1, D), F32)
        for m in range(micro_count):
            inverse = rms_scale(hidden[m])
            normed = hidden[m] * inverse
            grad = sums[0][m]
            gain_grad = gain_grad + jnp.sum(grad * normed, axis=0, keepdims=True)
            total = cot[m].astype(F32) + norm_back(grad * gain[...], normed, inverse)
            results[0][m] = total
            shares[0][m] = total.astype(BF16)
        results[1][...] = gain_grad

    out_sum = lax.psum_scatter(out_part, GROUP, scatter_dimension=0, tiled=False)
    grad_attn_low, grad_one, norm_ffn_grad = exchange(
        [
            SumThenShare(
                [to_owner(grad_sum)],
                [hidden_one, cot_own, gain_ffn[None]],
                finish_experts,
                [jax.ShapeDtypeStruct(own_shape, BF16)],
                [
                    jax.ShapeDtypeStruct(own_shape, F32),
                    jax.ShapeDtypeStruct((1, D), F32),
                ],
            ),
        ],
        5,
        90,
    )
    grad_attn_low = grad_attn_low.reshape(rows, D)
    grad_kv_part, grad_x_heads, query_grad, kv_up_grad, out_grad = attend_back(
        grad_attn_low, x_attn, kv_all, places, weights, kept, micro_count, heads_local
    )
    grad_x_heads, shared_grads = lax.optimization_barrier((grad_x_heads, shared_grads))
    shared_grads = lax.all_gather(shared_grads, GROUP, axis=0, tiled=True)
    router_part = router_grad.T.astype(BF16).reshape(1, tensor_size, -1, LANES)
    latent_own = own(latent_raw).reshape(micro_count, own_rows, LATENT)
    turns_own = [
        own(angle).reshape(micro_count, own_rows, ROPE)
        for angle in (
            jnp.tile(cos_query, (1, 2)),
            jnp.concatenate([sin_query, -sin_query], axis=1),
        )
    ]

    def finish_rows(sums, extras, shares, results):
        x_grad, kv_grad, router = sums
        x_own, one, ffn_gain_grad, raw, cosine, sine, gain, latent_gain, down_w = extras
        gain_grad = jnp.zeros((1, D), F32)
        latent_gain_grad = jnp.zeros((1, LATENT), F32)
        for m in range(micro_count):
            inverse = rms_scale(raw[m])
            normed = raw[m] * inverse
            grad = kv_grad[m, :, :LATENT]
            latent_gain_grad = latent_gain_grad + jnp.sum(grad * normed, axis=0, keepdims=True)
            kv_low = jnp.concatenate(
                [
                    norm_back(grad * latent_gain[...], normed, inverse),
                    turn(kv_grad[m, :, LATENT:], cosine[m], sine[m]),
                ],
                axis=1,
            ).astype(BF16)
            x = x_own[m].astype(F32)
            inverse = rms_scale(x)
            normed = x * inverse
            grad = x_grad[m] + mm(kv_low, down_w[...])
            gain_grad = gain_grad + jnp.sum(grad * normed, axis=0, keepdims=True)
            total = one[m] + norm_back(grad * gain[...], normed, inverse)
            shares[0][m, :, :D] = total.astype(BF16)
            shares[0][m, :, D:] = kv_low
        shares[1][0] = router[0].astype(BF16)
        shares[2][0, :, :D] = gain_grad
        shares[2][0, :, D : 2 * D] = ffn_gain_grad[...]
        shares[2][0, :, 2 * D :] = latent_gain_grad

    finished, router_all, small = exchange(
        [
            SumThenShare(
                [
                    to_owner(grad_x_heads),
                    ContextThenLine(
                        [
                            grad_kv_part[m].reshape(context_size, block_rows, LATENT + ROPE)
                            for m in range(micro_count)
                        ],
                        ("context",),
                        "tensor",
                    ),
                    LineScatter(router_part, "tensor"),
                ],
                [
                    tokens_own,
                    grad_one,
                    norm_ffn_grad,
                    latent_own,
                    *turns_own,
                    gain_attn[None],
                    gain_latent[None],
                    w_kv_down.T,
                ],
                finish_rows,
                [
                    jax.ShapeDtypeStruct((micro_count, own_rows, D + LATENT + ROPE), BF16),
                    jax.ShapeDtypeStruct((1,) + router_part.shape[2:], BF16),
                    jax.ShapeDtypeStruct((1, 1, 2 * D + LATENT), F32),
                ],
                [],
            ),
        ],
        8,
        100,
    )
    finished = finished.reshape(rows, -1)
    finished, out_sum = lax.optimization_barrier((finished, out_sum))
    out_sum = out_sum.astype(F32) + shared_out.astype(F32)
    out_sum = out_sum.astype(BF16).reshape(micro_count, tensor_size, own_rows, D)
    out_sum = out_sum.transpose(1, 0, 2, 3)
    out_sum = lax.psum_scatter(out_sum, "tensor", scatter_dimension=0, tiled=False)
    grad_tokens, grad_kv_raw = finished[:, :D], finished[:, D:]
    kv_width = -(-grad_kv_raw.shape[1] // (16 * groups)) * 16 * groups
    grad_kv_raw = jnp.pad(grad_kv_raw, ((0, 0), (0, kv_width - grad_kv_raw.shape[1])))
    kv_down_grad = mm_tn(grad_kv_raw, x_attn).astype(BF16)
    small = jnp.sum(small, axis=(0, 1, 2)).astype(BF16)
    query_grad, kv_up_grad, out_grad, kv_down_grad, router_grad, small = exchange(
        [
            GroupSum(part.reshape(groups, -1, part.shape[-1]), GROUP)
            for part in (
                query_grad,
                kv_up_grad,
                out_grad,
                kv_down_grad,
                router_all.reshape(groups * 16, -1),
                small.reshape(groups * 16, -1),
            )
        ],
        10,
        80,
    )
    query_grad, kv_up_grad, out_grad, kv_down_grad, out_sum, shared_grads = lax.optimization_barrier(
        (query_grad, kv_up_grad, out_grad, kv_down_grad, out_sum, shared_grads)
    )
    output = (hidden_one + out_sum.astype(F32)).astype(BF16)
    output = lax.all_gather(output, "tensor", axis=0)
    output = output.transpose(1, 0, 2, 3)
    kv_down_grad = kv_down_grad.reshape(-1, D)[: LATENT + ROPE].astype(F32).T
    router_grad = router_grad.reshape(D, experts).astype(F32)
    small = small.reshape(-1).astype(F32)
    return (
        output.reshape(tokens.shape),
        grad_tokens.reshape(tokens.shape),
        small[:D],
        flat(query_grad).reshape(D, -1).astype(F32),
        kv_down_grad,
        small[D + D :],
        kv_up_grad.reshape(LATENT, -1).astype(F32),
        out_grad.reshape(-1, D).astype(F32),
        small[D : D + D],
        router_grad,
        shared_grads[:ff_local].astype(F32).T,
        shared_grads[shared_units : shared_units + ff_local].astype(F32).T,
        shared_grads[2 * shared_units : 2 * shared_units + ff_local].astype(F32),
        gate_grad.transpose(0, 2, 1),
        up_grad.transpose(0, 2, 1),
        down_grad,
    )


def solution(mesh):
    return jax.shard_map(
        per_device,
        mesh=mesh,
        in_specs=(
            P("dp", "context", None),
            P("dp", None),
            P("dp", "context", None),
            P(),
            P(None, "tensor"),
            P(),
            P(),
            P(None, "tensor"),
            P("tensor", None),
            P(),
            P(),
            P(None, "tensor"),
            P(None, "tensor"),
            P("tensor", None),
            P(("dp", "context"), None, "tensor"),
            P(("dp", "context"), None, "tensor"),
            P(("dp", "context"), "tensor", None),
            P("dp", "context", None),
        ),
        out_specs=(
            P("dp", "context", None),
            P("dp", "context", None),
            P(),
            P(None, "tensor"),
            P(),
            P(),
            P(None, "tensor"),
            P("tensor", None),
            P(),
            P(),
            P(None, "tensor"),
            P(None, "tensor"),
            P("tensor", None),
            P(("dp", "context"), None, "tensor"),
            P(("dp", "context"), None, "tensor"),
            P(("dp", "context"), "tensor", None),
        ),
        check_vma=False,
    )
```

```python
import functools

import jax
import jax.numpy as jnp
from jax import lax
from jax.experimental import pallas as pl
from jax.experimental.pallas import tpu as pltpu
from jax.sharding import PartitionSpec as P

D = 2048
NOPE = 128
ROPE = 64
VDIM = 128
LATENT = 512
TOP = 6
EXP_DEV = 2
LANES = 128
GROUP = ("dp", "context")
EVERY = ("dp", "context", "tensor")
BF16 = jnp.bfloat16
F32 = jnp.float32
MESH = pl.DeviceIdType.MESH
MIB = 1024 * 1024

EPS = 1e-06


def rms_scale(rows):
    return lax.rsqrt(jnp.mean(rows * rows, axis=-1, keepdims=True) + EPS)


def norm_back(grad_out, normed, inverse):
    return inverse * (grad_out - normed * jnp.mean(grad_out * normed, axis=-1, keepdims=True))


def angles(positions, rope_dim):
    frequency = 10000.0 ** (-(jnp.arange(rope_dim // 2).astype(jnp.float32) * 2.0) / rope_dim)
    turned = positions[:, None] * frequency[None, :]
    return (jnp.cos(turned), jnp.sin(turned))


def rotate(vectors, cosine, sine):
    half_dim = vectors.shape[-1] // 2
    front_part = vectors[..., :half_dim]
    back_part = vectors[..., half_dim:]
    return jnp.concatenate(
        [front_part * cosine - back_part * sine, front_part * sine + back_part * cosine], axis=-1
    )


def unrotate(vectors, cosine, sine):
    half_dim = vectors.shape[-1] // 2
    front_part = vectors[..., :half_dim]
    back_part = vectors[..., half_dim:]
    return jnp.concatenate(
        [front_part * cosine + back_part * sine, back_part * cosine - front_part * sine], axis=-1
    )


def mm(left, right):
    return jnp.dot(left, right, preferred_element_type=F32)


def mm_nt(left, right):
    return lax.dot_general(left, right, (((1,), (1,)), ((), ())), preferred_element_type=F32)


def mm_tn(left, right):
    return lax.dot_general(left, right, (((0,), (0,)), ((), ())), preferred_element_type=F32)


def ring(axes, sizes):
    place = 0
    total = 1
    for axis, size in zip(axes, sizes):
        place = place * size + lax.axis_index(axis)
        total *= size

    def coordinates(index):
        found = {}
        for axis, size in reversed(list(zip(axes, sizes))):
            found[axis] = lax.rem(index, size)
            index = lax.div(index, size)
        return found

    return place, total, coordinates


def meet(devices):
    barrier = pltpu.get_barrier_semaphore()
    for device in devices:
        pl.semaphore_signal(barrier, inc=1, device_id=device, device_id_type=MESH)
    pl.semaphore_wait(barrier, len(devices))


def flip(index, mask, bits):
    total = 0
    for bit in range(bits):
        weight = 1 << bit
        ours = lax.rem(lax.div(index, weight), 2)
        theirs = lax.rem(lax.div(mask, weight), 2)
        total = total + lax.rem(ours + theirs, 2) * weight
    return total


def group_layout(axes, sizes):
    place, _, coordinates = ring(axes, sizes)
    return lax.div(place, 2), lax.rem(place, 2), lambda chip, core: coordinates(chip * 2 + core)


def group_sizes(axes):
    sizes = tuple(lax.axis_size(axis) for axis in axes)
    pairs = 1
    for size in sizes:
        pairs *= size
    return sizes, pairs // 2


def add_rows(out, terms, rows):
    def add(index, carry):
        at = pl.ds(pl.multiple_of(index * 16, 16), 16)
        value = terms[0](at).astype(F32)
        for term in terms[1:]:
            value = value + term(at).astype(F32)
        out(at, value)
        return carry

    lax.fori_loop(0, rows // 16, add, 0)


class LineGather:
    def __init__(self, v, axis):
        self.axis, self.size = axis, lax.axis_size(axis)
        dma = pltpu.SemaphoreType.DMA
        self.inputs = [(v, pltpu.VMEM)]
        shape = (v.shape[0], self.size) + v.shape[1:]
        self.outputs = [(jax.ShapeDtypeStruct(shape, v.dtype), pl.ANY)]
        self.scratch = [dma((2, self.size)), dma((2, self.size)), dma]

    def greets(self):
        index = lax.axis_index(self.axis)
        return [
            {self.axis: lax.rem(index + step, self.size)} for step in (1, self.size - 1)
        ]

    def run(self, v_ref, out_ref, send_sem, recv_sem, own_sem):
        index, size = lax.axis_index(self.axis), self.size

        def copy(way, hop, first):
            step = 1 - 2 * way
            source = lax.rem(index - step * (hop - 1) + size, size)
            return pltpu.make_async_remote_copy(
                src_ref=v_ref if first else out_ref.at[:, source],
                dst_ref=out_ref.at[:, source],
                send_sem=send_sem.at[way, hop],
                recv_sem=recv_sem.at[way, hop],
                device_id={self.axis: lax.rem(index + step + size, size)},
                device_id_type=MESH,
            )

        def arrival(way, hop):
            step = 1 - 2 * way
            source = lax.rem(index - step * hop + size, size)
            return pltpu.make_async_remote_copy(
                src_ref=v_ref,
                dst_ref=out_ref.at[:, source],
                send_sem=send_sem.at[way, hop],
                recv_sem=recv_sem.at[way, hop],
                device_id={self.axis: lax.rem(index + step + size, size)},
                device_id_type=MESH,
            )

        def sends(way, hop):
            if way == 0:
                return (index + 1 < size) & (index - hop + 1 >= 0)
            return (index - 1 >= 0) & (index + hop - 1 < size)

        def receives(way, hop):
            return index - hop >= 0 if way == 0 else index + hop < size

        for way in range(2):

            @pl.when(sends(way, 1))
            def _():
                copy(way, 1, True).start()

        own = pltpu.make_async_copy(v_ref, out_ref.at[:, index], own_sem)
        own.start()
        yield
        for hop in range(1, size):
            for way in range(2):

                @pl.when(receives(way, hop))
                def _():
                    arrival(way, hop).wait_recv()

                if hop + 1 < size:

                    @pl.when(sends(way, hop + 1))
                    def _():
                        copy(way, hop + 1, False).start()

            yield
        own.wait()
        for hop in range(1, size):
            for way in range(2):

                @pl.when(sends(way, hop))
                def _():
                    copy(way, hop, hop == 1).wait_send()


class LineScatter:
    def __init__(self, v, axis):
        self.axis, self.size = axis, lax.axis_size(axis)
        lead, total, rows, width = v.shape
        self.lead, self.rows = lead, rows
        if not isinstance(v, jax.ShapeDtypeStruct):
            v = v.reshape(lead, total * rows, width)
        dma = pltpu.SemaphoreType.DMA
        self.inputs = [(v, pltpu.VMEM)]
        self.outputs = [(jax.ShapeDtypeStruct((lead, rows, width), F32), pltpu.VMEM)]
        self.scratch = [
            pltpu.VMEM((2, total, lead, rows, width), v.dtype),
            dma((2, total)),
            dma((2, total)),
        ]

    greets = LineGather.greets

    def run(self, v_ref, out_ref, held, send_sem, recv_sem):
        index, size, rows = lax.axis_index(self.axis), self.size, self.rows

        def block(target):
            return pl.ds(pl.multiple_of(target * rows, rows), rows)

        def ours(lead, target):
            return lambda at: v_ref[
                lead, pl.ds(pl.multiple_of(target * rows + at.start, 16), 16), :
            ]

        def copy(way, target, first):
            step = 1 - 2 * way
            return pltpu.make_async_remote_copy(
                src_ref=v_ref.at[:, block(target)] if first else held.at[way, target],
                dst_ref=held.at[way, target],
                send_sem=send_sem.at[way, target],
                recv_sem=recv_sem.at[way, target],
                device_id={self.axis: lax.rem(index + step + size, size)},
                device_id_type=MESH,
            )

        def start(way):
            return index == 0 if way == 0 else index == size - 1

        def between(way, target):
            return (index > 0) & (index < target) if way == 0 else (index < size - 1) & (index > target)

        def targets(way):
            return range(size - 1, 0, -1) if way == 0 else range(size - 1)

        for way in range(2):

            @pl.when(start(way))
            def _():
                copy(way, targets(way)[0], True).start()

        yield
        def hand_on(way, position):
            target = targets(way)[position]
            if position + 1 < size - 1:

                @pl.when(start(way))
                def _():
                    copy(way, target, True).wait_send()
                    copy(way, targets(way)[position + 1], True).start()

            @pl.when(between(way, target))
            def _():
                copy(way, target, False).wait_recv()
                for lead in range(self.lead):

                    def store(at, value):
                        held[way, target, lead, at, :] = value.astype(BF16)

                    add_rows(
                        store,
                        [
                            lambda at: held[way, target, lead, at, :],
                            ours(lead, target),
                        ],
                        self.rows,
                    )
                copy(way, target, False).start()

        for position in range(size - 1):
            @pl.when(index < size // 2)
            def _():
                hand_on(0, position)
                hand_on(1, position)

            @pl.when(index >= size // 2)
            def _():
                hand_on(1, position)
                hand_on(0, position)

            yield
        for way in range(2):

            @pl.when(jnp.logical_not(start(way)))
            def _():
                copy(way, index, False).wait_recv()

        for lead in range(self.lead):

            def store(at, value, lead=lead):
                out_ref[lead, at, :] = value

            own = [ours(lead, index)]
            right = [lambda at, lead=lead: held[0, index, lead, at, :]]
            left = [lambda at, lead=lead: held[1, index, lead, at, :]]

            @pl.when(index == 0)
            def _():
                add_rows(store, own + left, self.rows)

            @pl.when(index == size - 1)
            def _():
                add_rows(store, own + right, self.rows)

            @pl.when((index > 0) & (index < size - 1))
            def _():
                add_rows(store, own + right + left, self.rows)

        for way in range(2):

            @pl.when(start(way))
            def _():
                copy(way, targets(way)[size - 2], True).wait_send()

            for target in targets(way):

                @pl.when(between(way, target))
                def _():
                    copy(way, target, False).wait_send()


class LineScatterSum(LineScatter):
    def __init__(self, parts, one, axis):
        lead, self.count, all_rows, width = parts.shape
        total = lax.axis_size(axis)
        self.all_rows = all_rows
        super().__init__(
            jax.ShapeDtypeStruct((lead, total, all_rows // total, width), BF16), axis
        )
        self.inputs = [(parts, pltpu.VMEM), (one, pltpu.VMEM)]
        self.scratch = [pltpu.VMEM((lead, all_rows, width), BF16)] + self.scratch

    def run(self, parts_ref, one_ref, out_ref, summed, *refs):
        for lead in range(self.lead):

            def store(at, value, lead=lead):
                summed[lead, at, :] = value.astype(BF16)

            terms = [lambda at, lead=lead: one_ref[lead, at, :]]
            for number in range(self.count):
                terms.append(lambda at, lead=lead, number=number: parts_ref[lead, number, at, :])
            add_rows(store, terms, self.all_rows)
        yield from super().run(summed, out_ref, *refs)


class GroupScatter:
    def __init__(self, v, axes, pick=None):
        self.axes, self.pick = axes, pick
        self.sizes, self.pairs = group_sizes(axes)
        tail = v.shape[1:] if pick is None else v.shape[2:]
        self.across = self.pairs == 4 and tail[0] % 32 == 0
        v = v.reshape((self.pairs, 2) + v.shape[1:])
        self.rows = tail[0]
        dma = pltpu.SemaphoreType.DMA
        self.inputs = [(v, pl.ANY)]
        self.outputs = [(jax.ShapeDtypeStruct(tail, BF16), pltpu.VMEM)]
        self.scratch = [pltpu.VMEM((self.pairs,) + tail, BF16)] * 4 + [
            pltpu.VMEM((2, tail[0] // 2 if self.across else 16) + tail[1:], BF16),
            dma,
            dma,
            dma,
            dma((self.pairs,)),
            dma((self.pairs,)),
            dma((2,)),
            dma((2,)),
        ]

    def greets(self):
        chip, core, device = group_layout(self.axes, self.sizes)
        bits = self.pairs.bit_length() - 1
        return [device(chip, 1 - core)] + [
            device(flip(chip, mask, bits), core) for mask in range(1, self.pairs)
        ]

    def run(
        self,
        v_ref,
        out_ref,
        mine,
        peer,
        summed,
        held,
        passed,
        load_sem,
        swap_send,
        swap_recv,
        sum_send,
        sum_recv,
        pass_send,
        pass_recv,
    ):
        pairs, rows = self.pairs, self.rows
        bits = pairs.bit_length() - 1
        chip, core, device = group_layout(self.axes, self.sizes)

        def side(which):
            if self.pick is None:
                return v_ref.at[:, which]
            return v_ref.at[:, which, self.pick]

        swap = pltpu.make_async_remote_copy(
            src_ref=side(1 - core),
            dst_ref=peer,
            send_sem=swap_send,
            recv_sem=swap_recv,
            device_id=device(chip, 1 - core),
            device_id_type=MESH,
        )
        swap.start()
        load = pltpu.make_async_copy(side(core), mine, load_sem)
        load.start()
        yield

        def push(mask):
            return pltpu.make_async_remote_copy(
                src_ref=summed.at[mask],
                dst_ref=held.at[mask],
                send_sem=sum_send.at[mask],
                recv_sem=sum_recv.at[mask],
                device_id=device(flip(chip, mask, bits), core),
                device_id_type=MESH,
            )

        middle = rows // 2
        halves = (pl.ds(0, middle), pl.ds(middle, rows - middle))

        def pass_on(part):
            return pltpu.make_async_remote_copy(
                src_ref=summed.at[3, halves[part]],
                dst_ref=passed.at[part],
                send_sem=pass_send.at[part],
                recv_sem=pass_recv.at[part],
                device_id=device(flip(chip, part + 1, bits), core),
                device_id_type=MESH,
            )

        load.wait()
        swap.wait()
        for mask in range(pairs - 1, -1, -1):
            target = flip(chip, mask, bits)

            def store(at, value, mask=mask):
                summed[mask, at, :] = value.astype(BF16)

            add_rows(
                store,
                [
                    lambda at, target=target: mine[target, at, :],
                    lambda at, target=target: peer[target, at, :],
                ],
                rows,
            )
            if self.across and mask == 3:
                for part in range(2):
                    pass_on(part).start()
            if not self.across and mask:
                push(mask).start()
        yield
        direct = (1, 2) if self.across else range(1, pairs)
        if self.across:
            for part in range(2):
                pass_on(part).wait_recv()
                mask = 2 - part
                start = part * middle

                def store(at, value, mask=mask, start=start):
                    summed[mask, pl.ds(pl.multiple_of(start + at.start, 16), 16), :] = value.astype(
                        BF16
                    )

                add_rows(
                    store,
                    [
                        lambda at, mask=mask, start=start: summed[
                            mask, pl.ds(pl.multiple_of(start + at.start, 16), 16), :
                        ],
                        lambda at, part=part: passed[part, at, :],
                    ],
                    middle,
                )
                push(mask).start()
        yield
        for mask in direct:
            push(mask).wait_recv()

        def finish(at, value):
            out_ref[at, :] = value.astype(BF16)

        add_rows(
            finish,
            [lambda at: summed[0, at, :]]
            + [lambda at, mask=mask: held[mask, at, :] for mask in direct],
            rows,
        )
        yield
        for mask in direct:
            push(mask).wait_send()
        if self.across:
            for part in range(2):
                pass_on(part).wait_send()


class GroupGather:
    def __init__(self, v, axes):
        self.axes = axes
        self.sizes, self.pairs = group_sizes(axes)
        self.rows = v.shape[0]
        self.across = self.pairs == 4 and v.shape[0] % 32 == 0
        dma = pltpu.SemaphoreType.DMA
        self.inputs = [(v, pltpu.VMEM)]
        self.outputs = [(jax.ShapeDtypeStruct((self.pairs, 2) + v.shape, v.dtype), pl.ANY)]
        self.scratch = [dma] + [dma((self.pairs,))] * 4 + [dma((2,))] * 2

    greets = GroupScatter.greets

    def run(
        self,
        v_ref,
        out_ref,
        own_sem,
        push_send,
        push_recv,
        relay_send,
        relay_recv,
        pass_send,
        pass_recv,
    ):
        pairs, rows = self.pairs, self.rows
        bits = pairs.bit_length() - 1
        chip, core, device = group_layout(self.axes, self.sizes)
        middle = rows // 2
        halves = (pl.ds(0, middle), pl.ds(middle, rows - middle))

        def push(mask, source):
            return pltpu.make_async_remote_copy(
                src_ref=v_ref,
                dst_ref=out_ref.at[source, core],
                send_sem=push_send.at[mask],
                recv_sem=push_recv.at[mask],
                device_id=device(flip(chip, mask, bits), core),
                device_id_type=MESH,
            )

        def pass_on(mask, source, part):
            return pltpu.make_async_remote_copy(
                src_ref=out_ref.at[source, core, halves[part]],
                dst_ref=out_ref.at[source, core, halves[part]],
                send_sem=pass_send.at[part],
                recv_sem=pass_recv.at[part],
                device_id=device(flip(chip, mask, bits), core),
                device_id_type=MESH,
            )

        def relay(mask, side):
            source = flip(chip, mask, bits)
            return pltpu.make_async_remote_copy(
                src_ref=v_ref if mask == 0 else out_ref.at[source, side],
                dst_ref=out_ref.at[source, side],
                send_sem=relay_send.at[mask],
                recv_sem=relay_recv.at[mask],
                device_id=device(chip, 1 - core),
                device_id_type=MESH,
            )

        direct = (1, 2) if self.across else tuple(range(1, pairs))
        for mask in direct:
            push(mask, chip).start()
        relay(0, core).start()
        own = pltpu.make_async_copy(v_ref, out_ref.at[chip, core], own_sem)
        own.start()
        yield
        for mask in direct:
            push(mask, flip(chip, mask, bits)).wait_recv()
            if self.across:
                pass_on(3 - mask, flip(chip, mask, bits), mask - 1).start()
            relay(mask, core).start()
        yield
        if self.across:
            for part in range(2):
                pass_on(part + 1, flip(chip, 3, bits), part).wait_recv()
            relay(3, core).start()
        own.wait()
        yield
        for mask in range(pairs):
            relay(mask, 1 - core).wait_recv()
        for mask in range(pairs):
            relay(mask, core).wait_send()
            if mask in direct:
                push(mask, chip).wait_send()
                if self.across:
                    pass_on(3 - mask, flip(chip, mask, bits), mask - 1).wait_send()


class ContextThenLine:
    def __init__(self, value, count, axes, axis):
        self.first = [GroupScatter(value, axes, pick=number) for number in range(count)]
        rows, width = value.shape[2:]
        total = lax.axis_size(axis)
        self.second = LineScatter(
            jax.ShapeDtypeStruct((count, total, rows // total, width), BF16), axis
        )
        self.inputs = [entry for job in self.first for entry in job.inputs]
        self.outputs = self.second.outputs
        self.scratch = [pltpu.VMEM((count, rows, width), BF16)]
        self.scratch += [entry for job in self.first for entry in job.scratch]
        self.scratch += self.second.scratch

    def greets(self):
        return [device for job in self.first + [self.second] for device in job.greets()]

    def run(self, *refs):
        refs = list(refs)
        count = len(self.first)
        inputs, out_ref, between, refs = refs[:count], refs[count], refs[count + 1], refs[count + 2 :]
        steps = []
        for number, job in enumerate(self.first):
            used = len(job.scratch)
            steps.append(job.run(inputs[number], between.at[number], *refs[:used]))
            refs = refs[used:]
        for _ in zip(*steps):
            yield
        for step in steps:
            for _ in step:
                pass
        yield from self.second.run(between, out_ref, *refs)


class SumThenShare:
    def __init__(self, parts, extras, finish, shares, results):
        self.parts, self.finish = parts, finish
        self.gathers = [LineGather(share, "tensor") for share in shares]
        self.counts = (len(extras), len(results))
        self.inputs = [entry for job in parts for entry in job.inputs]
        self.inputs += [(extra, pltpu.VMEM) for extra in extras]
        self.outputs = [entry for job in self.gathers for entry in job.outputs]
        self.outputs += [(result, pltpu.VMEM) for result in results]
        self.scratch = [pltpu.VMEM(shape.shape, shape.dtype) for job in parts for shape, _ in job.outputs]
        self.scratch += [pltpu.VMEM(share.shape, share.dtype) for share in shares]
        for job in parts + self.gathers:
            self.scratch += job.scratch

    def greets(self):
        return [device for job in self.parts + self.gathers[:1] for device in job.greets()]

    def run(self, *refs):
        refs = list(refs)

        def take(count):
            taken = refs[:count]
            del refs[:count]
            return taken

        part_inputs = [take(len(job.inputs)) for job in self.parts]
        extras = take(self.counts[0])
        outputs = take(len(self.gathers))
        results = take(self.counts[1])
        sums = take(len(self.parts))
        shares = take(len(self.gathers))
        running = [
            job.run(*inputs, total, *take(len(job.scratch)))
            for job, inputs, total in zip(self.parts, part_inputs, sums)
        ]
        gathers = [
            job.run(share, output, *take(len(job.scratch)))
            for job, share, output in zip(self.gathers, shares, outputs)
        ]
        yield from side_by_side(running)
        self.finish(sums, extras, shares, results)
        yield from side_by_side(gathers)


def side_by_side(running):
    while running:
        left = []
        for step in running:
            try:
                next(step)
                left.append(step)
            except StopIteration:
                pass
        running = left
        yield


class GroupSum:
    def __init__(self, v, axes):
        self.first = GroupScatter(v, axes)
        self.second = GroupGather(jax.ShapeDtypeStruct(v.shape[1:], BF16), axes)
        self.inputs, self.outputs = self.first.inputs, self.second.outputs
        self.scratch = [pltpu.VMEM(v.shape[1:], BF16)] + self.first.scratch + self.second.scratch
        self.greets = self.first.greets

    def run(self, v_ref, out_ref, between, *refs):
        used = len(self.first.scratch)
        yield from self.first.run(v_ref, between, *refs[:used])
        yield from self.second.run(between, out_ref, *refs[used:])


def exchange_kernel(jobs, *refs):
    refs = list(refs)
    taken = [[], [], []]
    for number, part in enumerate(("inputs", "outputs", "scratch")):
        for job in jobs:
            count = len(getattr(job, part))
            taken[number].append(refs[:count])
            refs = refs[count:]
    meet([device for job in jobs for device in job.greets()])
    running = [
        job.run(*taken[0][at], *taken[1][at], *taken[2][at]) for at, job in enumerate(jobs)
    ]
    for _ in side_by_side(running):
        pass


def exchange(jobs, collective_id, micros):
    inputs = [entry for job in jobs for entry in job.inputs]
    outputs = [entry for job in jobs for entry in job.outputs]
    return pl.pallas_call(
        functools.partial(exchange_kernel, jobs),
        out_shape=tuple(shape for shape, _ in outputs),
        in_specs=[pl.BlockSpec(memory_space=space) for _, space in inputs],
        out_specs=tuple(pl.BlockSpec(memory_space=space) for _, space in outputs),
        scratch_shapes=[entry for job in jobs for entry in job.scratch],
        compiler_params=pltpu.CompilerParams(
            collective_id=collective_id, has_side_effects=True, vmem_limit_bytes=56 * MIB
        ),
        cost_estimate=pl.CostEstimate(
            flops=0, bytes_accessed=360_000 * micros, transcendentals=0
        ),
        name="exchange_" + "_".join(type(job).__name__ for job in jobs[:3]),
    )(*[value for value, _ in inputs])


KV_WIDTH = 640


def turn(vectors, cosine, sine):
    half_dim = vectors.shape[-1] // 2
    swapped = jnp.concatenate([vectors[:, half_dim:], vectors[:, :half_dim]], axis=1)
    return vectors * cosine + swapped * sine


def head_scores(query, key_nope, key_rope, allowed):
    raw = mm_nt(query[:, :NOPE], key_nope) + mm_nt(query[:, NOPE:], key_rope)
    return jnp.where(allowed, raw * (NOPE + ROPE) ** (-0.5), -1e30)


def allowed_keys(row_ref, column_ref, row_place_ref, column_place_ref):
    return (row_ref[0] == column_ref[0]) & (column_place_ref[...] <= row_place_ref[...])


def attend_kernel(
    x_ref,
    kv_ref,
    row_ref,
    column_ref,
    row_place_ref,
    column_place_ref,
    cos_ref,
    sin_ref,
    query_w,
    up_w,
    out_w,
    part_ref,
    attended_ref,
    query_ref,
    expanded_ref,
    log_ref,
):
    heads = query_w.shape[1] // (NOPE + ROPE)
    allowed = allowed_keys(row_ref, column_ref, row_place_ref, column_place_ref)
    latent = kv_ref[:, :LATENT]
    key_rope = kv_ref[:, LATENT : LATENT + ROPE]
    query = mm(x_ref[...], query_w[...])
    for head in range(heads):
        start = head * (NOPE + ROPE)
        rope = turn(query[:, start + NOPE : start + NOPE + ROPE], cos_ref[...], sin_ref[...])
        query_ref[0, head, :, :NOPE] = query[:, start : start + NOPE].astype(BF16)
        query_ref[0, head, :, NOPE:] = rope.astype(BF16)
        at = slice(head * (NOPE + VDIM), (head + 1) * (NOPE + VDIM))
        expanded_ref[0, :, at] = mm(latent, up_w[:, at]).astype(BF16)
        key_nope = expanded_ref[0, :, at.start : at.start + NOPE]
        values = expanded_ref[0, :, at.start + NOPE : at.stop]
        scores = head_scores(query_ref[0, head], key_nope, key_rope, allowed)
        top = jnp.max(scores, axis=-1, keepdims=True)
        weights = jnp.where(allowed, jnp.exp(scores - top), 0.0)
        total = jnp.sum(weights, axis=-1, keepdims=True)
        log_ref[0, head] = top + jnp.log(total)
        probs = (weights / total).astype(BF16)
        attended_ref[:, head * VDIM : (head + 1) * VDIM] = mm(probs, values).astype(BF16)
    part_ref[...] = mm(attended_ref[...], out_w[...]).astype(BF16)


def attend_back_kernel(
    grad_ref,
    attended_ref,
    x_ref,
    kv_ref,
    row_ref,
    column_ref,
    row_place_ref,
    column_place_ref,
    cos_ref,
    sin_ref,
    query_ref,
    expanded_ref,
    log_ref,
    query_w,
    up_w,
    out_w,
    kv_grad_ref,
    x_grad_ref,
    query_w_ref,
    up_w_ref,
    out_w_ref,
    query_grad,
    expanded_grad,
    query_w_sum,
    up_w_sum,
    out_w_sum,
):
    heads = query_w.shape[1] // (NOPE + ROPE)
    scale = (NOPE + ROPE) ** (-0.5)
    allowed = allowed_keys(row_ref, column_ref, row_place_ref, column_place_ref)
    latent = kv_ref[:, :LATENT]
    key_rope = kv_ref[:, LATENT : LATENT + ROPE]
    grad = grad_ref[...]
    attended_grad = mm_nt(grad, out_w[...]).astype(BF16)
    rope_grad = jnp.zeros((kv_ref.shape[0], ROPE), F32)
    for head in range(heads):
        first = head * (NOPE + VDIM)
        key_nope = expanded_ref[0, :, first : first + NOPE]
        values = expanded_ref[0, :, first + NOPE : first + NOPE + VDIM]
        query = query_ref[0, head]
        scores = head_scores(query, key_nope, key_rope, allowed)
        probs = jnp.where(allowed, jnp.exp(scores - log_ref[0, head]), 0.0)
        own_grad = attended_grad[:, head * VDIM : (head + 1) * VDIM]
        probs_grad = mm_nt(own_grad, values)
        moved = probs * (probs_grad - jnp.sum(probs * probs_grad, axis=-1, keepdims=True))
        moved = moved.astype(BF16)
        expanded_grad[:, first : first + NOPE] = (
            scale * mm_tn(moved, query[:, :NOPE])
        ).astype(BF16)
        expanded_grad[:, first + NOPE : first + NOPE + VDIM] = mm_tn(
            probs.astype(BF16), own_grad
        ).astype(BF16)
        rope_grad = rope_grad + mm_tn(moved, query[:, NOPE:])
        start = head * (NOPE + ROPE)
        query_grad[:, start : start + NOPE] = (scale * mm(moved, key_nope)).astype(BF16)
        query_grad[:, start + NOPE : start + NOPE + ROPE] = turn(
            scale * mm(moved, key_rope), cos_ref[...], -sin_ref[...]
        ).astype(BF16)
    latent_grad = mm_nt(expanded_grad[...], up_w[...]).astype(BF16)
    rope_grad = (scale * rope_grad).astype(BF16)
    rows = x_ref.shape[0]
    for block in range(kv_grad_ref.shape[0]):
        at = slice(block * rows, (block + 1) * rows)
        kv_grad_ref[block, 0, :, :LATENT] = latent_grad[at]
        kv_grad_ref[block, 0, :, LATENT:] = rope_grad[at]
    x_grad_ref[...] = mm_nt(query_grad[...], query_w[...]).astype(BF16)
    pieces = (
        (query_w_sum, query_w_ref, x_ref[...], query_grad[...]),
        (up_w_sum, up_w_ref, latent, expanded_grad[...]),
        (out_w_sum, out_w_ref, attended_ref[...], grad),
    )
    step = pl.program_id(0)

    @pl.when(step == 0)
    def _():
        for total, _, left, right in pieces:
            total[...] = mm_tn(left, right)

    @pl.when(step > 0)
    def _():
        for total, _, left, right in pieces:
            total[...] += mm_tn(left, right)

    @pl.when(step == pl.num_programs(0) - 1)
    def _():
        for total, target, _, _ in pieces:
            target[...] = total[...].astype(BF16)


def attention_specs(micro_count, rows, seq_len, heads):
    per_micro = lambda *shape: pl.BlockSpec((1,) + shape, lambda m: (m,) + (0,) * len(shape))
    rows_of = lambda width: pl.BlockSpec((rows, width), lambda m: (m, 0))
    whole = lambda *shape: pl.BlockSpec(
        shape, lambda m: (0,) * len(shape), pipeline_mode=pl.Buffered(1)
    )
    places = [
        per_micro(rows, 1),
        per_micro(1, seq_len),
        whole(rows, 1),
        whole(1, seq_len),
        whole(rows, ROPE),
        whole(rows, ROPE),
    ]
    weights = [
        whole(D, heads * (NOPE + ROPE)),
        whole(LATENT, heads * (NOPE + VDIM)),
        whole(heads * VDIM, D),
    ]
    kept = [
        rows_of(heads * VDIM),
        per_micro(heads, rows, NOPE + ROPE),
        per_micro(seq_len, heads * (NOPE + VDIM)),
        per_micro(heads, rows, 1),
    ]
    return per_micro, rows_of, whole, places, weights, kept


def kv_spec(seq_len):
    return pl.BlockSpec((seq_len, KV_WIDTH), lambda m: (0, m))


def attend(x_attn, kv_all, places, weights, micro_count, heads):
    rows, seq_len = x_attn.shape[0] // micro_count, kv_all.shape[0]
    per_micro, rows_of, _, place_specs, weight_specs, kept = attention_specs(
        micro_count, rows, seq_len, heads
    )
    total = micro_count * rows
    return pl.pallas_call(
        attend_kernel,
        grid=(micro_count,),
        in_specs=[rows_of(D), kv_spec(seq_len)] + place_specs + weight_specs,
        out_specs=[rows_of(D)] + kept,
        out_shape=[
            jax.ShapeDtypeStruct((total, D), BF16),
            jax.ShapeDtypeStruct((total, heads * VDIM), BF16),
            jax.ShapeDtypeStruct((micro_count, heads, rows, NOPE + ROPE), BF16),
            jax.ShapeDtypeStruct((micro_count, seq_len, heads * (NOPE + VDIM)), BF16),
            jax.ShapeDtypeStruct((micro_count, heads, rows, 1), F32),
        ],
        compiler_params=pltpu.CompilerParams(vmem_limit_bytes=56 * MIB),
        cost_estimate=pl.CostEstimate(
            flops=9_000_000_000, bytes_accessed=60_000_000, transcendentals=0
        ),
        name="attend",
    )(x_attn, kv_all, *places, *weights)


def attend_back(grad, x_attn, kv_all, places, weights, kept, micro_count, heads):
    rows, seq_len = x_attn.shape[0] // micro_count, kv_all.shape[0]
    per_micro, rows_of, whole, place_specs, weight_specs, kept_specs = attention_specs(
        micro_count, rows, seq_len, heads
    )
    total = micro_count * rows
    return pl.pallas_call(
        attend_back_kernel,
        grid=(micro_count,),
        in_specs=[rows_of(D), kept_specs[0], rows_of(D), kv_spec(seq_len)]
        + place_specs
        + kept_specs[1:]
        + weight_specs,
        out_specs=[
            pl.BlockSpec((seq_len // rows, 1, rows, LATENT + ROPE), lambda m: (0, m, 0, 0)),
            rows_of(D),
        ]
        + weight_specs,
        out_shape=[
            jax.ShapeDtypeStruct((seq_len // rows, micro_count, rows, LATENT + ROPE), BF16),
            jax.ShapeDtypeStruct((total, D), BF16),
            jax.ShapeDtypeStruct(weights[0].shape, BF16),
            jax.ShapeDtypeStruct(weights[1].shape, BF16),
            jax.ShapeDtypeStruct(weights[2].shape, BF16),
        ],
        scratch_shapes=[
            pltpu.VMEM((rows, heads * (NOPE + ROPE)), BF16),
            pltpu.VMEM((seq_len, heads * (NOPE + VDIM)), BF16),
            pltpu.VMEM(weights[0].shape, F32),
            pltpu.VMEM(weights[1].shape, F32),
            pltpu.VMEM(weights[2].shape, F32),
        ],
        compiler_params=pltpu.CompilerParams(vmem_limit_bytes=60 * MIB),
        cost_estimate=pl.CostEstimate(
            flops=2_000_000_000, bytes_accessed=10_000_000, transcendentals=0
        ),
        name="attend_back",
    )(grad, kept[0], x_attn, kv_all, *places, *kept[1:], *weights)


PEER_SLOTS = 4


def expert_kernel(
    pairs,
    context_size,
    fe,
    x_ref,
    cot_ref,
    gate_in,
    up_in,
    down_in,
    router_in,
    shared_gate_in,
    shared_up_in,
    shared_down_in,
    out_ref,
    part_ref,
    gate_out,
    up_out,
    down_out,
    router_out,
    shared_out,
    shared_part,
    shared_grads,
    x_all,
    gate_ref,
    up_ref,
    down_ref,
    x_tile,
    cot_tile,
    out_tile,
    grad_tile,
    peer_tile,
    grad_gate,
    grad_up,
    hidden_low,
    gate_acc,
    up_acc,
    down_acc,
    x_send,
    x_recv,
    relay_send,
    relay_recv,
    pass_send,
    pass_recv,
    x_load,
    cot_load,
    out_store,
    swap_send,
    swap_recv,
    sum_send,
    sum_recv,
    weight_load,
    grad_store,
    shared_store,
    acc_store,
    credit,
):
    micro_count, rows = x_ref.shape[0], x_ref.shape[1]
    units = gate_ref.shape[0]
    shared_units = shared_gate_in.shape[0]
    half = units // EXP_DEV
    experts = 2 * pairs * EXP_DEV
    bits = pairs.bit_length() - 1
    steps = micro_count * pairs
    across = pairs == 4
    place = lax.axis_index("dp") * context_size + lax.axis_index("context")
    core = lax.rem(place, 2)
    chip = lax.div(place, 2)

    def device(chip_index, core_index):
        index = chip_index * 2 + core_index
        return {"dp": lax.div(index, context_size), "context": lax.rem(index, context_size)}

    sibling = device(chip, 1 - core)
    meet([sibling] + [device(flip(chip, mask, bits), core) for mask in range(1, pairs)])

    def step_of(step):
        micro = lax.div(step, pairs)
        turn = lax.rem(step, pairs)
        backward = lax.rem(micro, 2)
        return micro, lax.rem(turn + backward, pairs)

    def push_x(micro, mask):
        return pltpu.make_async_remote_copy(
            src_ref=x_ref.at[micro],
            dst_ref=x_all.at[micro, chip, core],
            send_sem=x_send.at[micro, mask],
            recv_sem=x_recv.at[micro, mask],
            device_id=device(flip(chip, mask, bits), core),
            device_id_type=MESH,
        )

    def relay(micro, mask, own=False):
        source = flip(chip, mask, bits)
        return pltpu.make_async_remote_copy(
            src_ref=x_ref.at[micro] if own else x_all.at[micro, source, core],
            dst_ref=x_all.at[micro, source, core],
            send_sem=relay_send.at[micro, mask],
            recv_sem=relay_recv.at[micro, mask],
            device_id=sibling,
            device_id_type=MESH,
        )

    def relay_arrival(micro, mask):
        source = flip(chip, mask, bits)
        return pltpu.make_async_remote_copy(
            src_ref=x_all.at[micro, source, 1 - core],
            dst_ref=x_all.at[micro, source, 1 - core],
            send_sem=relay_send.at[micro, mask],
            recv_sem=relay_recv.at[micro, mask],
            device_id=sibling,
            device_id_type=MESH,
        )

    def x_arrival(micro, mask):
        return pltpu.make_async_remote_copy(
            src_ref=x_ref.at[micro],
            dst_ref=x_all.at[micro, flip(chip, mask, bits), core],
            send_sem=x_send.at[micro, mask],
            recv_sem=x_recv.at[micro, mask],
            device_id=device(flip(chip, mask, bits), core),
            device_id_type=MESH,
        )

    middle = rows // 2
    parts = (pl.ds(0, middle), pl.ds(middle, rows - middle))

    def pass_on(micro, mask, source, part):
        return pltpu.make_async_remote_copy(
            src_ref=x_all.at[micro, source, core, parts[part]],
            dst_ref=x_all.at[micro, source, core, parts[part]],
            send_sem=pass_send.at[micro, part],
            recv_sem=pass_recv.at[micro, part],
            device_id=device(flip(chip, mask, bits), core),
            device_id_type=MESH,
        )

    def half_tile(side):
        return pl.ds(pl.multiple_of(side * rows, rows), rows)

    def load_cot(step):
        micro, mask = step_of(step)
        slot = lax.rem(step, 2)
        source = flip(chip, mask, bits)
        return [
            pltpu.make_async_copy(
                cot_ref.at[2 * source + side, micro],
                cot_tile.at[slot, half_tile(side)],
                cot_load.at[slot, side],
            )
            for side in range(2)
        ]

    def load_own(step):
        slot = lax.rem(step, 2)
        return pltpu.make_async_copy(
            x_ref.at[step_of(step)[0]], x_tile.at[slot, half_tile(core)], x_load.at[slot, 0]
        )

    def load_x(step, number):
        micro, mask = step_of(step)
        slot = lax.rem(step, 2)
        side = core if number == 0 else 1 - core
        return pltpu.make_async_copy(
            x_all.at[micro, flip(chip, mask, bits), side],
            x_tile.at[slot, half_tile(side)],
            x_load.at[slot, number],
        )

    def store(step):
        micro, mask = step_of(step)
        return [
            pltpu.make_async_copy(
                out_tile.at[pl.ds(side * rows, rows)],
                out_ref.at[2 * flip(chip, mask, bits) + side, micro],
                out_store.at[side],
            )
            for side in range(2)
        ]

    def swap(step):
        slot = lax.rem(step, 2)
        held = lax.rem(step, PEER_SLOTS)
        return pltpu.make_async_remote_copy(
            src_ref=grad_tile.at[pl.ds(pl.multiple_of((1 - core) * rows, rows), rows)],
            dst_ref=peer_tile.at[held],
            send_sem=swap_send.at[slot],
            recv_sem=swap_recv.at[held],
            device_id=sibling,
            device_id_type=MESH,
        )

    def push_sum(step):
        micro, mask = step_of(step)
        slot = lax.rem(step, PEER_SLOTS)
        return pltpu.make_async_remote_copy(
            src_ref=peer_tile.at[slot],
            dst_ref=part_ref.at[micro, mask],
            send_sem=sum_send.at[slot],
            recv_sem=sum_recv.at[micro, mask],
            device_id=device(flip(chip, mask, bits), core),
            device_id_type=MESH,
        )

    def keep_sum(step):
        micro, mask = step_of(step)
        slot = lax.rem(step, PEER_SLOTS)
        return pltpu.make_async_copy(
            peer_tile.at[slot], part_ref.at[micro, mask], sum_send.at[slot]
        )

    def wait_sum_sent(step):
        mask = step_of(step)[1]

        @pl.when(mask > 0)
        def _():
            push_sum(step).wait_send()

        @pl.when(mask == 0)
        def _():
            keep_sum(step).wait()

    def fetch(step):
        micro, mask = step_of(step)

        if not across:

            @pl.when(mask > 0)
            def _():
                x_arrival(micro, mask).wait_recv()
                relay(micro, mask).start()

        else:

            @pl.when((mask == 1) | (mask == 2))
            def _():
                x_arrival(micro, mask).wait_recv()
                relay(micro, mask).start()

            for part in range(2):

                @pl.when(mask == part + 1)
                def _():
                    pass_on(micro, 2 - part, flip(chip, part + 1, bits), part).start()

            @pl.when(mask == 3)
            def _():
                for part in range(2):
                    pass_on(micro, part + 1, flip(chip, 3, bits), part).wait_recv()
                relay(micro, mask).start()

        for copy in load_cot(step):
            copy.start()

        @pl.when(mask == 0)
        def _():
            load_own(step).start()

        @pl.when(mask > 0)
        def _():
            load_x(step, 0).start()

    def fetch_relayed(step):
        micro, mask = step_of(step)
        relay_arrival(micro, mask).wait_recv()
        load_x(step, 1).start()

    def finish_sum(step):
        slot = lax.rem(step, 2)
        held = lax.rem(step, PEER_SLOTS)
        swap(step).wait()

        def add(index, carry):
            at = pl.ds(pl.multiple_of(index * 16, 16), 16)
            mine = pl.ds(pl.multiple_of(core * rows + index * 16, 16), 16)
            value = grad_tile[mine, :].astype(F32) + peer_tile[held, at, :].astype(F32)
            peer_tile[held, at, :] = value.astype(BF16)
            return carry

        lax.fori_loop(0, rows // 16, add, 0)

        mask = step_of(step)[1]

        @pl.when(mask > 0)
        def _():
            push_sum(step).start()

        @pl.when(mask == 0)
        def _():
            keep_sum(step).start()

    direct = (1, 2) if across else tuple(range(1, pairs))
    for mask in direct:
        push_x(0, mask).start()
    for micro in range(micro_count):
        relay(micro, 0, own=True).start()

    def weights_in(pieces):
        copies = []
        for number, (source, target, start) in enumerate(pieces):
            copies.append(
                pltpu.make_async_copy(
                    source, target.at[pl.ds(start, source.shape[0])], weight_load.at[number]
                )
            )
        return copies

    shared_weights = weights_in(
        [(shared_gate_in, gate_ref, 0), (shared_up_in, up_ref, 0), (shared_down_in, down_ref, 0)]
    )
    for copy in shared_weights:
        copy.start()
    shared_rows = []
    for micro in range(micro_count):
        at = pl.ds(micro * rows, rows)
        shared_rows.append(
            pltpu.make_async_copy(x_ref.at[micro], x_tile.at[1, at], x_load.at[1, micro])
        )
        shared_rows.append(
            pltpu.make_async_copy(cot_ref.at[place, micro], cot_tile.at[1, at], cot_load.at[1, micro])
        )
    for copy in shared_rows:
        copy.start()
    for target in (gate_ref, up_ref, down_ref):
        target[shared_units:, :] = jnp.zeros((units - shared_units, D), BF16)
    fetch(0)

    chunk = 256 if units % 256 == 0 else LANES
    out_chunk = 512
    slab = half - LANES
    first_lane = fe % LANES
    slab_chunk = slab // chunk * chunk

    def hidden_pass(x, cot, here, start, gate, scale):
        at = slice(start, start + chunk)
        up = mm_nt(x, up_ref[at, :])
        back = mm_nt(cot, down_ref[at, :])
        sig = jax.nn.sigmoid(gate)
        act = gate * sig
        hidden = act * up
        grad_hidden = back if scale is None else back * scale
        scaled = hidden if scale is None else hidden * scale
        hidden_low[here, at] = scaled.astype(BF16)
        grad_gate[here, at] = (grad_hidden * up * (sig * (1.0 + gate * (1.0 - sig)))).astype(BF16)
        grad_up[here, at] = (grad_hidden * act).astype(BF16)
        return hidden * back

    def grad_pass():
        for start in range(0, D, out_chunk):
            at = slice(start, start + out_chunk)
            grad = mm(grad_gate[...], gate_ref[:, at]) + mm(grad_up[...], up_ref[:, at])
            grad_tile[:, at] = grad.astype(BF16)

    def out_pass():
        for start in range(0, D, out_chunk):
            at = slice(start, start + out_chunk)
            out_tile[:, at] = mm(hidden_low[...], down_ref[:, at]).astype(BF16)

    for copy in shared_weights + shared_rows:
        copy.wait()
    row_halves = (slice(0, rows), slice(rows, 2 * rows))
    for here in row_halves:
        x, cot = x_tile[1, here, :D], cot_tile[1, here]
        for start in range(0, units, chunk):
            gate = mm_nt(x, gate_ref[start : start + chunk, :])
            hidden_pass(x, cot, here, start, gate, None)
    grad_pass()
    out_pass()
    expert_weights = weights_in(
        [
            piece
            for number in range(EXP_DEV)
            for piece in (
                (gate_in.at[number], gate_ref, number * half),
                (up_in.at[number], up_ref, number * half),
                (down_in.at[number], down_ref, number * half),
            )
        ]
        + [(router_in, gate_ref, fe)]
    )
    for copy in expert_weights:
        copy.start()
    for target in (gate_ref, up_ref, down_ref):
        for number in range(EXP_DEV):
            first = number * half + fe
            if target is gate_ref and number == 0:
                first += experts
            last = (number + 1) * half
            if last > first:
                target[first:last, :] = jnp.zeros((last - first, D), BF16)
    shared_stores = []
    for micro in range(micro_count):
        at = pl.ds(micro * rows, rows)
        shared_stores.append(
            pltpu.make_async_copy(out_tile.at[at], shared_out.at[micro], shared_store.at[micro, 0])
        )
        shared_stores.append(
            pltpu.make_async_copy(
                grad_tile.at[at], shared_part.at[micro], shared_store.at[micro, 1]
            )
        )
    for copy in shared_stores:
        copy.start()
    fetch_relayed(0)
    for copy in shared_stores:
        copy.wait()
    staged = []
    for which, (left, right) in enumerate(
        ((grad_gate, x_tile[1, :, :D]), (grad_up, x_tile[1, :, :D]), (hidden_low, cot_tile[1]))
    ):
        for start in range(0, units, rows):
            stage = len(staged) % 2 * rows
            if len(staged) >= 2:
                staged[-2].wait()
            out_tile[stage : stage + rows, :] = mm_tn(
                left[:, start : start + rows], right
            ).astype(BF16)
            copy = pltpu.make_async_copy(
                out_tile.at[pl.ds(stage, rows)],
                shared_grads.at[which, pl.ds(start, rows)],
                grad_store.at[len(staged) % 2],
            )
            copy.start()
            staged.append(copy)
    for acc in (gate_acc, up_acc, down_acc):
        acc[...] = jnp.zeros_like(acc)
    for copy in staged[-2:] + expert_weights:
        copy.wait()

    def work(step, carry):
        slot = lax.rem(step, 2)

        for copy in load_cot(step):
            copy.wait()
        for number in range(2):
            load_x(step, number).wait()

        for here in row_halves:
            x = x_tile[slot, here, :D]
            chosen = x_tile[slot, here, D:].astype(F32)
            cot = cot_tile[slot, here]
            lane = lax.broadcasted_iota(jnp.int32, (rows, LANES), 1) - first_lane
            valid = (lane >= 0) & (lane < experts)

            first_gate = mm_nt(x, gate_ref[slab_chunk : slab_chunk + chunk, :])
            slab_gate = first_gate[:, slab - slab_chunk : slab - slab_chunk + LANES]
            logits = jnp.where(valid, slab_gate, -1e30)
            weights = jnp.where(
                valid, jnp.exp(logits - jnp.max(logits, axis=-1, keepdims=True)), 0.0
            )
            router_probs = weights / jnp.sum(weights, axis=-1, keepdims=True)
            named = router_probs * chosen
            picks = [lane == place * EXP_DEV + number for number in range(EXP_DEV)]
            scales = [
                jnp.sum(jnp.where(pick, named, 0.0), axis=-1, keepdims=True) for pick in picks
            ]
            flags = [
                jnp.sum(jnp.where(pick, chosen, 0.0), axis=-1, keepdims=True) for pick in picks
            ]
            dots = [jnp.zeros((rows, 1), F32) for _ in picks]
            column = lax.broadcasted_iota(jnp.int32, (rows, chunk), 1)
            starts = [slab_chunk] + [at for at in range(0, units, chunk) if at != slab_chunk]
            for start in starts:
                if start == slab_chunk:
                    gate = first_gate
                else:
                    gate = mm_nt(x, gate_ref[start : start + chunk, :])
                first, last = start // half, (start + chunk - 1) // half
                scale = scales[first]
                if last > first:
                    scale = jnp.where(column < last * half - start, scales[first], scales[last])
                product = hidden_pass(x, cot, here, start, gate, scale)
                if last > first:
                    split = last * half - start
                    dots[first] = dots[first] + jnp.sum(product[:, :split], axis=-1, keepdims=True)
                    dots[last] = dots[last] + jnp.sum(product[:, split:], axis=-1, keepdims=True)
                else:
                    dots[first] = dots[first] + jnp.sum(product, axis=-1, keepdims=True)
            spread = jnp.zeros((rows, LANES), F32)
            for pick, dot, flag in zip(picks, dots, flags):
                spread = spread + jnp.where(pick, dot * flag, 0.0)
            grad_logits = router_probs * (
                spread - jnp.sum(router_probs * spread, axis=-1, keepdims=True)
            )
            grad_gate[here, slab:half] = jnp.where(
                lane < 0, grad_gate[here, slab:half].astype(F32), grad_logits
            ).astype(BF16)

        @pl.when(step + 1 < steps)
        def _():
            fetch(step + 1)

        @pl.when(step == 0)
        def _():
            for micro in range(1, micro_count):
                for mask in direct:
                    push_x(micro, mask).start()

        @pl.when(step >= 1)
        def _():
            finish_sum(step - 1)

        @pl.when(step >= PEER_SLOTS)
        def _():
            wait_sum_sent(step - PEER_SLOTS)
            pl.semaphore_signal(credit, inc=1, device_id=sibling, device_id_type=MESH)
            pl.semaphore_wait(credit, 1)

        grad_pass()
        swap(step).start()


        @pl.when(step >= 1)
        def _():
            for copy in store(step - 1):
                copy.wait()

        out_pass()
        for copy in store(step):
            copy.start()

        @pl.when(step + 1 < steps)
        def _():
            fetch_relayed(step + 1)

        for acc, left, right in (
            (gate_acc, grad_gate, x_tile),
            (up_acc, grad_up, x_tile),
            (down_acc, hidden_low, cot_tile),
        ):
            for start in range(0, D, out_chunk):
                at = slice(start, start + out_chunk)
                acc[:, at] += mm_tn(left[...], right[slot, :, at])
        return carry


    lax.fori_loop(0, steps, work, 0)
    finals = [
        pltpu.make_async_copy(
            gate_acc.at[pl.ds(fe, experts)], router_out, acc_store.at[EXP_DEV, 0]
        )
    ]
    for number in range(EXP_DEV):
        for which, (acc, target) in enumerate(
            ((gate_acc, gate_out), (up_acc, up_out), (down_acc, down_out))
        ):
            finals.append(
                pltpu.make_async_copy(
                    acc.at[pl.ds(number * half, fe)],
                    target.at[number],
                    acc_store.at[number, which],
                )
            )
    for copy in finals:
        copy.start()
    finish_sum(steps - 1)
    for back in range(PEER_SLOTS, 0, -1):
        wait_sum_sent(steps - back)
    for copy in finals:
        copy.wait()
    for copy in store(steps - 1):
        copy.wait()
    for micro in range(micro_count):
        if across:
            for part in range(2):
                pass_on(micro, 2 - part, flip(chip, part + 1, bits), part).wait_send()
        for mask in range(pairs):
            relay(micro, mask).wait_send()
            if mask in direct:
                push_x(micro, mask).wait_send()
            if mask:
                pltpu.make_async_remote_copy(
                    src_ref=peer_tile.at[0],
                    dst_ref=part_ref.at[micro, mask],
                    send_sem=sum_send.at[0],
                    recv_sem=sum_recv.at[micro, mask],
                    device_id=device(flip(chip, mask, bits), core),
                    device_id_type=MESH,
                ).wait_recv()


def expert_pass(
    x_ext, cot_all, gate_w, up_w, down_w, router_w, shared_gate, shared_up, shared_down, collective_id
):
    micro_count, rows, width = x_ext.shape
    context_size = lax.axis_size("context")
    pairs = lax.axis_size("dp") * context_size // 2
    fe, experts, shared_units = gate_w.shape[1], router_w.shape[0], shared_gate.shape[0]
    half = -(-(fe + experts) // LANES) * LANES
    units = EXP_DEV * half
    dma = pltpu.SemaphoreType.DMA
    wide = jax.ShapeDtypeStruct((EXP_DEV, fe, D), F32)
    own = jax.ShapeDtypeStruct((micro_count, rows, D), BF16)
    return pl.pallas_call(
        functools.partial(expert_kernel, pairs, context_size, fe),
        out_shape=(
            jax.ShapeDtypeStruct((2 * pairs, micro_count, rows, D), BF16),
            jax.ShapeDtypeStruct((micro_count, pairs, rows, D), BF16),
            wide,
            wide,
            wide,
            jax.ShapeDtypeStruct((experts, D), F32),
            own,
            own,
            jax.ShapeDtypeStruct((3, units, D), BF16),
            jax.ShapeDtypeStruct((micro_count, pairs, 2, rows, width), BF16),
        ),
        in_specs=[pl.BlockSpec(memory_space=pl.ANY)] * 9,
        out_specs=(pl.BlockSpec(memory_space=pl.ANY),) * 10,
        scratch_shapes=[
            pltpu.VMEM((units, D), BF16),
            pltpu.VMEM((units, D), BF16),
            pltpu.VMEM((units, D), BF16),
            pltpu.VMEM((2, 2 * rows, width), BF16),
            pltpu.VMEM((2, 2 * rows, D), BF16),
            pltpu.VMEM((2 * rows, D), BF16),
            pltpu.VMEM((2 * rows, D), BF16),
            pltpu.VMEM((PEER_SLOTS, rows, D), BF16),
            pltpu.VMEM((2 * rows, units), BF16),
            pltpu.VMEM((2 * rows, units), BF16),
            pltpu.VMEM((2 * rows, units), BF16),
            pltpu.VMEM((units, D), F32),
            pltpu.VMEM((units, D), F32),
            pltpu.VMEM((units, D), F32),
            dma((micro_count, pairs)),
            dma((micro_count, pairs)),
            dma((micro_count, pairs)),
            dma((micro_count, pairs)),
            dma((micro_count, 2)),
            dma((micro_count, 2)),
            dma((2, 2)),
            dma((2, 2)),
            dma((2,)),
            dma((2,)),
            dma((PEER_SLOTS,)),
            dma((PEER_SLOTS,)),
            dma((micro_count, pairs)),
            dma((3 * EXP_DEV + 1,)),
            dma((2,)),
            dma((micro_count, 2)),
            dma((EXP_DEV + 1, 3)),
            pltpu.SemaphoreType.REGULAR,
        ],
        compiler_params=pltpu.CompilerParams(
            collective_id=collective_id, has_side_effects=True, vmem_limit_bytes=62 * MIB
        ),
        cost_estimate=pl.CostEstimate(
            flops=36 * (pairs * micro_count + 1) * rows * D * units,
            bytes_accessed=500_000_000,
            transcendentals=0,
        ),
        name="expert_pass",
    )(x_ext, cot_all, gate_w, up_w, down_w, router_w, shared_gate, shared_up, shared_down)[:9]


def per_device(
    tokens,
    segments,
    expert_ids,
    norm_attn,
    w_query,
    w_kv_down,
    norm_latent,
    w_kv_up,
    w_out,
    norm_ffn,
    w_router,
    w_shared_gate,
    w_shared_up,
    w_shared_down,
    w_expert_gate,
    w_expert_up,
    w_expert_down,
    cotangent,
):
    micro_count, block_rows = tokens.shape[:2]
    rows = micro_count * block_rows
    seq_len = segments.shape[1]
    context_size = lax.axis_size("context")
    groups = lax.axis_size("dp") * context_size
    tensor_size = lax.axis_size("tensor")
    group_index = lax.axis_index("dp") * context_size + lax.axis_index("context")
    own_rows = block_rows // tensor_size
    own_start = lax.axis_index("tensor") * own_rows
    experts = EXP_DEV * groups
    heads_local = w_query.shape[1] // (NOPE + ROPE)
    fe_local = w_expert_gate.shape[2]
    start_row = lax.axis_index("context") * block_rows
    query_index = start_row + jnp.arange(block_rows)
    key_index = jnp.arange(seq_len)
    cos_block, sin_block = angles(query_index.astype(F32), ROPE)
    cos_query = jnp.tile(cos_block, (micro_count, 1))
    sin_query = jnp.tile(sin_block, (micro_count, 1))
    gain_attn = norm_attn.astype(F32)
    gain_latent = norm_latent.astype(F32)
    gain_ffn = norm_ffn.astype(F32)

    def own(values):
        values = values.reshape((micro_count, block_rows) + values.shape[1:])
        part = lax.dynamic_slice_in_dim(values, own_start, own_rows, axis=1)
        return part.reshape((micro_count * own_rows,) + values.shape[2:])

    def to_owner(values):
        values = values.astype(BF16).reshape(micro_count, tensor_size, own_rows, values.shape[-1])
        return LineScatter(values, "tensor")

    def from_owners(values):
        return LineGather(values.reshape(micro_count, own_rows, values.shape[-1]), "tensor")

    def flat(values):
        return values.reshape(-1, values.shape[-1])

    ff_local = w_shared_gate.shape[1]
    slots = jnp.arange(LANES) - fe_local % LANES
    named = jnp.any(expert_ids[..., None] == slots, axis=2).astype(BF16)

    x_rows = tokens.reshape(rows, D).astype(F32)
    cot_rows = cotangent.reshape(rows, D)
    inv_attn = rms_scale(x_rows)
    normed_attn = x_rows * inv_attn
    x_attn = (normed_attn * gain_attn).astype(BF16)
    kv_raw = mm(x_attn, w_kv_down)
    latent_raw = kv_raw[:, :LATENT]
    inv_latent = rms_scale(latent_raw)
    normed_latent = latent_raw * inv_latent
    latent = (normed_latent * gain_latent).astype(BF16)
    key_rope = rotate(kv_raw[:, LATENT:], cos_query, sin_query).astype(BF16)
    blank = jnp.zeros((rows, KV_WIDTH - LATENT - ROPE), BF16)
    kv_own = jnp.concatenate([latent, key_rope, blank], axis=1)
    kv_own = kv_own.reshape(micro_count, block_rows, KV_WIDTH).transpose(1, 0, 2)
    kv_own = kv_own.reshape(block_rows, micro_count * KV_WIDTH)
    (kv_all,) = exchange([GroupGather(kv_own, ("context",))], 1, 20)
    kv_all, cot_late = lax.optimization_barrier((kv_all, cotangent))
    cot_all = lax.all_gather(cot_late, GROUP, axis=0)
    kv_all = kv_all.reshape(seq_len, micro_count * KV_WIDTH)
    seg_query = lax.dynamic_slice_in_dim(segments, start_row, block_rows, axis=1)
    places = (
        seg_query[:, :, None],
        segments[:, None, :],
        query_index[:, None],
        key_index[None, :],
        jnp.tile(cos_block, (1, 2)),
        jnp.concatenate([-sin_block, sin_block], axis=1),
    )
    weights = (w_query, w_kv_up, w_out)
    attn_part, *kept = attend(x_attn, kv_all, places, weights, micro_count, heads_local)
    own_shape = (micro_count, own_rows, D)
    tokens_own = own(tokens.reshape(rows, D)).reshape(own_shape)

    def finish_attention(sums, extras, shares, results):
        for m in range(micro_count):
            hidden = extras[0][m].astype(F32) + sums[0][m]
            results[0][m] = hidden
            shares[0][m] = (hidden * rms_scale(hidden) * extras[1][...]).astype(BF16)

    x_ffn, hidden_one = exchange(
        [
            SumThenShare(
                [to_owner(attn_part)],
                [tokens_own, gain_ffn[None]],
                finish_attention,
                [jax.ShapeDtypeStruct(own_shape, BF16)],
                [jax.ShapeDtypeStruct(own_shape, F32)],
            )
        ],
        2,
        80,
    )
    x_ffn = x_ffn.reshape(rows, D)
    x_ext = jnp.concatenate([x_ffn.reshape(micro_count, block_rows, D), named], axis=-1)

    (
        out_part,
        grad_part,
        gate_grad,
        up_grad,
        down_grad,
        router_grad,
        shared_out,
        shared_part,
        shared_grads,
    ) = expert_pass(
        x_ext,
        cot_all,
        w_expert_gate.transpose(0, 2, 1),
        w_expert_up.transpose(0, 2, 1),
        w_expert_down,
        w_router.T,
        w_shared_gate.T,
        w_shared_up.T,
        w_shared_down,
        4,
    )
    shared_units = shared_grads.shape[1]
    shared_grads = shared_grads.reshape(groups, -1, D)
    shared_grads = lax.psum_scatter(shared_grads, GROUP, scatter_dimension=0, tiled=False)
    cot_own = own(cot_rows).reshape(own_shape)

    def finish_experts(sums, extras, shares, results):
        hidden, cot, gain = extras
        gain_grad = jnp.zeros((1, D), F32)
        for m in range(micro_count):
            inverse = rms_scale(hidden[m])
            normed = hidden[m] * inverse
            grad = sums[0][m]
            gain_grad = gain_grad + jnp.sum(grad * normed, axis=0, keepdims=True)
            total = cot[m].astype(F32) + norm_back(grad * gain[...], normed, inverse)
            results[0][m] = total
            shares[0][m] = total.astype(BF16)
        results[1][...] = gain_grad

    out_sum = lax.psum_scatter(out_part, GROUP, scatter_dimension=0, tiled=False)
    grad_attn_low, grad_one, norm_ffn_grad = exchange(
        [
            SumThenShare(
                [LineScatterSum(grad_part, shared_part, "tensor")],
                [hidden_one, cot_own, gain_ffn[None]],
                finish_experts,
                [jax.ShapeDtypeStruct(own_shape, BF16)],
                [
                    jax.ShapeDtypeStruct(own_shape, F32),
                    jax.ShapeDtypeStruct((1, D), F32),
                ],
            ),
        ],
        5,
        90,
    )
    grad_attn_low = grad_attn_low.reshape(rows, D)
    grad_kv_part, grad_x_heads, query_grad, kv_up_grad, out_grad = attend_back(
        grad_attn_low, x_attn, kv_all, places, weights, kept, micro_count, heads_local
    )
    grad_x_heads, shared_grads = lax.optimization_barrier((grad_x_heads, shared_grads))
    shared_grads = lax.all_gather(shared_grads, GROUP, axis=0, tiled=True)
    router_part = router_grad.T.astype(BF16).reshape(1, tensor_size, -1, LANES)
    latent_own = own(latent_raw).reshape(micro_count, own_rows, LATENT)
    turns_own = [
        own(angle).reshape(micro_count, own_rows, ROPE)
        for angle in (
            jnp.tile(cos_query, (1, 2)),
            jnp.concatenate([sin_query, -sin_query], axis=1),
        )
    ]

    def finish_rows(sums, extras, shares, results):
        x_grad, kv_grad, router = sums
        x_own, one, ffn_gain_grad, raw, cosine, sine, gain, latent_gain, down_w = extras
        gain_grad = jnp.zeros((1, D), F32)
        latent_gain_grad = jnp.zeros((1, LATENT), F32)
        for m in range(micro_count):
            inverse = rms_scale(raw[m])
            normed = raw[m] * inverse
            grad = kv_grad[m, :, :LATENT]
            latent_gain_grad = latent_gain_grad + jnp.sum(grad * normed, axis=0, keepdims=True)
            kv_low = jnp.concatenate(
                [
                    norm_back(grad * latent_gain[...], normed, inverse),
                    turn(kv_grad[m, :, LATENT:], cosine[m], sine[m]),
                ],
                axis=1,
            ).astype(BF16)
            x = x_own[m].astype(F32)
            inverse = rms_scale(x)
            normed = x * inverse
            grad = x_grad[m] + mm(kv_low, down_w[...])
            gain_grad = gain_grad + jnp.sum(grad * normed, axis=0, keepdims=True)
            total = one[m] + norm_back(grad * gain[...], normed, inverse)
            shares[0][m, :, :D] = total.astype(BF16)
            shares[0][m, :, D:] = kv_low
        shares[1][0] = router[0].astype(BF16)
        shares[2][0, :, :D] = gain_grad
        shares[2][0, :, D : 2 * D] = ffn_gain_grad[...]
        shares[2][0, :, 2 * D :] = latent_gain_grad

    finished, router_all, small = exchange(
        [
            SumThenShare(
                [
                    to_owner(grad_x_heads),
                    ContextThenLine(
                        grad_kv_part, micro_count, ("context",), "tensor"
                    ),
                    LineScatter(router_part, "tensor"),
                ],
                [
                    tokens_own,
                    grad_one,
                    norm_ffn_grad,
                    latent_own,
                    *turns_own,
                    gain_attn[None],
                    gain_latent[None],
                    w_kv_down.T,
                ],
                finish_rows,
                [
                    jax.ShapeDtypeStruct((micro_count, own_rows, D + LATENT + ROPE), BF16),
                    jax.ShapeDtypeStruct((1,) + router_part.shape[2:], BF16),
                    jax.ShapeDtypeStruct((1, 1, 2 * D + LATENT), F32),
                ],
                [],
            ),
        ],
        8,
        100,
    )
    finished = finished.reshape(rows, -1)
    finished, out_sum = lax.optimization_barrier((finished, out_sum))
    out_sum = out_sum.astype(F32) + shared_out.astype(F32)
    out_sum = out_sum.astype(BF16).reshape(micro_count, tensor_size, own_rows, D)
    out_sum = out_sum.transpose(1, 0, 2, 3)
    out_sum = lax.psum_scatter(out_sum, "tensor", scatter_dimension=0, tiled=False)
    grad_tokens, grad_kv_raw = finished[:, :D], finished[:, D:]
    kv_width = -(-grad_kv_raw.shape[1] // (16 * groups)) * 16 * groups
    grad_kv_raw = jnp.pad(grad_kv_raw, ((0, 0), (0, kv_width - grad_kv_raw.shape[1])))
    kv_down_grad = mm_tn(grad_kv_raw, x_attn).astype(BF16)
    small = jnp.sum(small, axis=(0, 1, 2)).astype(BF16)
    query_grad, kv_up_grad, out_grad, kv_down_grad, router_grad, small = exchange(
        [
            GroupSum(part.reshape(groups, -1, part.shape[-1]), GROUP)
            for part in (
                query_grad,
                kv_up_grad,
                out_grad,
                kv_down_grad,
                router_all.reshape(groups * 16, -1),
                small.reshape(groups * 16, -1),
            )
        ],
        10,
        80,
    )
    query_grad, kv_up_grad, out_grad, kv_down_grad, out_sum, shared_grads, one = (
        lax.optimization_barrier(
            (query_grad, kv_up_grad, out_grad, kv_down_grad, out_sum, shared_grads, F32(1.0))
        )
    )
    output = (hidden_one + out_sum.astype(F32)).astype(BF16)
    output = lax.all_gather(output, "tensor", axis=0)
    output = output.transpose(1, 0, 2, 3)
    kv_down_grad = kv_down_grad.reshape(-1, D)[: LATENT + ROPE].astype(F32).T
    router_grad = router_grad.reshape(D, experts).astype(F32)
    small = small.reshape(-1).astype(F32)
    gate_grad, up_grad, down_grad = gate_grad * one, up_grad * one, down_grad * one
    return (
        output.reshape(tokens.shape),
        grad_tokens.reshape(tokens.shape),
        small[:D],
        flat(query_grad).reshape(D, -1).astype(F32),
        kv_down_grad,
        small[D + D :],
        kv_up_grad.reshape(LATENT, -1).astype(F32),
        out_grad.reshape(-1, D).astype(F32),
        small[D : D + D],
        router_grad,
        shared_grads[:ff_local].astype(F32).T,
        shared_grads[shared_units : shared_units + ff_local].astype(F32).T,
        shared_grads[2 * shared_units : 2 * shared_units + ff_local].astype(F32),
        gate_grad.transpose(0, 2, 1),
        up_grad.transpose(0, 2, 1),
        down_grad,
    )


def solution(mesh):
    return jax.shard_map(
        per_device,
        mesh=mesh,
        in_specs=(
            P("dp", "context", None),
            P("dp", None),
            P("dp", "context", None),
            P(),
            P(None, "tensor"),
            P(),
            P(),
            P(None, "tensor"),
            P("tensor", None),
            P(),
            P(),
            P(None, "tensor"),
            P(None, "tensor"),
            P("tensor", None),
            P(("dp", "context"), None, "tensor"),
            P(("dp", "context"), None, "tensor"),
            P(("dp", "context"), "tensor", None),
            P("dp", "context", None),
        ),
        out_specs=(
            P("dp", "context", None),
            P("dp", "context", None),
            P(),
            P(None, "tensor"),
            P(),
            P(),
            P(None, "tensor"),
            P("tensor", None),
            P(),
            P(),
            P(None, "tensor"),
            P(None, "tensor"),
            P("tensor", None),
            P(("dp", "context"), None, "tensor"),
            P(("dp", "context"), None, "tensor"),
            P(("dp", "context"), "tensor", None),
        ),
        check_vma=False,
    )
```

```python
import functools

import jax
import jax.numpy as jnp
from jax import lax
from jax.experimental import pallas as pl
from jax.experimental.pallas import tpu as pltpu
from jax.sharding import PartitionSpec as P

D = 2048
NOPE = 128
ROPE = 64
VDIM = 128
LATENT = 512
TOP = 6
EXP_DEV = 2
LANES = 128
GROUP = ("dp", "context")
EVERY = ("dp", "context", "tensor")
BF16 = jnp.bfloat16
F32 = jnp.float32
MESH = pl.DeviceIdType.MESH
MIB = 1024 * 1024

EPS = 1e-06


def rms_scale(rows):
    return lax.rsqrt(jnp.mean(rows * rows, axis=-1, keepdims=True) + EPS)


def norm_back(grad_out, normed, inverse):
    return inverse * (grad_out - normed * jnp.mean(grad_out * normed, axis=-1, keepdims=True))


def angles(positions, rope_dim):
    frequency = 10000.0 ** (-(jnp.arange(rope_dim // 2).astype(jnp.float32) * 2.0) / rope_dim)
    turned = positions[:, None] * frequency[None, :]
    return (jnp.cos(turned), jnp.sin(turned))


def rotate(vectors, cosine, sine):
    half_dim = vectors.shape[-1] // 2
    front_part = vectors[..., :half_dim]
    back_part = vectors[..., half_dim:]
    return jnp.concatenate(
        [front_part * cosine - back_part * sine, front_part * sine + back_part * cosine], axis=-1
    )


def unrotate(vectors, cosine, sine):
    half_dim = vectors.shape[-1] // 2
    front_part = vectors[..., :half_dim]
    back_part = vectors[..., half_dim:]
    return jnp.concatenate(
        [front_part * cosine + back_part * sine, back_part * cosine - front_part * sine], axis=-1
    )


def mm(left, right):
    return jnp.dot(left, right, preferred_element_type=F32)


def mm_nt(left, right):
    return lax.dot_general(left, right, (((1,), (1,)), ((), ())), preferred_element_type=F32)


def mm_tn(left, right):
    return lax.dot_general(left, right, (((0,), (0,)), ((), ())), preferred_element_type=F32)


def ring(axes, sizes):
    place = 0
    total = 1
    for axis, size in zip(axes, sizes):
        place = place * size + lax.axis_index(axis)
        total *= size

    def coordinates(index):
        found = {}
        for axis, size in reversed(list(zip(axes, sizes))):
            found[axis] = lax.rem(index, size)
            index = lax.div(index, size)
        return found

    return place, total, coordinates


def meet(devices):
    barrier = pltpu.get_barrier_semaphore()
    for device in devices:
        pl.semaphore_signal(barrier, inc=1, device_id=device, device_id_type=MESH)
    pl.semaphore_wait(barrier, len(devices))


def flip(index, mask, bits):
    total = 0
    for bit in range(bits):
        weight = 1 << bit
        ours = lax.rem(lax.div(index, weight), 2)
        theirs = lax.rem(lax.div(mask, weight), 2)
        total = total + lax.rem(ours + theirs, 2) * weight
    return total


def group_layout(axes, sizes):
    place, _, coordinates = ring(axes, sizes)
    return lax.div(place, 2), lax.rem(place, 2), lambda chip, core: coordinates(chip * 2 + core)


def group_sizes(axes):
    sizes = tuple(lax.axis_size(axis) for axis in axes)
    pairs = 1
    for size in sizes:
        pairs *= size
    return sizes, pairs // 2


def add_rows(out, terms, rows):
    def add(index, carry):
        at = pl.ds(pl.multiple_of(index * 16, 16), 16)
        value = terms[0](at).astype(F32)
        for term in terms[1:]:
            value = value + term(at).astype(F32)
        out(at, value)
        return carry

    lax.fori_loop(0, rows // 16, add, 0)


class LineGather:
    def __init__(self, v, axis):
        self.axis, self.size = axis, lax.axis_size(axis)
        dma = pltpu.SemaphoreType.DMA
        self.inputs = [(v, pltpu.VMEM)]
        shape = (v.shape[0], self.size) + v.shape[1:]
        self.outputs = [(jax.ShapeDtypeStruct(shape, v.dtype), pl.ANY)]
        self.scratch = [dma((2, self.size)), dma((2, self.size)), dma]

    def greets(self):
        index = lax.axis_index(self.axis)
        return [
            {self.axis: lax.rem(index + step, self.size)} for step in (1, self.size - 1)
        ]

    def run(self, v_ref, out_ref, send_sem, recv_sem, own_sem):
        index, size = lax.axis_index(self.axis), self.size

        def copy(way, hop, first):
            step = 1 - 2 * way
            source = lax.rem(index - step * (hop - 1) + size, size)
            return pltpu.make_async_remote_copy(
                src_ref=v_ref if first else out_ref.at[:, source],
                dst_ref=out_ref.at[:, source],
                send_sem=send_sem.at[way, hop],
                recv_sem=recv_sem.at[way, hop],
                device_id={self.axis: lax.rem(index + step + size, size)},
                device_id_type=MESH,
            )

        def arrival(way, hop):
            step = 1 - 2 * way
            source = lax.rem(index - step * hop + size, size)
            return pltpu.make_async_remote_copy(
                src_ref=v_ref,
                dst_ref=out_ref.at[:, source],
                send_sem=send_sem.at[way, hop],
                recv_sem=recv_sem.at[way, hop],
                device_id={self.axis: lax.rem(index + step + size, size)},
                device_id_type=MESH,
            )

        def sends(way, hop):
            if way == 0:
                return (index + 1 < size) & (index - hop + 1 >= 0)
            return (index - 1 >= 0) & (index + hop - 1 < size)

        def receives(way, hop):
            return index - hop >= 0 if way == 0 else index + hop < size

        for way in range(2):

            @pl.when(sends(way, 1))
            def _():
                copy(way, 1, True).start()

        own = pltpu.make_async_copy(v_ref, out_ref.at[:, index], own_sem)
        own.start()
        yield
        for hop in range(1, size):
            for way in range(2):

                @pl.when(receives(way, hop))
                def _():
                    arrival(way, hop).wait_recv()

                if hop + 1 < size:

                    @pl.when(sends(way, hop + 1))
                    def _():
                        copy(way, hop + 1, False).start()

            yield
        own.wait()
        for hop in range(1, size):
            for way in range(2):

                @pl.when(sends(way, hop))
                def _():
                    copy(way, hop, hop == 1).wait_send()


class LineScatter:
    def __init__(self, v, axis):
        self.axis, self.size = axis, lax.axis_size(axis)
        lead, total, rows, width = v.shape
        self.lead, self.rows = lead, rows
        if not isinstance(v, jax.ShapeDtypeStruct):
            v = v.reshape(lead, total * rows, width)
        dma = pltpu.SemaphoreType.DMA
        self.inputs = [(v, pltpu.VMEM)]
        self.outputs = [(jax.ShapeDtypeStruct((lead, rows, width), F32), pltpu.VMEM)]
        self.scratch = [
            pltpu.VMEM((2, total, lead, rows, width), v.dtype),
            dma((2, total)),
            dma((2, total)),
        ]

    greets = LineGather.greets

    def run(self, v_ref, out_ref, held, send_sem, recv_sem):
        index, size, rows = lax.axis_index(self.axis), self.size, self.rows

        def block(target):
            return pl.ds(pl.multiple_of(target * rows, rows), rows)

        def ours(lead, target):
            return lambda at: v_ref[
                lead, pl.ds(pl.multiple_of(target * rows + at.start, 16), 16), :
            ]

        def copy(way, target, first):
            step = 1 - 2 * way
            return pltpu.make_async_remote_copy(
                src_ref=v_ref.at[:, block(target)] if first else held.at[way, target],
                dst_ref=held.at[way, target],
                send_sem=send_sem.at[way, target],
                recv_sem=recv_sem.at[way, target],
                device_id={self.axis: lax.rem(index + step + size, size)},
                device_id_type=MESH,
            )

        def start(way):
            return index == 0 if way == 0 else index == size - 1

        def between(way, target):
            return (index > 0) & (index < target) if way == 0 else (index < size - 1) & (index > target)

        def targets(way):
            return range(size - 1, 0, -1) if way == 0 else range(size - 1)

        for way in range(2):

            @pl.when(start(way))
            def _():
                copy(way, targets(way)[0], True).start()

        yield
        def hand_on(way, position):
            target = targets(way)[position]
            if position + 1 < size - 1:

                @pl.when(start(way))
                def _():
                    copy(way, target, True).wait_send()
                    copy(way, targets(way)[position + 1], True).start()

            @pl.when(between(way, target))
            def _():
                copy(way, target, False).wait_recv()
                for lead in range(self.lead):

                    def store(at, value):
                        held[way, target, lead, at, :] = value.astype(BF16)

                    add_rows(
                        store,
                        [
                            lambda at: held[way, target, lead, at, :],
                            ours(lead, target),
                        ],
                        self.rows,
                    )
                copy(way, target, False).start()

        for position in range(size - 1):
            @pl.when(index < size // 2)
            def _():
                hand_on(0, position)
                hand_on(1, position)

            @pl.when(index >= size // 2)
            def _():
                hand_on(1, position)
                hand_on(0, position)

            yield
        for way in range(2):

            @pl.when(jnp.logical_not(start(way)))
            def _():
                copy(way, index, False).wait_recv()

        for lead in range(self.lead):

            def store(at, value, lead=lead):
                out_ref[lead, at, :] = value

            own = [ours(lead, index)]
            right = [lambda at, lead=lead: held[0, index, lead, at, :]]
            left = [lambda at, lead=lead: held[1, index, lead, at, :]]

            @pl.when(index == 0)
            def _():
                add_rows(store, own + left, self.rows)

            @pl.when(index == size - 1)
            def _():
                add_rows(store, own + right, self.rows)

            @pl.when((index > 0) & (index < size - 1))
            def _():
                add_rows(store, own + right + left, self.rows)

        for way in range(2):

            @pl.when(start(way))
            def _():
                copy(way, targets(way)[size - 2], True).wait_send()

            for target in targets(way):

                @pl.when(between(way, target))
                def _():
                    copy(way, target, False).wait_send()


class LineScatterSum(LineScatter):
    def __init__(self, parts, one, axis):
        lead, self.count, all_rows, width = parts.shape
        total = lax.axis_size(axis)
        self.all_rows = all_rows
        super().__init__(
            jax.ShapeDtypeStruct((lead, total, all_rows // total, width), BF16), axis
        )
        self.inputs = [(parts, pltpu.VMEM), (one, pltpu.VMEM)]
        self.scratch = [pltpu.VMEM((lead, all_rows, width), BF16)] + self.scratch

    def run(self, parts_ref, one_ref, out_ref, summed, *refs):
        for lead in range(self.lead):

            def store(at, value, lead=lead):
                summed[lead, at, :] = value.astype(BF16)

            terms = [lambda at, lead=lead: one_ref[lead, at, :]]
            for number in range(self.count):
                terms.append(lambda at, lead=lead, number=number: parts_ref[lead, number, at, :])
            add_rows(store, terms, self.all_rows)
        yield from super().run(summed, out_ref, *refs)


class GroupScatter:
    def __init__(self, v, axes, pick=None):
        self.axes, self.pick = axes, pick
        self.sizes, self.pairs = group_sizes(axes)
        tail = v.shape[1:] if pick is None else v.shape[2:]
        self.across = self.pairs == 4 and tail[0] % 32 == 0
        v = v.reshape((self.pairs, 2) + v.shape[1:])
        self.rows = tail[0]
        dma = pltpu.SemaphoreType.DMA
        self.inputs = [(v, pl.ANY)]
        self.outputs = [(jax.ShapeDtypeStruct(tail, BF16), pltpu.VMEM)]
        self.scratch = [pltpu.VMEM((self.pairs,) + tail, BF16)] * 4 + [
            pltpu.VMEM((2, tail[0] // 2 if self.across else 16) + tail[1:], BF16),
            dma,
            dma,
            dma,
            dma((self.pairs,)),
            dma((self.pairs,)),
            dma((2,)),
            dma((2,)),
        ]

    def greets(self):
        chip, core, device = group_layout(self.axes, self.sizes)
        bits = self.pairs.bit_length() - 1
        return [device(chip, 1 - core)] + [
            device(flip(chip, mask, bits), core) for mask in range(1, self.pairs)
        ]

    def run(
        self,
        v_ref,
        out_ref,
        mine,
        peer,
        summed,
        held,
        passed,
        load_sem,
        swap_send,
        swap_recv,
        sum_send,
        sum_recv,
        pass_send,
        pass_recv,
    ):
        pairs, rows = self.pairs, self.rows
        bits = pairs.bit_length() - 1
        chip, core, device = group_layout(self.axes, self.sizes)

        def side(which):
            if self.pick is None:
                return v_ref.at[:, which]
            return v_ref.at[:, which, self.pick]

        swap = pltpu.make_async_remote_copy(
            src_ref=side(1 - core),
            dst_ref=peer,
            send_sem=swap_send,
            recv_sem=swap_recv,
            device_id=device(chip, 1 - core),
            device_id_type=MESH,
        )
        swap.start()
        load = pltpu.make_async_copy(side(core), mine, load_sem)
        load.start()
        yield

        def push(mask):
            return pltpu.make_async_remote_copy(
                src_ref=summed.at[mask],
                dst_ref=held.at[mask],
                send_sem=sum_send.at[mask],
                recv_sem=sum_recv.at[mask],
                device_id=device(flip(chip, mask, bits), core),
                device_id_type=MESH,
            )

        middle = rows // 2
        halves = (pl.ds(0, middle), pl.ds(middle, rows - middle))

        def pass_on(part):
            return pltpu.make_async_remote_copy(
                src_ref=summed.at[3, halves[part]],
                dst_ref=passed.at[part],
                send_sem=pass_send.at[part],
                recv_sem=pass_recv.at[part],
                device_id=device(flip(chip, part + 1, bits), core),
                device_id_type=MESH,
            )

        load.wait()
        swap.wait()
        for mask in range(pairs - 1, -1, -1):
            target = flip(chip, mask, bits)

            def store(at, value, mask=mask):
                summed[mask, at, :] = value.astype(BF16)

            add_rows(
                store,
                [
                    lambda at, target=target: mine[target, at, :],
                    lambda at, target=target: peer[target, at, :],
                ],
                rows,
            )
            if self.across and mask == 3:
                for part in range(2):
                    pass_on(part).start()
            if not self.across and mask:
                push(mask).start()
        yield
        direct = (1, 2) if self.across else range(1, pairs)
        if self.across:
            for part in range(2):
                pass_on(part).wait_recv()
                mask = 2 - part
                start = part * middle

                def store(at, value, mask=mask, start=start):
                    summed[mask, pl.ds(pl.multiple_of(start + at.start, 16), 16), :] = value.astype(
                        BF16
                    )

                add_rows(
                    store,
                    [
                        lambda at, mask=mask, start=start: summed[
                            mask, pl.ds(pl.multiple_of(start + at.start, 16), 16), :
                        ],
                        lambda at, part=part: passed[part, at, :],
                    ],
                    middle,
                )
                push(mask).start()
        yield
        for mask in direct:
            push(mask).wait_recv()

        def finish(at, value):
            out_ref[at, :] = value.astype(BF16)

        add_rows(
            finish,
            [lambda at: summed[0, at, :]]
            + [lambda at, mask=mask: held[mask, at, :] for mask in direct],
            rows,
        )
        yield
        for mask in direct:
            push(mask).wait_send()
        if self.across:
            for part in range(2):
                pass_on(part).wait_send()


class GroupGather:
    def __init__(self, v, axes):
        self.axes = axes
        self.sizes, self.pairs = group_sizes(axes)
        self.rows = v.shape[0]
        self.across = self.pairs == 4 and v.shape[0] % 32 == 0
        dma = pltpu.SemaphoreType.DMA
        self.inputs = [(v, pltpu.VMEM)]
        self.outputs = [(jax.ShapeDtypeStruct((self.pairs, 2) + v.shape, v.dtype), pl.ANY)]
        self.scratch = [dma] + [dma((self.pairs,))] * 4 + [dma((2,))] * 2

    greets = GroupScatter.greets

    def run(
        self,
        v_ref,
        out_ref,
        own_sem,
        push_send,
        push_recv,
        relay_send,
        relay_recv,
        pass_send,
        pass_recv,
    ):
        pairs, rows = self.pairs, self.rows
        bits = pairs.bit_length() - 1
        chip, core, device = group_layout(self.axes, self.sizes)
        middle = rows // 2
        halves = (pl.ds(0, middle), pl.ds(middle, rows - middle))

        def push(mask, source):
            return pltpu.make_async_remote_copy(
                src_ref=v_ref,
                dst_ref=out_ref.at[source, core],
                send_sem=push_send.at[mask],
                recv_sem=push_recv.at[mask],
                device_id=device(flip(chip, mask, bits), core),
                device_id_type=MESH,
            )

        def pass_on(mask, source, part):
            return pltpu.make_async_remote_copy(
                src_ref=out_ref.at[source, core, halves[part]],
                dst_ref=out_ref.at[source, core, halves[part]],
                send_sem=pass_send.at[part],
                recv_sem=pass_recv.at[part],
                device_id=device(flip(chip, mask, bits), core),
                device_id_type=MESH,
            )

        def relay(mask, side):
            source = flip(chip, mask, bits)
            return pltpu.make_async_remote_copy(
                src_ref=v_ref if mask == 0 else out_ref.at[source, side],
                dst_ref=out_ref.at[source, side],
                send_sem=relay_send.at[mask],
                recv_sem=relay_recv.at[mask],
                device_id=device(chip, 1 - core),
                device_id_type=MESH,
            )

        direct = (1, 2) if self.across else tuple(range(1, pairs))
        for mask in direct:
            push(mask, chip).start()
        relay(0, core).start()
        own = pltpu.make_async_copy(v_ref, out_ref.at[chip, core], own_sem)
        own.start()
        yield
        for mask in direct:
            push(mask, flip(chip, mask, bits)).wait_recv()
            if self.across:
                pass_on(3 - mask, flip(chip, mask, bits), mask - 1).start()
            relay(mask, core).start()
        yield
        if self.across:
            for part in range(2):
                pass_on(part + 1, flip(chip, 3, bits), part).wait_recv()
            relay(3, core).start()
        own.wait()
        yield
        for mask in range(pairs):
            relay(mask, 1 - core).wait_recv()
        for mask in range(pairs):
            relay(mask, core).wait_send()
            if mask in direct:
                push(mask, chip).wait_send()
                if self.across:
                    pass_on(3 - mask, flip(chip, mask, bits), mask - 1).wait_send()


class ContextThenLine:
    def __init__(self, value, count, axes, axis):
        self.first = [GroupScatter(value, axes, pick=number) for number in range(count)]
        rows, width = value.shape[2:]
        total = lax.axis_size(axis)
        self.second = LineScatter(
            jax.ShapeDtypeStruct((count, total, rows // total, width), BF16), axis
        )
        self.inputs = [entry for job in self.first for entry in job.inputs]
        self.outputs = self.second.outputs
        self.scratch = [pltpu.VMEM((count, rows, width), BF16)]
        self.scratch += [entry for job in self.first for entry in job.scratch]
        self.scratch += self.second.scratch

    def greets(self):
        return [device for job in self.first + [self.second] for device in job.greets()]

    def run(self, *refs):
        refs = list(refs)
        count = len(self.first)
        inputs, out_ref, between, refs = refs[:count], refs[count], refs[count + 1], refs[count + 2 :]
        steps = []
        for number, job in enumerate(self.first):
            used = len(job.scratch)
            steps.append(job.run(inputs[number], between.at[number], *refs[:used]))
            refs = refs[used:]
        for _ in zip(*steps):
            yield
        for step in steps:
            for _ in step:
                pass
        yield from self.second.run(between, out_ref, *refs)


class SumThenShare:
    def __init__(self, parts, extras, finish, shares, results):
        self.parts, self.finish = parts, finish
        self.gathers = [LineGather(share, "tensor") for share in shares]
        self.counts = (len(extras), len(results))
        self.inputs = [entry for job in parts for entry in job.inputs]
        self.inputs += [(extra, pltpu.VMEM) for extra in extras]
        self.outputs = [entry for job in self.gathers for entry in job.outputs]
        self.outputs += [(result, pltpu.VMEM) for result in results]
        self.scratch = [pltpu.VMEM(shape.shape, shape.dtype) for job in parts for shape, _ in job.outputs]
        self.scratch += [pltpu.VMEM(share.shape, share.dtype) for share in shares]
        for job in parts + self.gathers:
            self.scratch += job.scratch

    def greets(self):
        return [device for job in self.parts + self.gathers[:1] for device in job.greets()]

    def run(self, *refs):
        refs = list(refs)

        def take(count):
            taken = refs[:count]
            del refs[:count]
            return taken

        part_inputs = [take(len(job.inputs)) for job in self.parts]
        extras = take(self.counts[0])
        outputs = take(len(self.gathers))
        results = take(self.counts[1])
        sums = take(len(self.parts))
        shares = take(len(self.gathers))
        running = [
            job.run(*inputs, total, *take(len(job.scratch)))
            for job, inputs, total in zip(self.parts, part_inputs, sums)
        ]
        gathers = [
            job.run(share, output, *take(len(job.scratch)))
            for job, share, output in zip(self.gathers, shares, outputs)
        ]
        yield from side_by_side(running)
        self.finish(sums, extras, shares, results)
        yield from side_by_side(gathers)


def side_by_side(running):
    while running:
        left = []
        for step in running:
            try:
                next(step)
                left.append(step)
            except StopIteration:
                pass
        running = left
        yield


class GroupSum:
    def __init__(self, v, axes):
        self.first = GroupScatter(v, axes)
        self.second = GroupGather(jax.ShapeDtypeStruct(v.shape[1:], BF16), axes)
        self.inputs, self.outputs = self.first.inputs, self.second.outputs
        self.scratch = [pltpu.VMEM(v.shape[1:], BF16)] + self.first.scratch + self.second.scratch
        self.greets = self.first.greets

    def run(self, v_ref, out_ref, between, *refs):
        used = len(self.first.scratch)
        yield from self.first.run(v_ref, between, *refs[:used])
        yield from self.second.run(between, out_ref, *refs[used:])


def exchange_kernel(jobs, *refs):
    refs = list(refs)
    taken = [[], [], []]
    for number, part in enumerate(("inputs", "outputs", "scratch")):
        for job in jobs:
            count = len(getattr(job, part))
            taken[number].append(refs[:count])
            refs = refs[count:]
    meet([device for job in jobs for device in job.greets()])
    running = [
        job.run(*taken[0][at], *taken[1][at], *taken[2][at]) for at, job in enumerate(jobs)
    ]
    for _ in side_by_side(running):
        pass


def exchange(jobs, collective_id, micros):
    inputs = [entry for job in jobs for entry in job.inputs]
    outputs = [entry for job in jobs for entry in job.outputs]
    return pl.pallas_call(
        functools.partial(exchange_kernel, jobs),
        out_shape=tuple(shape for shape, _ in outputs),
        in_specs=[pl.BlockSpec(memory_space=space) for _, space in inputs],
        out_specs=tuple(pl.BlockSpec(memory_space=space) for _, space in outputs),
        scratch_shapes=[entry for job in jobs for entry in job.scratch],
        compiler_params=pltpu.CompilerParams(
            collective_id=collective_id, has_side_effects=True, vmem_limit_bytes=56 * MIB
        ),
        cost_estimate=pl.CostEstimate(
            flops=0, bytes_accessed=360_000 * micros, transcendentals=0
        ),
        name="exchange_" + "_".join(type(job).__name__ for job in jobs[:3]),
    )(*[value for value, _ in inputs])


KV_WIDTH = 640


def turn(vectors, cosine, sine):
    half_dim = vectors.shape[-1] // 2
    swapped = jnp.concatenate([vectors[:, half_dim:], vectors[:, :half_dim]], axis=1)
    return vectors * cosine + swapped * sine


def head_scores(query, key_nope, key_rope, allowed):
    raw = mm_nt(query[:, :NOPE], key_nope) + mm_nt(query[:, NOPE:], key_rope)
    return jnp.where(allowed, raw * (NOPE + ROPE) ** (-0.5), -1e30)


def allowed_keys(row_ref, column_ref, row_place_ref, column_place_ref):
    return (row_ref[0] == column_ref[0]) & (column_place_ref[...] <= row_place_ref[...])


def attend_kernel(
    x_ref,
    kv_ref,
    row_ref,
    column_ref,
    row_place_ref,
    column_place_ref,
    cos_ref,
    sin_ref,
    query_w,
    up_w,
    out_w,
    part_ref,
    attended_ref,
    query_ref,
    expanded_ref,
    log_ref,
):
    heads = query_w.shape[1] // (NOPE + ROPE)
    allowed = allowed_keys(row_ref, column_ref, row_place_ref, column_place_ref)
    latent = kv_ref[:, :LATENT]
    key_rope = kv_ref[:, LATENT : LATENT + ROPE]
    query = mm(x_ref[...], query_w[...])
    for head in range(heads):
        start = head * (NOPE + ROPE)
        rope = turn(query[:, start + NOPE : start + NOPE + ROPE], cos_ref[...], sin_ref[...])
        query_ref[0, head, :, :NOPE] = query[:, start : start + NOPE].astype(BF16)
        query_ref[0, head, :, NOPE:] = rope.astype(BF16)
        at = slice(head * (NOPE + VDIM), (head + 1) * (NOPE + VDIM))
        expanded_ref[0, :, at] = mm(latent, up_w[:, at]).astype(BF16)
        key_nope = expanded_ref[0, :, at.start : at.start + NOPE]
        values = expanded_ref[0, :, at.start + NOPE : at.stop]
        scores = head_scores(query_ref[0, head], key_nope, key_rope, allowed)
        top = jnp.max(scores, axis=-1, keepdims=True)
        weights = jnp.where(allowed, jnp.exp(scores - top), 0.0)
        total = jnp.sum(weights, axis=-1, keepdims=True)
        log_ref[0, head] = top + jnp.log(total)
        probs = (weights / total).astype(BF16)
        attended_ref[:, head * VDIM : (head + 1) * VDIM] = mm(probs, values).astype(BF16)
    part_ref[...] = mm(attended_ref[...], out_w[...]).astype(BF16)


def attend_back_kernel(
    grad_ref,
    attended_ref,
    x_ref,
    kv_ref,
    row_ref,
    column_ref,
    row_place_ref,
    column_place_ref,
    cos_ref,
    sin_ref,
    query_ref,
    expanded_ref,
    log_ref,
    query_w,
    up_w,
    out_w,
    kv_grad_ref,
    x_grad_ref,
    query_w_ref,
    up_w_ref,
    out_w_ref,
    query_grad,
    expanded_grad,
    query_w_sum,
    up_w_sum,
    out_w_sum,
):
    heads = query_w.shape[1] // (NOPE + ROPE)
    scale = (NOPE + ROPE) ** (-0.5)
    allowed = allowed_keys(row_ref, column_ref, row_place_ref, column_place_ref)
    latent = kv_ref[:, :LATENT]
    key_rope = kv_ref[:, LATENT : LATENT + ROPE]
    grad = grad_ref[...]
    attended_grad = mm_nt(grad, out_w[...]).astype(BF16)
    rope_grad = jnp.zeros((kv_ref.shape[0], ROPE), F32)
    for head in range(heads):
        first = head * (NOPE + VDIM)
        key_nope = expanded_ref[0, :, first : first + NOPE]
        values = expanded_ref[0, :, first + NOPE : first + NOPE + VDIM]
        query = query_ref[0, head]
        scores = head_scores(query, key_nope, key_rope, allowed)
        probs = jnp.where(allowed, jnp.exp(scores - log_ref[0, head]), 0.0)
        own_grad = attended_grad[:, head * VDIM : (head + 1) * VDIM]
        probs_grad = mm_nt(own_grad, values)
        moved = probs * (probs_grad - jnp.sum(probs * probs_grad, axis=-1, keepdims=True))
        moved = moved.astype(BF16)
        expanded_grad[:, first : first + NOPE] = (
            scale * mm_tn(moved, query[:, :NOPE])
        ).astype(BF16)
        expanded_grad[:, first + NOPE : first + NOPE + VDIM] = mm_tn(
            probs.astype(BF16), own_grad
        ).astype(BF16)
        rope_grad = rope_grad + mm_tn(moved, query[:, NOPE:])
        start = head * (NOPE + ROPE)
        query_grad[:, start : start + NOPE] = (scale * mm(moved, key_nope)).astype(BF16)
        query_grad[:, start + NOPE : start + NOPE + ROPE] = turn(
            scale * mm(moved, key_rope), cos_ref[...], -sin_ref[...]
        ).astype(BF16)
    latent_grad = mm_nt(expanded_grad[...], up_w[...]).astype(BF16)
    rope_grad = (scale * rope_grad).astype(BF16)
    rows = x_ref.shape[0]
    for block in range(kv_grad_ref.shape[0]):
        at = slice(block * rows, (block + 1) * rows)
        kv_grad_ref[block, 0, :, :LATENT] = latent_grad[at]
        kv_grad_ref[block, 0, :, LATENT:] = rope_grad[at]
    x_grad_ref[...] = mm_nt(query_grad[...], query_w[...]).astype(BF16)
    pieces = (
        (query_w_sum, query_w_ref, x_ref[...], query_grad[...]),
        (up_w_sum, up_w_ref, latent, expanded_grad[...]),
        (out_w_sum, out_w_ref, attended_ref[...], grad),
    )
    step = pl.program_id(0)

    @pl.when(step == 0)
    def _():
        for total, _, left, right in pieces:
            total[...] = mm_tn(left, right)

    @pl.when(step > 0)
    def _():
        for total, _, left, right in pieces:
            total[...] += mm_tn(left, right)

    @pl.when(step == pl.num_programs(0) - 1)
    def _():
        for total, target, _, _ in pieces:
            target[...] = total[...].astype(BF16)


def attention_specs(micro_count, rows, seq_len, heads):
    per_micro = lambda *shape: pl.BlockSpec((1,) + shape, lambda m: (m,) + (0,) * len(shape))
    rows_of = lambda width: pl.BlockSpec((rows, width), lambda m: (m, 0))
    whole = lambda *shape: pl.BlockSpec(
        shape, lambda m: (0,) * len(shape), pipeline_mode=pl.Buffered(1)
    )
    places = [
        per_micro(rows, 1),
        per_micro(1, seq_len),
        whole(rows, 1),
        whole(1, seq_len),
        whole(rows, ROPE),
        whole(rows, ROPE),
    ]
    weights = [
        whole(D, heads * (NOPE + ROPE)),
        whole(LATENT, heads * (NOPE + VDIM)),
        whole(heads * VDIM, D),
    ]
    kept = [
        rows_of(heads * VDIM),
        per_micro(heads, rows, NOPE + ROPE),
        per_micro(seq_len, heads * (NOPE + VDIM)),
        per_micro(heads, rows, 1),
    ]
    return per_micro, rows_of, whole, places, weights, kept


def kv_spec(seq_len):
    return pl.BlockSpec((seq_len, KV_WIDTH), lambda m: (0, m))


def attend(x_attn, kv_all, places, weights, micro_count, heads):
    rows, seq_len = x_attn.shape[0] // micro_count, kv_all.shape[0]
    per_micro, rows_of, _, place_specs, weight_specs, kept = attention_specs(
        micro_count, rows, seq_len, heads
    )
    total = micro_count * rows
    return pl.pallas_call(
        attend_kernel,
        grid=(micro_count,),
        in_specs=[rows_of(D), kv_spec(seq_len)] + place_specs + weight_specs,
        out_specs=[rows_of(D)] + kept,
        out_shape=[
            jax.ShapeDtypeStruct((total, D), BF16),
            jax.ShapeDtypeStruct((total, heads * VDIM), BF16),
            jax.ShapeDtypeStruct((micro_count, heads, rows, NOPE + ROPE), BF16),
            jax.ShapeDtypeStruct((micro_count, seq_len, heads * (NOPE + VDIM)), BF16),
            jax.ShapeDtypeStruct((micro_count, heads, rows, 1), F32),
        ],
        compiler_params=pltpu.CompilerParams(vmem_limit_bytes=56 * MIB),
        cost_estimate=pl.CostEstimate(
            flops=9_000_000_000, bytes_accessed=60_000_000, transcendentals=0
        ),
        name="attend",
    )(x_attn, kv_all, *places, *weights)


def attend_back(grad, x_attn, kv_all, places, weights, kept, micro_count, heads):
    rows, seq_len = x_attn.shape[0] // micro_count, kv_all.shape[0]
    per_micro, rows_of, whole, place_specs, weight_specs, kept_specs = attention_specs(
        micro_count, rows, seq_len, heads
    )
    total = micro_count * rows
    return pl.pallas_call(
        attend_back_kernel,
        grid=(micro_count,),
        in_specs=[rows_of(D), kept_specs[0], rows_of(D), kv_spec(seq_len)]
        + place_specs
        + kept_specs[1:]
        + weight_specs,
        out_specs=[
            pl.BlockSpec((seq_len // rows, 1, rows, LATENT + ROPE), lambda m: (0, m, 0, 0)),
            rows_of(D),
        ]
        + weight_specs,
        out_shape=[
            jax.ShapeDtypeStruct((seq_len // rows, micro_count, rows, LATENT + ROPE), BF16),
            jax.ShapeDtypeStruct((total, D), BF16),
            jax.ShapeDtypeStruct(weights[0].shape, BF16),
            jax.ShapeDtypeStruct(weights[1].shape, BF16),
            jax.ShapeDtypeStruct(weights[2].shape, BF16),
        ],
        scratch_shapes=[
            pltpu.VMEM((rows, heads * (NOPE + ROPE)), BF16),
            pltpu.VMEM((seq_len, heads * (NOPE + VDIM)), BF16),
            pltpu.VMEM(weights[0].shape, F32),
            pltpu.VMEM(weights[1].shape, F32),
            pltpu.VMEM(weights[2].shape, F32),
        ],
        compiler_params=pltpu.CompilerParams(vmem_limit_bytes=60 * MIB),
        cost_estimate=pl.CostEstimate(
            flops=2_000_000_000, bytes_accessed=10_000_000, transcendentals=0
        ),
        name="attend_back",
    )(grad, kept[0], x_attn, kv_all, *places, *kept[1:], *weights)


PEER_SLOTS = 4


def expert_kernel(
    pairs,
    context_size,
    fe,
    x_ref,
    cot_ref,
    gate_in,
    up_in,
    down_in,
    router_in,
    shared_gate_in,
    shared_up_in,
    shared_down_in,
    out_ref,
    part_ref,
    gate_out,
    up_out,
    down_out,
    router_out,
    shared_out,
    shared_part,
    shared_grads,
    x_all,
    gate_ref,
    up_ref,
    down_ref,
    x_tile,
    cot_tile,
    out_tile,
    grad_tile,
    peer_tile,
    grad_gate,
    grad_up,
    hidden_low,
    gate_acc,
    up_acc,
    down_acc,
    x_send,
    x_recv,
    relay_send,
    relay_recv,
    pass_send,
    pass_recv,
    x_load,
    cot_load,
    out_store,
    swap_send,
    swap_recv,
    sum_send,
    sum_recv,
    weight_load,
    grad_store,
    shared_store,
    acc_store,
    credit,
):
    micro_count, rows = x_ref.shape[0], x_ref.shape[1]
    units = gate_ref.shape[0]
    shared_units = shared_gate_in.shape[0]
    half = units // EXP_DEV
    experts = 2 * pairs * EXP_DEV
    bits = pairs.bit_length() - 1
    steps = micro_count * pairs
    across = pairs == 4
    place = lax.axis_index("dp") * context_size + lax.axis_index("context")
    core = lax.rem(place, 2)
    chip = lax.div(place, 2)

    def device(chip_index, core_index):
        index = chip_index * 2 + core_index
        return {"dp": lax.div(index, context_size), "context": lax.rem(index, context_size)}

    sibling = device(chip, 1 - core)
    meet([sibling] + [device(flip(chip, mask, bits), core) for mask in range(1, pairs)])

    def step_of(step):
        micro = lax.div(step, pairs)
        turn = lax.rem(step, pairs)
        backward = lax.rem(micro, 2)
        return micro, lax.rem(turn + backward, pairs)

    def push_x(micro, mask):
        return pltpu.make_async_remote_copy(
            src_ref=x_ref.at[micro],
            dst_ref=x_all.at[micro, chip, core],
            send_sem=x_send.at[micro, mask],
            recv_sem=x_recv.at[micro, mask],
            device_id=device(flip(chip, mask, bits), core),
            device_id_type=MESH,
        )

    def relay(micro, mask, own=False):
        source = flip(chip, mask, bits)
        return pltpu.make_async_remote_copy(
            src_ref=x_ref.at[micro] if own else x_all.at[micro, source, core],
            dst_ref=x_all.at[micro, source, core],
            send_sem=relay_send.at[micro, mask],
            recv_sem=relay_recv.at[micro, mask],
            device_id=sibling,
            device_id_type=MESH,
        )

    def relay_arrival(micro, mask):
        source = flip(chip, mask, bits)
        return pltpu.make_async_remote_copy(
            src_ref=x_all.at[micro, source, 1 - core],
            dst_ref=x_all.at[micro, source, 1 - core],
            send_sem=relay_send.at[micro, mask],
            recv_sem=relay_recv.at[micro, mask],
            device_id=sibling,
            device_id_type=MESH,
        )

    def x_arrival(micro, mask):
        return pltpu.make_async_remote_copy(
            src_ref=x_ref.at[micro],
            dst_ref=x_all.at[micro, flip(chip, mask, bits), core],
            send_sem=x_send.at[micro, mask],
            recv_sem=x_recv.at[micro, mask],
            device_id=device(flip(chip, mask, bits), core),
            device_id_type=MESH,
        )

    middle = rows // 2
    parts = (pl.ds(0, middle), pl.ds(middle, rows - middle))

    def pass_on(micro, mask, source, part):
        return pltpu.make_async_remote_copy(
            src_ref=x_all.at[micro, source, core, parts[part]],
            dst_ref=x_all.at[micro, source, core, parts[part]],
            send_sem=pass_send.at[micro, part],
            recv_sem=pass_recv.at[micro, part],
            device_id=device(flip(chip, mask, bits), core),
            device_id_type=MESH,
        )

    def half_tile(side):
        return pl.ds(pl.multiple_of(side * rows, rows), rows)

    def load_cot(step):
        micro, mask = step_of(step)
        slot = lax.rem(step, 2)
        source = flip(chip, mask, bits)
        return [
            pltpu.make_async_copy(
                cot_ref.at[2 * source + side, micro],
                cot_tile.at[slot, half_tile(side)],
                cot_load.at[slot, side],
            )
            for side in range(2)
        ]

    def load_own(step):
        slot = lax.rem(step, 2)
        return pltpu.make_async_copy(
            x_ref.at[step_of(step)[0]], x_tile.at[slot, half_tile(core)], x_load.at[slot, 0]
        )

    def load_x(step, number):
        micro, mask = step_of(step)
        slot = lax.rem(step, 2)
        side = core if number == 0 else 1 - core
        return pltpu.make_async_copy(
            x_all.at[micro, flip(chip, mask, bits), side],
            x_tile.at[slot, half_tile(side)],
            x_load.at[slot, number],
        )

    def store(step):
        micro, mask = step_of(step)
        return [
            pltpu.make_async_copy(
                out_tile.at[pl.ds(side * rows, rows)],
                out_ref.at[2 * flip(chip, mask, bits) + side, micro],
                out_store.at[side],
            )
            for side in range(2)
        ]

    def swap(step):
        slot = lax.rem(step, 2)
        held = lax.rem(step, PEER_SLOTS)
        return pltpu.make_async_remote_copy(
            src_ref=grad_tile.at[pl.ds(pl.multiple_of((1 - core) * rows, rows), rows)],
            dst_ref=peer_tile.at[held],
            send_sem=swap_send.at[slot],
            recv_sem=swap_recv.at[held],
            device_id=sibling,
            device_id_type=MESH,
        )

    def push_sum(step):
        micro, mask = step_of(step)
        slot = lax.rem(step, PEER_SLOTS)
        return pltpu.make_async_remote_copy(
            src_ref=peer_tile.at[slot],
            dst_ref=part_ref.at[micro, mask],
            send_sem=sum_send.at[slot],
            recv_sem=sum_recv.at[micro, mask],
            device_id=device(flip(chip, mask, bits), core),
            device_id_type=MESH,
        )

    def keep_sum(step):
        micro, mask = step_of(step)
        slot = lax.rem(step, PEER_SLOTS)
        return pltpu.make_async_copy(
            peer_tile.at[slot], part_ref.at[micro, mask], sum_send.at[slot]
        )

    def wait_sum_sent(step):
        mask = step_of(step)[1]

        @pl.when(mask > 0)
        def _():
            push_sum(step).wait_send()

        @pl.when(mask == 0)
        def _():
            keep_sum(step).wait()

    def fetch(step):
        micro, mask = step_of(step)

        if not across:

            @pl.when(mask > 0)
            def _():
                x_arrival(micro, mask).wait_recv()
                relay(micro, mask).start()

        else:

            @pl.when((mask == 1) | (mask == 2))
            def _():
                x_arrival(micro, mask).wait_recv()
                relay(micro, mask).start()

            for part in range(2):

                @pl.when(mask == part + 1)
                def _():
                    pass_on(micro, 2 - part, flip(chip, part + 1, bits), part).start()

            @pl.when(mask == 3)
            def _():
                for part in range(2):
                    pass_on(micro, part + 1, flip(chip, 3, bits), part).wait_recv()
                relay(micro, mask).start()

        for copy in load_cot(step):
            copy.start()

        @pl.when(mask == 0)
        def _():
            load_own(step).start()

        @pl.when(mask > 0)
        def _():
            load_x(step, 0).start()

    def fetch_relayed(step):
        micro, mask = step_of(step)
        relay_arrival(micro, mask).wait_recv()
        load_x(step, 1).start()

    def finish_sum(step):
        slot = lax.rem(step, 2)
        held = lax.rem(step, PEER_SLOTS)
        swap(step).wait()

        def add(index, carry):
            at = pl.ds(pl.multiple_of(index * 16, 16), 16)
            mine = pl.ds(pl.multiple_of(core * rows + index * 16, 16), 16)
            value = grad_tile[mine, :].astype(F32) + peer_tile[held, at, :].astype(F32)
            peer_tile[held, at, :] = value.astype(BF16)
            return carry

        lax.fori_loop(0, rows // 16, add, 0)

        mask = step_of(step)[1]

        @pl.when(mask > 0)
        def _():
            push_sum(step).start()

        @pl.when(mask == 0)
        def _():
            keep_sum(step).start()

    direct = (1, 2) if across else tuple(range(1, pairs))
    for mask in direct:
        push_x(0, mask).start()
    for micro in range(micro_count):
        relay(micro, 0, own=True).start()

    def weights_in(pieces):
        copies = []
        for number, (source, target, start) in enumerate(pieces):
            copies.append(
                pltpu.make_async_copy(
                    source, target.at[pl.ds(start, source.shape[0])], weight_load.at[number]
                )
            )
        return copies

    shared_weights = weights_in(
        [(shared_gate_in, gate_ref, 0), (shared_up_in, up_ref, 0), (shared_down_in, down_ref, 0)]
    )
    for copy in shared_weights:
        copy.start()
    shared_rows = []
    for micro in range(micro_count):
        at = pl.ds(micro * rows, rows)
        shared_rows.append(
            pltpu.make_async_copy(x_ref.at[micro], x_tile.at[1, at], x_load.at[1, micro])
        )
        shared_rows.append(
            pltpu.make_async_copy(cot_ref.at[place, micro], cot_tile.at[1, at], cot_load.at[1, micro])
        )
    for copy in shared_rows:
        copy.start()
    for target in (gate_ref, up_ref, down_ref):
        target[shared_units:, :] = jnp.zeros((units - shared_units, D), BF16)
    fetch(0)

    chunk = 256 if units % 256 == 0 else LANES
    out_chunk = 512
    slab = half - LANES
    first_lane = fe % LANES
    slab_chunk = slab // chunk * chunk

    def hidden_pass(x, cot, here, start, gate, scale):
        at = slice(start, start + chunk)
        up = mm_nt(x, up_ref[at, :])
        back = mm_nt(cot, down_ref[at, :])
        sig = jax.nn.sigmoid(gate)
        act = gate * sig
        hidden = act * up
        grad_hidden = back if scale is None else back * scale
        scaled = hidden if scale is None else hidden * scale
        hidden_low[here, at] = scaled.astype(BF16)
        grad_gate[here, at] = (grad_hidden * up * (sig * (1.0 + gate * (1.0 - sig)))).astype(BF16)
        grad_up[here, at] = (grad_hidden * act).astype(BF16)
        return hidden * back

    def grad_pass():
        for start in range(0, D, out_chunk):
            at = slice(start, start + out_chunk)
            grad = mm(grad_gate[...], gate_ref[:, at]) + mm(grad_up[...], up_ref[:, at])
            grad_tile[:, at] = grad.astype(BF16)

    def out_pass():
        for start in range(0, D, out_chunk):
            at = slice(start, start + out_chunk)
            out_tile[:, at] = mm(hidden_low[...], down_ref[:, at]).astype(BF16)

    for copy in shared_weights + shared_rows:
        copy.wait()
    row_halves = (slice(0, rows), slice(rows, 2 * rows))
    for here in row_halves:
        x, cot = x_tile[1, here, :D], cot_tile[1, here]
        for start in range(0, units, chunk):
            gate = mm_nt(x, gate_ref[start : start + chunk, :])
            hidden_pass(x, cot, here, start, gate, None)
    grad_pass()
    out_pass()
    expert_weights = weights_in(
        [
            piece
            for number in range(EXP_DEV)
            for piece in (
                (gate_in.at[number], gate_ref, number * half),
                (up_in.at[number], up_ref, number * half),
                (down_in.at[number], down_ref, number * half),
            )
        ]
        + [(router_in, gate_ref, fe)]
    )
    for copy in expert_weights:
        copy.start()
    for target in (gate_ref, up_ref, down_ref):
        for number in range(EXP_DEV):
            first = number * half + fe
            if target is gate_ref and number == 0:
                first += experts
            last = (number + 1) * half
            if last > first:
                target[first:last, :] = jnp.zeros((last - first, D), BF16)
    shared_stores = []
    for micro in range(micro_count):
        at = pl.ds(micro * rows, rows)
        shared_stores.append(
            pltpu.make_async_copy(out_tile.at[at], shared_out.at[micro], shared_store.at[micro, 0])
        )
        shared_stores.append(
            pltpu.make_async_copy(
                grad_tile.at[at], shared_part.at[micro], shared_store.at[micro, 1]
            )
        )
    for copy in shared_stores:
        copy.start()
    fetch_relayed(0)
    for copy in shared_stores:
        copy.wait()
    staged = []
    for which, (left, right) in enumerate(
        ((grad_gate, x_tile[1, :, :D]), (grad_up, x_tile[1, :, :D]), (hidden_low, cot_tile[1]))
    ):
        for start in range(0, shared_units, rows):
            stage = len(staged) % 2 * rows
            count = min(rows, shared_units - start)
            if len(staged) >= 2:
                staged[-2].wait()
            out_tile[stage : stage + rows, :] = mm_tn(
                left[:, start : start + rows], right
            ).astype(BF16)
            copy = pltpu.make_async_copy(
                out_tile.at[pl.ds(stage, count)],
                shared_grads.at[which, pl.ds(start, count)],
                grad_store.at[len(staged) % 2],
            )
            copy.start()
            staged.append(copy)
    for acc in (gate_acc, up_acc, down_acc):
        acc[...] = jnp.zeros_like(acc)
    for copy in staged[-2:] + expert_weights:
        copy.wait()

    def work(step, carry):
        slot = lax.rem(step, 2)

        for copy in load_cot(step):
            copy.wait()
        for number in range(2):
            load_x(step, number).wait()

        for here in row_halves:
            x = x_tile[slot, here, :D]
            chosen = x_tile[slot, here, D:].astype(F32)
            cot = cot_tile[slot, here]
            lane = lax.broadcasted_iota(jnp.int32, (rows, LANES), 1) - first_lane
            valid = (lane >= 0) & (lane < experts)

            first_gate = mm_nt(x, gate_ref[slab_chunk : slab_chunk + chunk, :])
            slab_gate = first_gate[:, slab - slab_chunk : slab - slab_chunk + LANES]
            logits = jnp.where(valid, slab_gate, -1e30)
            weights = jnp.where(
                valid, jnp.exp(logits - jnp.max(logits, axis=-1, keepdims=True)), 0.0
            )
            router_probs = weights / jnp.sum(weights, axis=-1, keepdims=True)
            named = router_probs * chosen
            picks = [lane == place * EXP_DEV + number for number in range(EXP_DEV)]
            scales = [
                jnp.sum(jnp.where(pick, named, 0.0), axis=-1, keepdims=True) for pick in picks
            ]
            flags = [
                jnp.sum(jnp.where(pick, chosen, 0.0), axis=-1, keepdims=True) for pick in picks
            ]
            dots = [jnp.zeros((rows, 1), F32) for _ in picks]
            column = lax.broadcasted_iota(jnp.int32, (rows, chunk), 1)
            starts = [slab_chunk] + [at for at in range(0, units, chunk) if at != slab_chunk]
            for start in starts:
                if start == slab_chunk:
                    gate = first_gate
                else:
                    gate = mm_nt(x, gate_ref[start : start + chunk, :])
                first, last = start // half, (start + chunk - 1) // half
                scale = scales[first]
                if last > first:
                    scale = jnp.where(column < last * half - start, scales[first], scales[last])
                product = hidden_pass(x, cot, here, start, gate, scale)
                if last > first:
                    split = last * half - start
                    dots[first] = dots[first] + jnp.sum(product[:, :split], axis=-1, keepdims=True)
                    dots[last] = dots[last] + jnp.sum(product[:, split:], axis=-1, keepdims=True)
                else:
                    dots[first] = dots[first] + jnp.sum(product, axis=-1, keepdims=True)
            spread = jnp.zeros((rows, LANES), F32)
            for pick, dot, flag in zip(picks, dots, flags):
                spread = spread + jnp.where(pick, dot * flag, 0.0)
            grad_logits = router_probs * (
                spread - jnp.sum(router_probs * spread, axis=-1, keepdims=True)
            )
            grad_gate[here, slab:half] = jnp.where(
                lane < 0, grad_gate[here, slab:half].astype(F32), grad_logits
            ).astype(BF16)

        @pl.when(step + 1 < steps)
        def _():
            fetch(step + 1)

        @pl.when(step == 0)
        def _():
            for micro in range(1, micro_count):
                for mask in direct:
                    push_x(micro, mask).start()

        @pl.when(step >= 1)
        def _():
            finish_sum(step - 1)

        @pl.when(step >= PEER_SLOTS)
        def _():
            wait_sum_sent(step - PEER_SLOTS)
            pl.semaphore_signal(credit, inc=1, device_id=sibling, device_id_type=MESH)
            pl.semaphore_wait(credit, 1)

        grad_pass()
        swap(step).start()


        @pl.when(step >= 1)
        def _():
            for copy in store(step - 1):
                copy.wait()

        out_pass()
        for copy in store(step):
            copy.start()

        @pl.when(step + 1 < steps)
        def _():
            fetch_relayed(step + 1)

        for acc, left, right in (
            (gate_acc, grad_gate, x_tile),
            (up_acc, grad_up, x_tile),
            (down_acc, hidden_low, cot_tile),
        ):
            for start in range(0, D, out_chunk):
                at = slice(start, start + out_chunk)
                acc[:, at] += mm_tn(left[...], right[slot, :, at])
        return carry


    lax.fori_loop(0, steps, work, 0)
    finals = [
        pltpu.make_async_copy(
            gate_acc.at[pl.ds(fe, experts)], router_out, acc_store.at[EXP_DEV, 0]
        )
    ]
    for number in range(EXP_DEV):
        for which, (acc, target) in enumerate(
            ((gate_acc, gate_out), (up_acc, up_out), (down_acc, down_out))
        ):
            finals.append(
                pltpu.make_async_copy(
                    acc.at[pl.ds(number * half, fe)],
                    target.at[number],
                    acc_store.at[number, which],
                )
            )
    for copy in finals:
        copy.start()
    finish_sum(steps - 1)
    for back in range(PEER_SLOTS, 0, -1):
        wait_sum_sent(steps - back)
    for copy in finals:
        copy.wait()
    for copy in store(steps - 1):
        copy.wait()
    for micro in range(micro_count):
        if across:
            for part in range(2):
                pass_on(micro, 2 - part, flip(chip, part + 1, bits), part).wait_send()
        for mask in range(pairs):
            relay(micro, mask).wait_send()
            if mask in direct:
                push_x(micro, mask).wait_send()
            if mask:
                pltpu.make_async_remote_copy(
                    src_ref=peer_tile.at[0],
                    dst_ref=part_ref.at[micro, mask],
                    send_sem=sum_send.at[0],
                    recv_sem=sum_recv.at[micro, mask],
                    device_id=device(flip(chip, mask, bits), core),
                    device_id_type=MESH,
                ).wait_recv()


def expert_pass(
    x_ext, cot_all, gate_w, up_w, down_w, router_w, shared_gate, shared_up, shared_down, collective_id
):
    micro_count, rows, width = x_ext.shape
    context_size = lax.axis_size("context")
    pairs = lax.axis_size("dp") * context_size // 2
    fe, experts, shared_units = gate_w.shape[1], router_w.shape[0], shared_gate.shape[0]
    half = -(-(fe + experts) // LANES) * LANES
    units = EXP_DEV * half
    dma = pltpu.SemaphoreType.DMA
    wide = jax.ShapeDtypeStruct((EXP_DEV, fe, D), F32)
    own = jax.ShapeDtypeStruct((micro_count, rows, D), BF16)
    return pl.pallas_call(
        functools.partial(expert_kernel, pairs, context_size, fe),
        out_shape=(
            jax.ShapeDtypeStruct((2 * pairs, micro_count, rows, D), BF16),
            jax.ShapeDtypeStruct((micro_count, pairs, rows, D), BF16),
            wide,
            wide,
            wide,
            jax.ShapeDtypeStruct((experts, D), F32),
            own,
            own,
            jax.ShapeDtypeStruct((3, shared_units, D), BF16),
            jax.ShapeDtypeStruct((micro_count, pairs, 2, rows, width), BF16),
        ),
        in_specs=[pl.BlockSpec(memory_space=pl.ANY)] * 9,
        out_specs=(pl.BlockSpec(memory_space=pl.ANY),) * 10,
        scratch_shapes=[
            pltpu.VMEM((units, D), BF16),
            pltpu.VMEM((units, D), BF16),
            pltpu.VMEM((units, D), BF16),
            pltpu.VMEM((2, 2 * rows, width), BF16),
            pltpu.VMEM((2, 2 * rows, D), BF16),
            pltpu.VMEM((2 * rows, D), BF16),
            pltpu.VMEM((2 * rows, D), BF16),
            pltpu.VMEM((PEER_SLOTS, rows, D), BF16),
            pltpu.VMEM((2 * rows, units), BF16),
            pltpu.VMEM((2 * rows, units), BF16),
            pltpu.VMEM((2 * rows, units), BF16),
            pltpu.VMEM((units, D), F32),
            pltpu.VMEM((units, D), F32),
            pltpu.VMEM((units, D), F32),
            dma((micro_count, pairs)),
            dma((micro_count, pairs)),
            dma((micro_count, pairs)),
            dma((micro_count, pairs)),
            dma((micro_count, 2)),
            dma((micro_count, 2)),
            dma((2, 2)),
            dma((2, 2)),
            dma((2,)),
            dma((2,)),
            dma((PEER_SLOTS,)),
            dma((PEER_SLOTS,)),
            dma((micro_count, pairs)),
            dma((3 * EXP_DEV + 1,)),
            dma((2,)),
            dma((micro_count, 2)),
            dma((EXP_DEV + 1, 3)),
            pltpu.SemaphoreType.REGULAR,
        ],
        compiler_params=pltpu.CompilerParams(
            collective_id=collective_id, has_side_effects=True, vmem_limit_bytes=62 * MIB
        ),
        cost_estimate=pl.CostEstimate(
            flops=36 * (pairs * micro_count + 1) * rows * D * units,
            bytes_accessed=500_000_000,
            transcendentals=0,
        ),
        name="expert_pass",
    )(x_ext, cot_all, gate_w, up_w, down_w, router_w, shared_gate, shared_up, shared_down)[:9]


def per_device(
    tokens,
    segments,
    expert_ids,
    norm_attn,
    w_query,
    w_kv_down,
    norm_latent,
    w_kv_up,
    w_out,
    norm_ffn,
    w_router,
    w_shared_gate,
    w_shared_up,
    w_shared_down,
    w_expert_gate,
    w_expert_up,
    w_expert_down,
    cotangent,
):
    micro_count, block_rows = tokens.shape[:2]
    rows = micro_count * block_rows
    seq_len = segments.shape[1]
    context_size = lax.axis_size("context")
    groups = lax.axis_size("dp") * context_size
    tensor_size = lax.axis_size("tensor")
    group_index = lax.axis_index("dp") * context_size + lax.axis_index("context")
    own_rows = block_rows // tensor_size
    own_start = lax.axis_index("tensor") * own_rows
    experts = EXP_DEV * groups
    heads_local = w_query.shape[1] // (NOPE + ROPE)
    fe_local = w_expert_gate.shape[2]
    start_row = lax.axis_index("context") * block_rows
    query_index = start_row + jnp.arange(block_rows)
    key_index = jnp.arange(seq_len)
    cos_block, sin_block = angles(query_index.astype(F32), ROPE)
    cos_query = jnp.tile(cos_block, (micro_count, 1))
    sin_query = jnp.tile(sin_block, (micro_count, 1))
    gain_attn = norm_attn.astype(F32)
    gain_latent = norm_latent.astype(F32)
    gain_ffn = norm_ffn.astype(F32)

    def own(values):
        values = values.reshape((micro_count, block_rows) + values.shape[1:])
        part = lax.dynamic_slice_in_dim(values, own_start, own_rows, axis=1)
        return part.reshape((micro_count * own_rows,) + values.shape[2:])

    def to_owner(values):
        values = values.astype(BF16).reshape(micro_count, tensor_size, own_rows, values.shape[-1])
        return LineScatter(values, "tensor")

    def from_owners(values):
        return LineGather(values.reshape(micro_count, own_rows, values.shape[-1]), "tensor")

    def flat(values):
        return values.reshape(-1, values.shape[-1])

    ff_local = w_shared_gate.shape[1]
    slots = jnp.arange(LANES) - fe_local % LANES
    named = jnp.any(expert_ids[..., None] == slots, axis=2).astype(BF16)

    x_rows = tokens.reshape(rows, D).astype(F32)
    cot_rows = cotangent.reshape(rows, D)
    inv_attn = rms_scale(x_rows)
    normed_attn = x_rows * inv_attn
    x_attn = (normed_attn * gain_attn).astype(BF16)
    kv_raw = mm(x_attn, w_kv_down)
    latent_raw = kv_raw[:, :LATENT]
    inv_latent = rms_scale(latent_raw)
    normed_latent = latent_raw * inv_latent
    latent = (normed_latent * gain_latent).astype(BF16)
    key_rope = rotate(kv_raw[:, LATENT:], cos_query, sin_query).astype(BF16)
    blank = jnp.zeros((rows, KV_WIDTH - LATENT - ROPE), BF16)
    kv_own = jnp.concatenate([latent, key_rope, blank], axis=1)
    kv_own = kv_own.reshape(micro_count, block_rows, KV_WIDTH).transpose(1, 0, 2)
    kv_own = kv_own.reshape(block_rows, micro_count * KV_WIDTH)
    (kv_all,) = exchange([GroupGather(kv_own, ("context",))], 1, 20)
    kv_all, cot_late = lax.optimization_barrier((kv_all, cotangent))
    cot_all = lax.all_gather(cot_late, GROUP, axis=0)
    kv_all = kv_all.reshape(seq_len, micro_count * KV_WIDTH)
    seg_query = lax.dynamic_slice_in_dim(segments, start_row, block_rows, axis=1)
    places = (
        seg_query[:, :, None],
        segments[:, None, :],
        query_index[:, None],
        key_index[None, :],
        jnp.tile(cos_block, (1, 2)),
        jnp.concatenate([-sin_block, sin_block], axis=1),
    )
    weights = (w_query, w_kv_up, w_out)
    attn_part, *kept = attend(x_attn, kv_all, places, weights, micro_count, heads_local)
    own_shape = (micro_count, own_rows, D)
    tokens_own = own(tokens.reshape(rows, D)).reshape(own_shape)

    def finish_attention(sums, extras, shares, results):
        for m in range(micro_count):
            hidden = extras[0][m].astype(F32) + sums[0][m]
            results[0][m] = hidden
            shares[0][m] = (hidden * rms_scale(hidden) * extras[1][...]).astype(BF16)

    x_ffn, hidden_one = exchange(
        [
            SumThenShare(
                [to_owner(attn_part)],
                [tokens_own, gain_ffn[None]],
                finish_attention,
                [jax.ShapeDtypeStruct(own_shape, BF16)],
                [jax.ShapeDtypeStruct(own_shape, F32)],
            )
        ],
        2,
        80,
    )
    x_ffn = x_ffn.reshape(rows, D)
    x_ext = jnp.concatenate([x_ffn.reshape(micro_count, block_rows, D), named], axis=-1)

    (
        out_part,
        grad_part,
        gate_grad,
        up_grad,
        down_grad,
        router_grad,
        shared_out,
        shared_part,
        shared_grads,
    ) = expert_pass(
        x_ext,
        cot_all,
        w_expert_gate.transpose(0, 2, 1),
        w_expert_up.transpose(0, 2, 1),
        w_expert_down,
        w_router.T,
        w_shared_gate.T,
        w_shared_up.T,
        w_shared_down,
        4,
    )
    shared_units = shared_grads.shape[1]
    shared_grads = shared_grads.reshape(groups, -1, D)
    shared_grads = lax.psum_scatter(shared_grads, GROUP, scatter_dimension=0, tiled=False)
    cot_own = own(cot_rows).reshape(own_shape)

    def finish_experts(sums, extras, shares, results):
        hidden, cot, gain = extras
        gain_grad = jnp.zeros((1, D), F32)
        for m in range(micro_count):
            inverse = rms_scale(hidden[m])
            normed = hidden[m] * inverse
            grad = sums[0][m]
            gain_grad = gain_grad + jnp.sum(grad * normed, axis=0, keepdims=True)
            total = cot[m].astype(F32) + norm_back(grad * gain[...], normed, inverse)
            results[0][m] = total
            shares[0][m] = total.astype(BF16)
        results[1][...] = gain_grad

    out_sum = lax.psum_scatter(out_part, GROUP, scatter_dimension=0, tiled=False)
    grad_attn_low, grad_one, norm_ffn_grad = exchange(
        [
            SumThenShare(
                [LineScatterSum(grad_part, shared_part, "tensor")],
                [hidden_one, cot_own, gain_ffn[None]],
                finish_experts,
                [jax.ShapeDtypeStruct(own_shape, BF16)],
                [
                    jax.ShapeDtypeStruct(own_shape, F32),
                    jax.ShapeDtypeStruct((1, D), F32),
                ],
            ),
        ],
        5,
        90,
    )
    grad_attn_low = grad_attn_low.reshape(rows, D)
    grad_kv_part, grad_x_heads, query_grad, kv_up_grad, out_grad = attend_back(
        grad_attn_low, x_attn, kv_all, places, weights, kept, micro_count, heads_local
    )
    grad_x_heads, shared_grads = lax.optimization_barrier((grad_x_heads, shared_grads))
    shared_grads = lax.all_gather(shared_grads, GROUP, axis=0, tiled=True)
    router_part = router_grad.T.astype(BF16).reshape(1, tensor_size, -1, LANES)
    latent_own = own(latent_raw).reshape(micro_count, own_rows, LATENT)
    turns_own = [
        own(angle).reshape(micro_count, own_rows, ROPE)
        for angle in (
            jnp.tile(cos_query, (1, 2)),
            jnp.concatenate([sin_query, -sin_query], axis=1),
        )
    ]

    def finish_rows(sums, extras, shares, results):
        x_grad, kv_grad, router = sums
        x_own, one, ffn_gain_grad, raw, cosine, sine, gain, latent_gain, down_w = extras
        gain_grad = jnp.zeros((1, D), F32)
        latent_gain_grad = jnp.zeros((1, LATENT), F32)
        for m in range(micro_count):
            inverse = rms_scale(raw[m])
            normed = raw[m] * inverse
            grad = kv_grad[m, :, :LATENT]
            latent_gain_grad = latent_gain_grad + jnp.sum(grad * normed, axis=0, keepdims=True)
            kv_low = jnp.concatenate(
                [
                    norm_back(grad * latent_gain[...], normed, inverse),
                    turn(kv_grad[m, :, LATENT:], cosine[m], sine[m]),
                ],
                axis=1,
            ).astype(BF16)
            x = x_own[m].astype(F32)
            inverse = rms_scale(x)
            normed = x * inverse
            grad = x_grad[m] + mm(kv_low, down_w[...])
            gain_grad = gain_grad + jnp.sum(grad * normed, axis=0, keepdims=True)
            total = one[m] + norm_back(grad * gain[...], normed, inverse)
            shares[0][m, :, :D] = total.astype(BF16)
            shares[0][m, :, D:] = kv_low
        shares[1][0] = router[0].astype(BF16)
        shares[2][0, :, :D] = gain_grad
        shares[2][0, :, D : 2 * D] = ffn_gain_grad[...]
        shares[2][0, :, 2 * D :] = latent_gain_grad

    finished, router_all, small = exchange(
        [
            SumThenShare(
                [
                    to_owner(grad_x_heads),
                    ContextThenLine(
                        grad_kv_part, micro_count, ("context",), "tensor"
                    ),
                    LineScatter(router_part, "tensor"),
                ],
                [
                    tokens_own,
                    grad_one,
                    norm_ffn_grad,
                    latent_own,
                    *turns_own,
                    gain_attn[None],
                    gain_latent[None],
                    w_kv_down.T,
                ],
                finish_rows,
                [
                    jax.ShapeDtypeStruct((micro_count, own_rows, D + LATENT + ROPE), BF16),
                    jax.ShapeDtypeStruct((1,) + router_part.shape[2:], BF16),
                    jax.ShapeDtypeStruct((1, 1, 2 * D + LATENT), F32),
                ],
                [],
            ),
        ],
        8,
        100,
    )
    finished = finished.reshape(rows, -1)
    finished, out_sum = lax.optimization_barrier((finished, out_sum))
    out_sum = out_sum.astype(F32) + shared_out.astype(F32)
    out_sum = out_sum.astype(BF16).reshape(micro_count, tensor_size, own_rows, D)
    out_sum = out_sum.transpose(1, 0, 2, 3)
    out_sum = lax.psum_scatter(out_sum, "tensor", scatter_dimension=0, tiled=False)
    grad_tokens, grad_kv_raw = finished[:, :D], finished[:, D:]
    kv_width = -(-grad_kv_raw.shape[1] // (16 * groups)) * 16 * groups
    grad_kv_raw = jnp.pad(grad_kv_raw, ((0, 0), (0, kv_width - grad_kv_raw.shape[1])))
    kv_down_grad = mm_tn(grad_kv_raw, x_attn).astype(BF16)
    small = jnp.sum(small, axis=(0, 1, 2)).astype(BF16)
    query_grad, kv_up_grad, out_grad, kv_down_grad, router_grad, small = exchange(
        [
            GroupSum(part.reshape(groups, -1, part.shape[-1]), GROUP)
            for part in (
                query_grad,
                kv_up_grad,
                out_grad,
                kv_down_grad,
                router_all.reshape(groups * 16, -1),
                small.reshape(groups * 16, -1),
            )
        ],
        10,
        80,
    )
    query_grad, kv_up_grad, out_grad, kv_down_grad, out_sum, shared_grads, one = (
        lax.optimization_barrier(
            (query_grad, kv_up_grad, out_grad, kv_down_grad, out_sum, shared_grads, F32(1.0))
        )
    )
    output = (hidden_one + out_sum.astype(F32)).astype(BF16)
    output = lax.all_gather(output, "tensor", axis=0)
    output = output.transpose(1, 0, 2, 3)
    kv_down_grad = kv_down_grad.reshape(-1, D)[: LATENT + ROPE].astype(F32).T
    router_grad = router_grad.reshape(D, experts).astype(F32)
    small = small.reshape(-1).astype(F32)
    gate_grad, up_grad, down_grad = gate_grad * one, up_grad * one, down_grad * one
    return (
        output.reshape(tokens.shape),
        grad_tokens.reshape(tokens.shape),
        small[:D],
        flat(query_grad).reshape(D, -1).astype(F32),
        kv_down_grad,
        small[D + D :],
        kv_up_grad.reshape(LATENT, -1).astype(F32),
        out_grad.reshape(-1, D).astype(F32),
        small[D : D + D],
        router_grad,
        shared_grads[:ff_local].astype(F32).T,
        shared_grads[shared_units : shared_units + ff_local].astype(F32).T,
        shared_grads[2 * shared_units : 2 * shared_units + ff_local].astype(F32),
        gate_grad.transpose(0, 2, 1),
        up_grad.transpose(0, 2, 1),
        down_grad,
    )


def solution(mesh):
    return jax.shard_map(
        per_device,
        mesh=mesh,
        in_specs=(
            P("dp", "context", None),
            P("dp", None),
            P("dp", "context", None),
            P(),
            P(None, "tensor"),
            P(),
            P(),
            P(None, "tensor"),
            P("tensor", None),
            P(),
            P(),
            P(None, "tensor"),
            P(None, "tensor"),
            P("tensor", None),
            P(("dp", "context"), None, "tensor"),
            P(("dp", "context"), None, "tensor"),
            P(("dp", "context"), "tensor", None),
            P("dp", "context", None),
        ),
        out_specs=(
            P("dp", "context", None),
            P("dp", "context", None),
            P(),
            P(None, "tensor"),
            P(),
            P(),
            P(None, "tensor"),
            P("tensor", None),
            P(),
            P(),
            P(None, "tensor"),
            P(None, "tensor"),
            P("tensor", None),
            P(("dp", "context"), None, "tensor"),
            P(("dp", "context"), None, "tensor"),
            P(("dp", "context"), "tensor", None),
        ),
        check_vma=False,
    )
```
